32 devices in a mesh: node: 16 (over z, y, x), head: 2 (over core).
Axes of the slice: x: 2, y: 2, z: 4, core: 2. Of those that a mesh axis runs over, the one named last changes fastest.
Arguments:
- node_queries: bfloat16 [4096, 1024], P('node', 'head'), may hold values from -56 to 56, as said below
- node_keys: bfloat16 [4096, 1024], P('node', 'head'), may hold values from -56 to 56, as said below
- node_values: bfloat16 [4096, 1024], P('node', 'head'), may hold values from -6 to 6
- tile_index: int32 [4, 32, 2], P(None, 'node'), may hold values from 0 to 1
- tile_count: int32 [4, 32], P(None, 'node'), may hold values from 0 to 2, as said below
- out_weight: bfloat16 [1024, 1024], replicated, may hold values from -0.1875 to 0.1875
Outputs:
- updated: bfloat16 [1024, 4096], P('head', 'node')
The draws below stay inside these ranges and needn't reach their ends.
Inputs may be any that keep to these rules, and one draw needn't show every extreme that they name: `node_queries`: queries, each row usually of order one; some rows may carry a large entry at a head's first column. `node_keys`: keys, likewise. `tile_index`: tile numbers may repeat within a row. `tile_count`: 2 is reached in every draw.
All inputs are finite; a program needn't handle non-finite values.
Results may differ from the reference program's by a relative error of at most 0.015.
Values may be sent and summed in bfloat16 or wider, within the bound.
No kernel may reach another device: no remote copies, remote signals or barrier semaphores. Data moves between devices by JAX's collectives and lax.ppermute only.
A program may use at most 64 MiB of HBM per device.

```python
import jax
import jax.numpy as jnp
from jax import lax

HEADS = 8
HD = 128
D = 1024
TILE = 128
SLOTS = 2
STEPS = 4
DST_DEV = 256
NODES = 4096
TILES = 32


def drawn_rows(key, row_count, total_width):
    first = jax.random.fold_in(key, 0)
    sample = jnp.clip(jax.random.normal(first, (row_count, total_width), jnp.float32), -6.0, 6.0)
    return sample.astype(jnp.bfloat16)


def draw_node_queries(key, part):
    key = jax.random.fold_in(key, 1)
    return drawn_rows(key, NODES, D)


def draw_node_keys(key, part):
    key = jax.random.fold_in(key, 2)
    return drawn_rows(key, NODES, D)


def draw_tile_count(key, part):
    key = jax.random.fold_in(key, 3)
    counts = jax.random.randint(key, (STEPS, TILES), 0, SLOTS + 1, jnp.int32)
    return counts.at[0, 0].set(SLOTS)


def plant(entries, rng, least, high):
    longest = entries.shape.index(max(entries.shape))
    spots = []
    for shift in (0, 1):
        where = [jax.random.randint(jax.random.fold_in(rng, axis), (), 0, length) for axis, length in enumerate(entries.shape)]
        where[longest] = (where[longest] + shift) % entries.shape[longest]
        spots.append(tuple(where))
    return entries.at[spots[0]].set(least).at[spots[1]].set(high)


def level_of(rng, extent, pieces, low, largest):
    level = 1.0
    for position, blocks in pieces:
        heights = jax.random.uniform(jax.random.fold_in(jax.random.fold_in(rng, 6), position), (blocks,), jnp.float32, low / len(pieces), largest / len(pieces))
        level = level * jnp.repeat(jnp.exp(heights), extent[position] // blocks).reshape((-1,) + (1,) * (len(extent) - 1 - position))
    return level


def noise(stream_key, dims, spread, limit, cuts=(), kind=jnp.bfloat16):
    factor_of = level_of(stream_key, dims, cuts, -0.22, 0.18) if cuts else 1.0
    array = jax.random.normal(stream_key, dims, jnp.float32) * spread * factor_of
    return jnp.minimum(jnp.maximum(array, -limit), limit).astype(kind)


def setup_inputs(seed: int = 0) -> dict:
    streams_of = jax.random.split(jax.random.key(seed), 7)
    node_queries = draw_node_queries(jax.random.fold_in(streams_of[6], 71), 0)
    node_keys = draw_node_keys(jax.random.fold_in(streams_of[6], 71), 0)
    node_values = noise(streams_of[2], (NODES, D), 1.0, 6.0, ((0, 16), (1, 2)))
    tile_index = plant(jax.random.randint(streams_of[3], (STEPS, TILES, SLOTS), 0, DST_DEV // TILE), jax.random.fold_in(streams_of[3], 1), 0, (DST_DEV // TILE) - 1).astype(jnp.int32)
    tile_count = draw_tile_count(jax.random.fold_in(streams_of[6], 71), 0)
    out_weight = noise(streams_of[5], (D, D), D ** -0.5, 0.1875)
    return {"node_queries": node_queries, "node_keys": node_keys, "node_values": node_values, "tile_index": tile_index, "tile_count": tile_count, "out_weight": out_weight}


def reference(node_queries, node_keys, node_values, tile_index, tile_count, out_weight):
    tile_total = DST_DEV // TILE
    score_scale = HD ** -0.5
    slab_total = NODES // DST_DEV

    def slab_mix(slab_index):
        row_start = (slab_index * DST_DEV).astype(jnp.int32)
        queries = lax.dynamic_slice_in_dim(node_queries, row_start, DST_DEV, 0).astype(jnp.float32).reshape(tile_total, TILE, HEADS, HD)
        own_keys = lax.dynamic_slice_in_dim(node_keys, row_start, DST_DEV, 0).astype(jnp.float32).reshape(tile_total, TILE, HEADS, HD)
        own_values = lax.dynamic_slice_in_dim(node_values, row_start, DST_DEV, 0).astype(jnp.float32).reshape(tile_total, TILE, HEADS, HD)
        self_score = jnp.transpose(jnp.sum(queries * own_keys, axis=-1) * score_scale, (0, 2, 1))
        score_list = []
        value_list = []
        for turn in range(STEPS):
            source_start = (((slab_index - turn) % slab_total) * DST_DEV).astype(jnp.int32)
            key_block = lax.dynamic_slice_in_dim(node_keys, source_start, DST_DEV, 0).astype(jnp.float32).reshape(tile_total, TILE, HEADS, HD)
            value_block = lax.dynamic_slice_in_dim(node_values, source_start, DST_DEV, 0).astype(jnp.float32).reshape(tile_total, TILE, HEADS, HD)
            tile_start = (slab_index * tile_total).astype(jnp.int32)
            index_rows = lax.dynamic_slice_in_dim(tile_index[turn], tile_start, tile_total, 0)
            count_rows = lax.dynamic_slice_in_dim(tile_count[turn], tile_start, tile_total, 0)
            key_tiles = key_block[index_rows]
            value_tiles = value_block[index_rows]
            scores = jnp.einsum('trhd,tjkhd->thrjk', queries, key_tiles) * score_scale
            usable = (jnp.arange(SLOTS, dtype=jnp.int32)[None, :] < count_rows[:, None])[:, None, None, :, None]
            score_list.append(jnp.where(usable, scores, -jnp.inf))
            value_list.append(value_tiles)
        top_score = self_score
        for scores in score_list:
            top_score = jnp.maximum(top_score, jnp.max(scores, axis=(3, 4)))
        self_weight = jnp.exp(self_score - top_score)
        running_sum = self_weight
        weighted = self_weight[..., None] * jnp.transpose(own_values, (0, 2, 1, 3))
        for scores, value_tiles in zip(score_list, value_list):
            weights = jnp.exp(scores - top_score[..., None, None])
            running_sum = running_sum + jnp.sum(weights, axis=(3, 4))
            rounded = weights.astype(jnp.bfloat16).astype(jnp.float32)
            weighted = weighted + jnp.einsum('thrjk,tjkhd->thrd', rounded, value_tiles)
        mixed = weighted / running_sum[..., None]
        return jnp.transpose(mixed, (0, 2, 1, 3)).reshape(DST_DEV, D).astype(jnp.bfloat16)

    mixed_all = lax.map(slab_mix, jnp.arange(slab_total, dtype=jnp.int32)).reshape(NODES, D)
    product = jnp.dot(mixed_all.astype(jnp.float32), out_weight.astype(jnp.float32), precision=lax.Precision.HIGHEST)
    return jnp.transpose(product).astype(jnp.bfloat16)
```

```python
import functools

import jax
import jax.numpy as jnp
from jax import lax
from jax.experimental import pallas as pl
from jax.experimental.pallas import tpu as pltpu
from jax.sharding import Mesh, PartitionSpec as P

HEADS = 8
HD = 128
TILE = 128
SLOTS = 2
STEPS = 4
LOG2E = 1.4426950408889634
SCALE = LOG2E * HD ** (-0.5)
MASKED = -1e30
EXTRA = 16
VMEM = pl.BlockSpec(memory_space=pltpu.VMEM)
SMEM = pl.BlockSpec(memory_space=pltpu.SMEM)
ANY = pl.BlockSpec(memory_space=pl.ANY)
PARAMS = pltpu.CompilerParams(vmem_limit_bytes=48 * 1024 * 1024)


def use_rows(index_ref, count_ref, tiles):
    row = lax.broadcasted_iota(jnp.int32, (EXTRA, HD), 0)
    uses = jnp.zeros((EXTRA, HD), jnp.float32)
    for turn in range(STEPS):
        for dest in range(tiles):
            for source in range(tiles):
                times = jnp.float32(0)
                for slot in range(SLOTS):
                    used = (slot < count_ref[turn, dest]) & (index_ref[turn, dest, slot] == source)
                    times += jnp.where(used, 1.0, 0.0)
                uses = jnp.where(row == (turn * tiles + dest) * tiles + source, times, uses)
    return uses


def pack_kernel(query_ref, key_ref, value_ref, index_ref, count_ref, kv_ref, q_ref):
    rows, width = query_ref.shape
    tiles = rows // TILE
    uses = use_rows(index_ref, count_ref, tiles).astype(jnp.bfloat16)
    for head in range(width // HD):
        cols = slice(head * HD, (head + 1) * HD)
        kv_ref[head, :rows] = key_ref[:, cols]
        for tile in range(tiles):
            part = value_ref[tile * TILE : (tile + 1) * TILE, cols]
            kv_ref[head, rows + tile * TILE : rows + (tile + 1) * TILE] = part.T
        q_ref[head, :rows] = query_ref[:, cols]
        q_ref[head, rows:] = uses


def source_scores(kv_ref, place, q_ref, dest, turn, rows):
    tiles = rows // TILE
    queries = q_ref[dest, :rows]
    keys = kv_ref[place, :rows]
    raw = (
        lax.dot_general(keys, queries, (((1,), (1,)), ((), ())), preferred_element_type=jnp.float32)
        * SCALE
    )
    parts = []
    for source in range(tiles):
        bias = []
        for tile in range(tiles):
            at = rows + (turn * tiles + tile) * tiles + source
            times = q_ref[dest, at : at + 1].astype(jnp.float32)
            bias.append(jnp.where(times > 0.5, times - 1.0, MASKED))
        parts.append(
            raw[source * TILE : (source + 1) * TILE] + jnp.concatenate(bias, axis=1)
        )
    return raw, jnp.concatenate(parts, axis=0)


def slab_values(kv_ref, place, rows):
    return jnp.concatenate(
        [kv_ref[place, rows + at : rows + at + TILE] for at in range(0, rows, TILE)], axis=1
    )


def add_sources(scores, values, top, total, mixed):
    for score, value in zip(scores, values):
        weights = jnp.exp2(score - top)
        total = total + jnp.sum(weights, axis=0, keepdims=True)
        mixed = mixed + jnp.dot(
            value, weights.astype(jnp.bfloat16), preferred_element_type=jnp.float32
        )
    return total, mixed


def near_kernel(head_total, kv_ref, q_ref, weight_ref, mixed_ref, state_ref, turned_ref, held, sem):
    group = kv_ref.shape[0]
    rows = kv_ref.shape[1] // 2
    me = lax.axis_index("head")
    depth = weight_ref.shape[0] // head_total
    features = weight_ref.shape[1] // head_total
    copies = []
    for other in range(head_total):
        start = pl.multiple_of(jnp.bitwise_xor(me, other) * depth, depth)
        cols = pl.ds(pl.multiple_of(me * features, features), features)
        copies.append(
            pltpu.make_async_copy(
                weight_ref.at[pl.ds(start, depth), cols], held.at[other], sem.at[other]
            )
        )
        copies[-1].start()
    eye = lax.broadcasted_iota(jnp.int32, (TILE, TILE), 0) == lax.broadcasted_iota(
        jnp.int32, (TILE, TILE), 1
    )
    for dest in range(group):
        scores, values = [], []
        for turn in range(STEPS):
            place = dest - turn
            if place < 0:
                continue
            raw, score = source_scores(kv_ref, place, q_ref, dest, turn, rows)
            if turn == 0:
                own = jnp.concatenate(
                    [
                        jnp.sum(
                            jnp.where(eye, raw[at : at + TILE, at : at + TILE], 0.0),
                            axis=0,
                            keepdims=True,
                        )
                        for at in range(0, rows, TILE)
                    ],
                    axis=1,
                )
            scores.append(score)
            values.append(slab_values(kv_ref, place, rows))
        top = own
        for score in scores:
            top = jnp.maximum(top, jnp.max(score, axis=0, keepdims=True))
        weight = jnp.exp2(own - top)
        total, mixed = add_sources(
            scores, values, top, weight, weight * values[0].astype(jnp.float32)
        )
        mixed_ref[dest] = mixed
        state_ref[dest, 0:1] = top
        state_ref[dest, 1:2] = total
    for other in range(head_total):
        copies[other].wait()
        turned_ref[other] = held[other].T


def far_kernel(offsets, q_ref, mixed_ref, state_ref, *refs):
    far_refs, out_ref = refs[:-1], refs[-1]
    group, _, rows = mixed_ref.shape
    for dest in range(group):
        scores, values = [], []
        for turn in range(STEPS):
            place = dest - turn
            if place >= 0:
                continue
            offset = -(place // group)
            slot = place % group - max(0, offset * group - STEPS + 1)
            far = far_refs[offsets.index(offset)]
            _, score = source_scores(far, slot, q_ref, dest, turn, rows)
            scores.append(score)
            values.append(slab_values(far, slot, rows))
        top = state_ref[dest, 0:1]
        total = state_ref[dest, 1:2]
        mixed = mixed_ref[dest]
        if scores:
            before = top
            for score in scores:
                top = jnp.maximum(top, jnp.max(score, axis=0, keepdims=True))
            factor = jnp.exp2(before - top)
            total, mixed = add_sources(scores, values, top, total * factor, mixed * factor)
        out_ref[dest] = (mixed / total).astype(out_ref.dtype)


def project_kernel(turned_ref, *refs):
    mix_refs, out_ref = refs[:-1], refs[-1]
    result = None
    for other, mix_ref in enumerate(mix_refs):
        part = jnp.dot(turned_ref[other], mix_ref[...], preferred_element_type=jnp.float32)
        result = part if result is None else result + part
    out_ref[...] = result.astype(out_ref.dtype)


def on_device(node_queries, node_keys, node_values, tile_index, tile_count, out_weight):
    rows, width = node_queries.shape
    group = width // HD
    groups = lax.axis_size("group")
    head_total = lax.axis_size("head")
    depth, feature_total = out_weight.shape
    features = feature_total // head_total
    bf16, f32 = jnp.bfloat16, jnp.float32
    shape = jax.ShapeDtypeStruct

    kv, q = pl.pallas_call(
        pack_kernel,
        out_shape=(
            shape((group, 2 * rows, HD), bf16),
            shape((group, rows + EXTRA, HD), bf16),
        ),
        in_specs=[VMEM, VMEM, VMEM, SMEM, SMEM],
        out_specs=(VMEM, VMEM),
        compiler_params=PARAMS,
        name="pack",
    )(node_queries, node_keys, node_values, tile_index, tile_count)

    kv = lax.all_to_all(kv, "place", 0, 0)
    offsets = list(range(1, -(-(STEPS - 1) // group) + 1))
    far = []
    for offset in offsets:
        first = max(0, offset * group - STEPS + 1)
        pairs = [(source, (source + offset) % groups) for source in range(groups)]
        far.append(lax.ppermute(kv[first:], "group", pairs))
    q = lax.all_to_all(q, "place", 0, 0)

    mixed, state, turned = pl.pallas_call(
        functools.partial(near_kernel, head_total),
        out_shape=(
            shape((group, HD, rows), f32),
            shape((group, 8, rows), f32),
            shape((head_total, features, depth // head_total), bf16),
        ),
        in_specs=[VMEM, VMEM, ANY],
        out_specs=(VMEM, VMEM, VMEM),
        scratch_shapes=[
            pltpu.VMEM((head_total, depth // head_total, features), bf16),
            pltpu.SemaphoreType.DMA((head_total,)),
        ],
        compiler_params=PARAMS,
        name="near",
    )(kv, q, out_weight)

    mix = pl.pallas_call(
        functools.partial(far_kernel, offsets),
        out_shape=shape((group, HD, rows), bf16),
        in_specs=[VMEM] * (3 + len(far)),
        out_specs=VMEM,
        compiler_params=PARAMS,
        name="far",
    )(q, mixed, state, *far)

    mix = lax.all_to_all(mix, "place", 0, 0).reshape(width, rows)
    mixes = [mix]
    for other in range(1, head_total):
        pairs = [(source, source ^ other) for source in range(head_total)]
        mixes.append(lax.ppermute(mix, "head", pairs))
    return pl.pallas_call(
        project_kernel,
        out_shape=shape((features, rows), bf16),
        in_specs=[VMEM] * (1 + head_total),
        out_specs=VMEM,
        compiler_params=PARAMS,
        name="project",
    )(turned, *mixes)


def solution(mesh):
    nodes, heads = mesh.devices.shape
    place = HEADS // heads
    split = Mesh(
        mesh.devices.reshape(nodes // place, place, heads), ("group", "place", "head")
    )
    node = ("group", "place")
    return jax.shard_map(
        on_device,
        mesh=split,
        in_specs=(
            P(node, "head"),
            P(node, "head"),
            P(node, "head"),
            P(None, node, None),
            P(None, node),
            P(),
        ),
        out_specs=P("head", node),
        check_vma=False,
    )
```

```python
import functools

import jax
import jax.numpy as jnp
from jax import lax
from jax.experimental import pallas as pl
from jax.experimental.pallas import tpu as pltpu
from jax.sharding import Mesh, PartitionSpec as P

HEADS = 8
HD = 128
TILE = 128
SLOTS = 2
STEPS = 4
LOG2E = 1.4426950408889634
SCALE = LOG2E * HD ** (-0.5)
MASKED = -1e30
EXTRA = 16
VMEM = pl.BlockSpec(memory_space=pltpu.VMEM)
HBM = pl.BlockSpec(memory_space=pltpu.HBM)
PARAMS = pltpu.CompilerParams(vmem_limit_bytes=48 * 1024 * 1024)


def use_rows(index_ref, count_ref, tiles):
    row = lax.broadcasted_iota(jnp.int32, (EXTRA, HD), 0)
    uses = jnp.zeros((EXTRA, HD), jnp.float32)
    for turn in range(STEPS):
        for dest in range(tiles):
            for source in range(tiles):
                times = jnp.float32(0)
                for slot in range(SLOTS):
                    used = (slot < count_ref[dest, turn]) & (index_ref[dest, slot, turn] == source)
                    times += jnp.where(used, 1.0, 0.0)
                uses = jnp.where(row == (turn * tiles + dest) * tiles + source, times, uses)
    return uses


def pack_kernel(query_ref, key_ref, value_ref, index_ref, count_ref, *refs):
    out_refs, (values, index, count, sem) = refs[:-4], refs[-4:]
    rows, width = query_ref.shape
    group = width // HD
    tiles = rows // TILE
    place = lax.axis_index("place")
    value_copy = pltpu.make_async_copy(value_ref, values, sem.at[0])
    value_copy.start()
    table_copies = [
        pltpu.make_async_copy(index_ref, index, sem.at[1]),
        pltpu.make_async_copy(count_ref, count, sem.at[2]),
    ]
    for copy in table_copies:
        copy.start()
    copies = []
    for step in range(group):
        cols = pl.ds(pl.multiple_of(jnp.bitwise_xor(place, step) * HD, HD), HD)
        out = out_refs[step]
        copies += [
            pltpu.make_async_copy(
                key_ref.at[:, cols], out.at[pl.ds(0, rows)], sem.at[3 + 2 * step]
            ),
            pltpu.make_async_copy(
                query_ref.at[:, cols], out.at[pl.ds(2 * rows, rows)], sem.at[4 + 2 * step]
            ),
        ]
    for copy in copies:
        copy.start()
    for copy in table_copies:
        copy.wait()
    uses = use_rows(index, count, tiles).astype(jnp.bfloat16)
    value_copy.wait()
    for step in range(group):
        cols = pl.ds(pl.multiple_of(jnp.bitwise_xor(place, step) * HD, HD), HD)
        out = out_refs[step]
        out[3 * rows :] = uses
        for at in range(0, rows, TILE):
            out[rows + at : rows + at + TILE] = values[at : at + TILE, cols].T
    for copy in copies:
        copy.wait()


def source_scores(keys, query_uses, turn, rows):
    tiles = rows // TILE
    raw = (
        lax.dot_general(
            keys, query_uses[:rows], (((1,), (1,)), ((), ())), preferred_element_type=jnp.float32
        )
        * SCALE
    )
    parts = []
    for source in range(tiles):
        bias = []
        for tile in range(tiles):
            at = rows + (turn * tiles + tile) * tiles + source
            times = query_uses[at : at + 1].astype(jnp.float32)
            bias.append(jnp.where(times > 0.5, times - 1.0, MASKED))
        parts.append(
            raw[source * TILE : (source + 1) * TILE] + jnp.concatenate(bias, axis=1)
        )
    return raw, jnp.concatenate(parts, axis=0)


def slab_values(kv_ref, slot, rows):
    return jnp.concatenate(
        [kv_ref[slot, rows + at : rows + at + TILE] for at in range(0, rows, TILE)], axis=1
    )


def add_sources(scores, values, top, total, mixed):
    for score, value in zip(scores, values):
        weights = jnp.exp2(score - top)
        total = total + jnp.sum(weights, axis=0, keepdims=True)
        mixed = mixed + jnp.dot(
            value, weights.astype(jnp.bfloat16), preferred_element_type=jnp.float32
        )
    return total, mixed


def near_kernel(*refs, group, head_total):
    got_refs, weight_ref = refs[:group], refs[group]
    query_ref, mixed_ref, state_ref, turned_ref, kv, held, sem = refs[group + 1 :]
    rows = mixed_ref.shape[2]
    place = lax.axis_index("place")
    me = lax.axis_index("head")
    depth = weight_ref.shape[0] // head_total
    features = weight_ref.shape[1] // head_total
    copies = []
    for other in range(head_total):
        start = pl.multiple_of(jnp.bitwise_xor(me, other) * depth, depth)
        cols = pl.ds(pl.multiple_of(me * features, features), features)
        copies.append(
            pltpu.make_async_copy(
                weight_ref.at[pl.ds(start, depth), cols], held.at[other], sem.at[other]
            )
        )
        copies[-1].start()
    for step in range(group):
        slab = jnp.bitwise_xor(place, step)
        kv[slab] = got_refs[step][: 2 * rows]
        query_ref[slab] = got_refs[step][2 * rows :]
    eye = lax.broadcasted_iota(jnp.int32, (TILE, TILE), 0) == lax.broadcasted_iota(
        jnp.int32, (TILE, TILE), 1
    )
    for dest in range(group):
        scores, values = [], []
        query_uses = query_ref[dest]
        for turn in range(STEPS):
            slab = dest - turn
            if slab < 0:
                continue
            raw, score = source_scores(kv[slab, :rows], query_uses, turn, rows)
            if turn == 0:
                own = jnp.concatenate(
                    [
                        jnp.sum(
                            jnp.where(eye, raw[at : at + TILE, at : at + TILE], 0.0),
                            axis=0,
                            keepdims=True,
                        )
                        for at in range(0, rows, TILE)
                    ],
                    axis=1,
                )
            scores.append(score)
            values.append(slab_values(kv, slab, rows))
        top = own
        for score in scores:
            top = jnp.maximum(top, jnp.max(score, axis=0, keepdims=True))
        weight = jnp.exp2(own - top)
        total, mixed = add_sources(
            scores, values, top, weight, weight * values[0].astype(jnp.float32)
        )
        mixed_ref[dest] = mixed
        state_ref[dest, 0:1] = top
        state_ref[dest, 1:2] = total
    for other in range(head_total):
        copies[other].wait()
        turned_ref[other] = held[other].T


def halo_steps(group, first):
    return [[k for k in range(group) if place ^ k >= first] for place in range(group)]


def pick(place, choices):
    result = jnp.int32(choices[-1])
    for at, choice in enumerate(choices[:-1]):
        result = jnp.where(place == at, jnp.int32(choice), result)
    return result


def far_kernel(*refs, group, halos):
    query_ref, mixed_ref, state_ref = refs[:3]
    messages = sum(group - first for _, first in halos)
    far_refs = refs[3 : 3 + messages]
    out_refs = refs[3 + messages : 3 + messages + group]
    far, done = refs[3 + messages + group :]
    rows = mixed_ref.shape[2]
    place = lax.axis_index("place")
    slots = {}
    base = 0
    for offset, first in halos:
        steps = halo_steps(group, first)
        for at in range(group - first):
            slab = pick(place, [p ^ steps[p][at] for p in range(group)])
            far[base + slab - first] = far_refs[base + at][...]
            slots[offset, first + at] = base + at
        base += group - first
    for dest in range(group):
        scores, values = [], []
        query_uses = query_ref[dest]
        for turn in range(STEPS):
            slab = dest - turn
            if slab >= 0:
                continue
            slot = slots[-(slab // group), slab % group]
            scores.append(source_scores(far[slot, :rows], query_uses, turn, rows)[1])
            values.append(slab_values(far, slot, rows))
        top = state_ref[dest, 0:1]
        total = state_ref[dest, 1:2]
        mixed = mixed_ref[dest]
        if scores:
            before = top
            for score in scores:
                top = jnp.maximum(top, jnp.max(score, axis=0, keepdims=True))
            factor = jnp.exp2(before - top)
            total, mixed = add_sources(scores, values, top, total * factor, mixed * factor)
        done[dest] = (mixed / total).astype(done.dtype)
    for step in range(group):
        out_refs[step][...] = done[jnp.bitwise_xor(place, step)]


def project_kernel(turned_ref, *refs, group, head_total):
    mix_refs, out_ref, mix = refs[:-2], refs[-2], refs[-1]
    place = lax.axis_index("place")
    for other in range(head_total):
        for step in range(group):
            mix[other, jnp.bitwise_xor(place, step)] = mix_refs[other * group + step][...]
    result = None
    for other in range(head_total):
        part = jnp.dot(
            turned_ref[other],
            mix[other].reshape(turned_ref.shape[2], out_ref.shape[1]),
            preferred_element_type=jnp.float32,
        )
        result = part if result is None else result + part
    out_ref[...] = result.astype(out_ref.dtype)


def swapped(value, axis, step):
    count = lax.axis_size(axis)
    return lax.ppermute(value, axis, [(source, source ^ step) for source in range(count)])


def on_device(node_queries, node_keys, node_values, tile_index, tile_count, out_weight):
    rows, width = node_queries.shape
    group = width // HD
    groups = lax.axis_size("group")
    head_total = lax.axis_size("head")
    depth, feature_total = out_weight.shape
    features = feature_total // head_total
    bf16, f32 = jnp.bfloat16, jnp.float32
    shape = jax.ShapeDtypeStruct
    place = lax.axis_index("place")

    packed = pl.pallas_call(
        pack_kernel,
        out_shape=[shape((3 * rows + EXTRA, HD), bf16)] * group,
        in_specs=[HBM] * 5,
        out_specs=[VMEM] * group,
        scratch_shapes=[
            pltpu.VMEM((rows, width), bf16),
            pltpu.SMEM((rows // TILE, SLOTS, STEPS), jnp.int32),
            pltpu.SMEM((rows // TILE, STEPS), jnp.int32),
            pltpu.SemaphoreType.DMA((3 + 2 * group,)),
        ],
        compiler_params=PARAMS,
        name="pack",
    )(
        *[
            pltpu.with_memory_space_constraint(array, pltpu.HBM)
            for array in (
                node_queries,
                node_keys,
                node_values,
                jnp.transpose(tile_index, (1, 2, 0)),
                jnp.transpose(tile_count, (1, 0)),
            )
        ],
    )

    got = [packed[0]] + [swapped(packed[step], "place", step) for step in range(1, group)]
    halos = []
    for offset in range(1, -(-(STEPS - 1) // group) + 1):
        halos.append((offset, max(0, offset * group - STEPS + 1)))
    far = []
    for offset, first in halos:
        steps = halo_steps(group, first)
        pairs = [(source, (source + offset) % groups) for source in range(groups)]
        for at in range(group - first):
            piece = got[steps[-1][at]][: 2 * rows]
            for p in range(group - 1):
                if steps[p][at] != steps[-1][at]:
                    piece = jnp.where(place == p, got[steps[p][at]][: 2 * rows], piece)
            piece, *got = lax.optimization_barrier([piece, *got])
            if at > 1:
                far[-2], piece = lax.optimization_barrier((far[-2], piece))
            far.append(lax.ppermute(piece, "group", pairs))

    queries, mixed, state, turned = pl.pallas_call(
        functools.partial(near_kernel, group=group, head_total=head_total),
        out_shape=(
            shape((group, rows + EXTRA, HD), bf16),
            shape((group, HD, rows), f32),
            shape((group, 8, rows), f32),
            shape((head_total, features, depth // head_total), bf16),
        ),
        in_specs=[VMEM] * group + [HBM],
        out_specs=(VMEM, VMEM, VMEM, VMEM),
        scratch_shapes=[
            pltpu.VMEM((group, 2 * rows, HD), bf16),
            pltpu.VMEM((head_total, depth // head_total, features), bf16),
            pltpu.SemaphoreType.DMA((head_total,)),
        ],
        compiler_params=PARAMS,
        name="near",
    )(*got, out_weight)

    mix = pl.pallas_call(
        functools.partial(far_kernel, group=group, halos=halos),
        out_shape=[shape((HD, rows), bf16)] * group,
        in_specs=[VMEM] * (3 + len(far)),
        out_specs=[VMEM] * group,
        scratch_shapes=[
            pltpu.VMEM((len(far), 2 * rows, HD), bf16),
            pltpu.VMEM((group, HD, rows), bf16),
        ],
        compiler_params=PARAMS,
        name="far",
    )(queries, mixed, state, *far)

    mixes = [mix[0]] + [swapped(mix[step], "place", step) for step in range(1, group)]
    for other in range(1, head_total):
        mixes += [swapped(mixes[step], "head", other) for step in range(group)]
    return pl.pallas_call(
        functools.partial(project_kernel, group=group, head_total=head_total),
        out_shape=shape((features, rows), bf16),
        in_specs=[VMEM] * (1 + head_total * group),
        out_specs=VMEM,
        scratch_shapes=[pltpu.VMEM((head_total, group, HD, rows), bf16)],
        compiler_params=PARAMS,
        name="project",
    )(turned, *mixes)


def solution(mesh):
    nodes, heads = mesh.devices.shape
    place = HEADS // heads
    split = Mesh(
        mesh.devices.reshape(nodes // place, place, heads), ("group", "place", "head")
    )
    node = ("group", "place")
    return jax.shard_map(
        on_device,
        mesh=split,
        in_specs=(
            P(node, "head"),
            P(node, "head"),
            P(node, "head"),
            P(None, node, None),
            P(None, node),
            P(),
        ),
        out_specs=P("head", node),
        check_vma=False,
    )
```

```python
import functools

import jax
import jax.numpy as jnp
from jax import lax
from jax.experimental import pallas as pl
from jax.experimental.pallas import tpu as pltpu
from jax.sharding import Mesh, PartitionSpec as P

HEADS = 8
HD = 128
TILE = 128
SLOTS = 2
STEPS = 4
LOG2E = 1.4426950408889634
SCALE = LOG2E * HD ** (-0.5)
MASKED = -1e30
EXTRA = 16
COST = 10**9
VMEM = pl.BlockSpec(memory_space=pltpu.VMEM)
HBM = pl.BlockSpec(memory_space=pltpu.HBM)
PARAMS = pltpu.CompilerParams(vmem_limit_bytes=48 * 1024 * 1024)


def use_rows(index_ref, count_ref, tiles):
    row = lax.broadcasted_iota(jnp.int32, (EXTRA, HD), 0)
    uses = jnp.zeros((EXTRA, HD), jnp.float32)
    for turn in range(STEPS):
        for dest in range(tiles):
            for source in range(tiles):
                times = jnp.float32(0)
                for slot in range(SLOTS):
                    used = (slot < count_ref[dest, turn]) & (index_ref[dest, slot, turn] == source)
                    times += jnp.where(used, 1.0, 0.0)
                uses = jnp.where(row == (turn * tiles + dest) * tiles + source, times, uses)
    return uses


def pack_kernel(query_ref, key_ref, value_ref, index_ref, count_ref, *refs):
    out_refs, (values, index, count, sem) = refs[:-4], refs[-4:]
    rows, width = query_ref.shape
    group = width // HD
    tiles = rows // TILE
    place = lax.axis_index("place")
    value_copy = pltpu.make_async_copy(value_ref, values, sem.at[0])
    value_copy.start()
    table_copies = [
        pltpu.make_async_copy(index_ref, index, sem.at[1]),
        pltpu.make_async_copy(count_ref, count, sem.at[2]),
    ]
    for copy in table_copies:
        copy.start()
    copies = []
    for step in range(group):
        cols = pl.ds(pl.multiple_of(jnp.bitwise_xor(place, step) * HD, HD), HD)
        out = out_refs[step]
        copies += [
            pltpu.make_async_copy(
                key_ref.at[:, cols], out.at[pl.ds(0, rows)], sem.at[3 + 2 * step]
            ),
            pltpu.make_async_copy(
                query_ref.at[:, cols], out.at[pl.ds(2 * rows, rows)], sem.at[4 + 2 * step]
            ),
        ]
    for copy in copies:
        copy.start()
    for copy in table_copies:
        copy.wait()
    uses = use_rows(index, count, tiles).astype(jnp.bfloat16)
    value_copy.wait()
    for step in range(group):
        cols = pl.ds(pl.multiple_of(jnp.bitwise_xor(place, step) * HD, HD), HD)
        out = out_refs[step]
        out[3 * rows :] = uses
        for at in range(0, rows, TILE):
            out[rows + at : rows + at + TILE] = values[at : at + TILE, cols].T
    for copy in copies:
        copy.wait()


def source_scores(keys, query_uses, turn, rows):
    tiles = rows // TILE
    raw = (
        lax.dot_general(
            keys, query_uses[:rows], (((1,), (1,)), ((), ())), preferred_element_type=jnp.float32
        )
        * SCALE
    )
    parts = []
    for source in range(tiles):
        bias = []
        for tile in range(tiles):
            at = rows + (turn * tiles + tile) * tiles + source
            times = query_uses[at : at + 1].astype(jnp.float32)
            bias.append(jnp.where(times > 0.5, times - 1.0, MASKED))
        parts.append(
            raw[source * TILE : (source + 1) * TILE] + jnp.concatenate(bias, axis=1)
        )
    return raw, jnp.concatenate(parts, axis=0)


def slab_values(kv_ref, slot, rows):
    return jnp.concatenate(
        [kv_ref[slot, rows + at : rows + at + TILE] for at in range(0, rows, TILE)], axis=1
    )


def add_sources(scores, values, top, total, mixed):
    for score, value in zip(scores, values):
        weights = jnp.exp2(score - top)
        total = total + jnp.sum(weights, axis=0, keepdims=True)
        mixed = mixed + jnp.dot(
            value, weights.astype(jnp.bfloat16), preferred_element_type=jnp.float32
        )
    return total, mixed


def near_kernel(*refs, group, head_total):
    got_refs, weight_ref = refs[:group], refs[group]
    query_ref, mixed_ref, state_ref, turned_ref, kv, held, sem = refs[group + 1 :]
    rows = mixed_ref.shape[2]
    place = lax.axis_index("place")
    me = lax.axis_index("head")
    depth = weight_ref.shape[0] // head_total
    features = weight_ref.shape[1] // head_total
    copies = []
    for other in range(head_total):
        start = pl.multiple_of(jnp.bitwise_xor(me, other) * depth, depth)
        cols = pl.ds(pl.multiple_of(me * features, features), features)
        copies.append(
            pltpu.make_async_copy(
                weight_ref.at[pl.ds(start, depth), cols], held.at[other], sem.at[other]
            )
        )
        copies[-1].start()
    for step in range(group):
        slab = jnp.bitwise_xor(place, step)
        kv[slab] = got_refs[step][: 2 * rows]
        query_ref[slab] = got_refs[step][2 * rows :]
    eye = lax.broadcasted_iota(jnp.int32, (TILE, TILE), 0) == lax.broadcasted_iota(
        jnp.int32, (TILE, TILE), 1
    )
    for dest in range(group):
        scores, values = [], []
        query_uses = query_ref[dest]
        for turn in range(STEPS):
            slab = dest - turn
            if slab < 0:
                continue
            raw, score = source_scores(kv[slab, :rows], query_uses, turn, rows)
            if turn == 0:
                own = jnp.concatenate(
                    [
                        jnp.sum(
                            jnp.where(eye, raw[at : at + TILE, at : at + TILE], 0.0),
                            axis=0,
                            keepdims=True,
                        )
                        for at in range(0, rows, TILE)
                    ],
                    axis=1,
                )
            scores.append(score)
            values.append(slab_values(kv, slab, rows))
        top = own
        for score in scores:
            top = jnp.maximum(top, jnp.max(score, axis=0, keepdims=True))
        weight = jnp.exp2(own - top)
        total, mixed = add_sources(
            scores, values, top, weight, weight * values[0].astype(jnp.float32)
        )
        mixed_ref[dest] = mixed
        state_ref[dest, 0:1] = top
        state_ref[dest, 1:2] = total
    for other in range(head_total):
        copies[other].wait()
        turned_ref[other] = held[other].T


def halo_steps(group, first):
    return [[k for k in range(group) if place ^ k >= first] for place in range(group)]


def message_parts(total):
    return [(0, total)] if total < 3 else [(0, total - 1), (total - 1, total)]


def pick(place, choices):
    result = jnp.int32(choices[-1])
    for at, choice in enumerate(choices[:-1]):
        result = jnp.where(place == at, jnp.int32(choice), result)
    return result


def far_kernel(*refs, group, halo, at, last):
    query_ref, mixed_ref, state_ref, far_ref = refs[:4]
    if last:
        out_refs, (mixed_out, state_out, done) = refs[4:-3], refs[-3:]
    else:
        mixed_out, state_out = refs[4:]
    rows = mixed_ref.shape[2]
    place = lax.axis_index("place")
    offset, first = halo
    steps = halo_steps(group, first)
    mixed_out[...] = mixed_ref[...]
    state_out[...] = state_ref[...]
    for low in range(far_ref.shape[0]):
        slabs = [p ^ steps[p][at + low] for p in range(group)]
        mine = pick(place, slabs)
        for slab in sorted(set(slabs)):

            @pl.when(mine == slab)
            def _(low=low, slab=slab):
                value = slab_values(far_ref, low, rows)
                for dest in range(group):
                    turn = dest + offset * group - slab
                    if turn >= STEPS:
                        continue
                    score = source_scores(far_ref[low, :rows], query_ref[dest], turn, rows)[1]
                    before = state_out[dest, 0:1]
                    top = jnp.maximum(before, jnp.max(score, axis=0, keepdims=True))
                    factor = jnp.exp2(before - top)
                    total, mixed = add_sources(
                        [score],
                        [value],
                        top,
                        state_out[dest, 1:2] * factor,
                        mixed_out[dest] * factor,
                    )
                    mixed_out[dest] = mixed
                    state_out[dest, 0:1] = top
                    state_out[dest, 1:2] = total

    if last:
        for dest in range(group):
            done[dest] = (mixed_out[dest] / state_out[dest, 1:2]).astype(done.dtype)
        for steps, out_ref in zip(stage_steps(group), out_refs):
            for low, step in enumerate(steps):
                out_ref[low * HD : (low + 1) * HD] = done[jnp.bitwise_xor(place, step)]


def stage_steps(group):
    stages, bit = [[0]], 1
    while bit < group:
        stages.append([step for step in range(group) if step & -step == bit])
        bit *= 2
    return stages


def project_kernel(turned_ref, *refs, group, head_total):
    mix_refs, out_ref, mix = refs[:-2], refs[-2], refs[-1]
    place = lax.axis_index("place")
    for other in range(head_total):
        step = 0
        for mix_ref in mix_refs[other :: head_total]:
            for low in range(0, mix_ref.shape[0], HD):
                mix[other, jnp.bitwise_xor(place, step)] = mix_ref[low : low + HD]
                step += 1
    result = None
    for other in range(head_total):
        part = jnp.dot(
            turned_ref[other],
            mix[other].reshape(turned_ref.shape[2], out_ref.shape[1]),
            preferred_element_type=jnp.float32,
        )
        result = part if result is None else result + part
    out_ref[...] = result.astype(out_ref.dtype)


def swapped(value, axis, step):
    count = lax.axis_size(axis)
    return lax.ppermute(value, axis, [(source, source ^ step) for source in range(count)])


def on_device(node_queries, node_keys, node_values, tile_index, tile_count, out_weight):
    rows, width = node_queries.shape
    group = width // HD
    groups = lax.axis_size("group")
    head_total = lax.axis_size("head")
    depth, feature_total = out_weight.shape
    features = feature_total // head_total
    bf16, f32 = jnp.bfloat16, jnp.float32
    shape = jax.ShapeDtypeStruct
    place = lax.axis_index("place")

    packed = pl.pallas_call(
        pack_kernel,
        out_shape=[shape((3 * rows + EXTRA, HD), bf16)] * group,
        in_specs=[HBM] * 5,
        out_specs=[VMEM] * group,
        scratch_shapes=[
            pltpu.VMEM((rows, width), bf16),
            pltpu.SMEM((rows // TILE, SLOTS, STEPS), jnp.int32),
            pltpu.SMEM((rows // TILE, STEPS), jnp.int32),
            pltpu.SemaphoreType.DMA((3 + 2 * group,)),
        ],
        compiler_params=PARAMS,
        name="pack",
    )(
        *[
            pltpu.with_memory_space_constraint(array, pltpu.HBM)
            for array in (
                node_queries,
                node_keys,
                node_values,
                jnp.transpose(tile_index, (1, 2, 0)),
                jnp.transpose(tile_count, (1, 0)),
            )
        ],
    )

    halos = []
    for offset in range(1, -(-(STEPS - 1) // group) + 1):
        halos.append((offset, max(0, offset * group - STEPS + 1)))
    got, far = [packed[0]], []
    waiting = [
        (halo, part, max(row[part[1] - 1] for row in halo_steps(group, halo[1])))
        for halo in halos
        for part in message_parts(group - halo[1])
    ]
    for step in range(group):
        if step:
            got.append(swapped(packed[step], "place", step))
        for (offset, first), (at, until), needed in waiting:
            if needed != step:
                continue
            steps = halo_steps(group, first)
            pairs = [(source, (source + offset) % groups) for source in range(groups)]
            parts = []
            for low in range(at, until):
                piece = got[steps[-1][low]][: 2 * rows]
                for p in range(group - 1):
                    if steps[p][low] != steps[-1][low]:
                        piece = jnp.where(place == p, got[steps[p][low]][: 2 * rows], piece)
                parts.append(piece)
            message = jnp.stack(parts)
            message, *got = lax.optimization_barrier([message, *got])
            far.append(((offset, first), at, lax.ppermute(message, "group", pairs)))

    queries, mixed, state, turned = pl.pallas_call(
        functools.partial(near_kernel, group=group, head_total=head_total),
        out_shape=(
            shape((group, rows + EXTRA, HD), bf16),
            shape((group, HD, rows), f32),
            shape((group, 8, rows), f32),
            shape((head_total, features, depth // head_total), bf16),
        ),
        in_specs=[VMEM] * group + [HBM],
        out_specs=(VMEM, VMEM, VMEM, VMEM),
        scratch_shapes=[
            pltpu.VMEM((group, 2 * rows, HD), bf16),
            pltpu.VMEM((head_total, depth // head_total, features), bf16),
            pltpu.SemaphoreType.DMA((head_total,)),
        ],
        compiler_params=PARAMS,
        cost_estimate=pl.CostEstimate(flops=1, transcendentals=1, bytes_accessed=1),
        name="near",
    )(*got, pltpu.with_memory_space_constraint(out_weight, pltpu.HBM))

    for number, (halo, at, message) in enumerate(far):
        last = number == len(far) - 1
        state_shapes = [shape(mixed.shape, f32), shape(state.shape, f32)]
        stages = stage_steps(group)
        outs = pl.pallas_call(
            functools.partial(far_kernel, group=group, halo=halo, at=at, last=last),
            out_shape=[shape((HD * len(steps), rows), bf16) for steps in stages]
            if last
            else state_shapes,
            in_specs=[VMEM] * 4,
            out_specs=[VMEM] * (len(stages) if last else 2),
            scratch_shapes=[
                pltpu.VMEM(mixed.shape, f32),
                pltpu.VMEM(state.shape, f32),
                pltpu.VMEM((group, HD, rows), bf16),
            ]
            if last
            else [],
            compiler_params=PARAMS,
            cost_estimate=pl.CostEstimate(
                flops=COST, transcendentals=1, bytes_accessed=1
            ),
            name="far",
        )(queries, mixed, state, message)
        if not last:
            mixed, state = outs

    mine, pieces = [outs[0]], {}
    for steps, fresh in zip(stages[1:], outs[1:]):
        bit = steps[0]
        sent = [fresh] + [pieces[head, step] for head in range(1, bit) for step in steps]
        got_mix = swapped(jnp.concatenate(sent) if len(sent) > 1 else fresh, "place", bit)
        if len(steps) == 1:
            mine.append(got_mix)
            continue
        for at, (head, step) in enumerate((h, s) for h in range(bit) for s in steps):
            pieces[head ^ bit, step ^ bit] = got_mix[at * HD : (at + 1) * HD]
        mine[0] = jnp.concatenate([mine[0]] + [pieces[head, 0] for head in range(bit, 2 * bit)])
    mixes = []
    for entry in mine:
        mixes += [entry] + [swapped(entry, "head", other) for other in range(1, head_total)]
    return pl.pallas_call(
        functools.partial(project_kernel, group=group, head_total=head_total),
        out_shape=shape((features, rows), bf16),
        in_specs=[VMEM] * (1 + len(mixes)),
        out_specs=VMEM,
        scratch_shapes=[pltpu.VMEM((head_total, group, HD, rows), bf16)],
        compiler_params=PARAMS,
        name="project",
    )(turned, *mixes)


def solution(mesh):
    nodes, heads = mesh.devices.shape
    place = HEADS // heads
    split = Mesh(
        mesh.devices.reshape(nodes // place, place, heads), ("group", "place", "head")
    )
    node = ("group", "place")
    return jax.shard_map(
        on_device,
        mesh=split,
        in_specs=(
            P(node, "head"),
            P(node, "head"),
            P(node, "head"),
            P(None, node, None),
            P(None, node),
            P(),
        ),
        out_specs=P("head", node),
        check_vma=False,
    )
```

```python
import functools

import jax
import jax.numpy as jnp
from jax import lax
from jax.experimental import pallas as pl
from jax.experimental.pallas import tpu as pltpu
from jax.sharding import Mesh, PartitionSpec as P

HEADS = 8
HD = 128
TILE = 128
SLOTS = 2
STEPS = 4
LOG2E = 1.4426950408889634
SCALE = LOG2E * HD ** (-0.5)
MASKED = -1e30
EXTRA = 16
COST = 10**9
VMEM = pl.BlockSpec(memory_space=pltpu.VMEM)
HBM = pl.BlockSpec(memory_space=pltpu.HBM)
PARAMS = pltpu.CompilerParams(vmem_limit_bytes=48 * 1024 * 1024)


def use_rows(index_ref, count_ref, tiles):
    row = lax.broadcasted_iota(jnp.int32, (EXTRA, HD), 0)
    uses = jnp.zeros((EXTRA, HD), jnp.float32)
    for turn in range(STEPS):
        for dest in range(tiles):
            for source in range(tiles):
                times = jnp.float32(0)
                for slot in range(SLOTS):
                    used = (slot < count_ref[dest, turn]) & (index_ref[dest, slot, turn] == source)
                    times += jnp.where(used, 1.0, 0.0)
                uses = jnp.where(row == (turn * tiles + dest) * tiles + source, times, uses)
    return uses


def pack_kernel(query_ref, key_ref, value_ref, index_ref, count_ref, *refs):
    out_refs, (values, index, count, sem) = refs[:-4], refs[-4:]
    rows, width = query_ref.shape
    group = width // HD
    tiles = rows // TILE
    place = lax.axis_index("place")
    value_copy = pltpu.make_async_copy(value_ref, values, sem.at[0])
    value_copy.start()
    table_copies = [
        pltpu.make_async_copy(index_ref, index, sem.at[1]),
        pltpu.make_async_copy(count_ref, count, sem.at[2]),
    ]
    for copy in table_copies:
        copy.start()
    copies = []
    for step in range(group):
        cols = pl.ds(pl.multiple_of(jnp.bitwise_xor(place, step) * HD, HD), HD)
        out = out_refs[step]
        copies += [
            pltpu.make_async_copy(
                key_ref.at[:, cols], out.at[pl.ds(0, rows)], sem.at[3 + 2 * step]
            ),
            pltpu.make_async_copy(
                query_ref.at[:, cols], out.at[pl.ds(2 * rows, rows)], sem.at[4 + 2 * step]
            ),
        ]
    for copy in copies:
        copy.start()
    for copy in table_copies:
        copy.wait()
    uses = use_rows(index, count, tiles).astype(jnp.bfloat16)
    value_copy.wait()
    for step in range(group):
        cols = pl.ds(pl.multiple_of(jnp.bitwise_xor(place, step) * HD, HD), HD)
        out = out_refs[step]
        out[3 * rows :] = uses
        for at in range(0, rows, TILE):
            out[rows + at : rows + at + TILE] = values[at : at + TILE, cols].T
    for copy in copies:
        copy.wait()


def source_scores(keys, query_uses, turn, rows):
    tiles = rows // TILE
    raw = (
        lax.dot_general(
            keys, query_uses[:rows], (((1,), (1,)), ((), ())), preferred_element_type=jnp.float32
        )
        * SCALE
    )
    parts = []
    for source in range(tiles):
        bias = []
        for tile in range(tiles):
            at = rows + (turn * tiles + tile) * tiles + source
            times = query_uses[at : at + 1].astype(jnp.float32)
            bias.append(jnp.where(times > 0.5, times - 1.0, MASKED))
        parts.append(
            raw[source * TILE : (source + 1) * TILE] + jnp.concatenate(bias, axis=1)
        )
    return raw, jnp.concatenate(parts, axis=0)


def slab_values(kv_ref, slot, rows):
    return jnp.concatenate(
        [kv_ref[slot, rows + at : rows + at + TILE] for at in range(0, rows, TILE)], axis=1
    )


def add_sources(scores, values, top, total, mixed):
    for score, value in zip(scores, values):
        weights = jnp.exp2(score - top)
        total = total + jnp.sum(weights, axis=0, keepdims=True)
        mixed = mixed + jnp.dot(
            value, weights.astype(jnp.bfloat16), preferred_element_type=jnp.float32
        )
    return total, mixed


def near_kernel(*refs, group, head_total):
    got_refs, weight_ref = refs[:group], refs[group]
    query_ref, mixed_ref, state_ref, turned_ref, kv, held, sem = refs[group + 1 :]
    rows = mixed_ref.shape[2]
    place = lax.axis_index("place")
    me = lax.axis_index("head")
    depth = weight_ref.shape[0] // head_total
    features = weight_ref.shape[1] // head_total
    copies = []
    for other in range(head_total):
        start = pl.multiple_of(jnp.bitwise_xor(me, other) * depth, depth)
        cols = pl.ds(pl.multiple_of(me * features, features), features)
        copies.append(
            pltpu.make_async_copy(
                weight_ref.at[pl.ds(start, depth), cols], held.at[other], sem.at[other]
            )
        )
        copies[-1].start()
    for step in range(group):
        slab = jnp.bitwise_xor(place, step)
        kv[slab] = got_refs[step][: 2 * rows]
        query_ref[slab] = got_refs[step][2 * rows :]
    eye = lax.broadcasted_iota(jnp.int32, (TILE, TILE), 0) == lax.broadcasted_iota(
        jnp.int32, (TILE, TILE), 1
    )
    for dest in range(group):
        scores, values = [], []
        query_uses = query_ref[dest]
        for turn in range(STEPS):
            slab = dest - turn
            if slab < 0:
                continue
            raw, score = source_scores(kv[slab, :rows], query_uses, turn, rows)
            if turn == 0:
                own = jnp.concatenate(
                    [
                        jnp.sum(
                            jnp.where(eye, raw[at : at + TILE, at : at + TILE], 0.0),
                            axis=0,
                            keepdims=True,
                        )
                        for at in range(0, rows, TILE)
                    ],
                    axis=1,
                )
            scores.append(score)
            values.append(slab_values(kv, slab, rows))
        top = own
        for score in scores:
            top = jnp.maximum(top, jnp.max(score, axis=0, keepdims=True))
        weight = jnp.exp2(own - top)
        total, mixed = add_sources(
            scores, values, top, weight, weight * values[0].astype(jnp.float32)
        )
        mixed_ref[dest] = mixed
        state_ref[dest, 0:1] = top
        state_ref[dest, 1:2] = total
    for other in range(head_total):
        copies[other].wait()
        turned_ref[other] = held[other].T


def halo_steps(group, first):
    return [[k for k in range(group) if place ^ k >= first] for place in range(group)]


def hops(step):
    return step.bit_count()


def sending_order(group):
    return sorted(range(group), key=lambda step: (step > 0, -hops(step), step))


def message_parts(total):
    return [(0, total)] if total < 3 else [(0, total - 1), (total - 1, total)]


def pick(place, choices):
    result = jnp.int32(choices[-1])
    for at, choice in enumerate(choices[:-1]):
        result = jnp.where(place == at, jnp.int32(choice), result)
    return result


def far_kernel(*refs, group, halo, at, last):
    query_ref, mixed_ref, state_ref, far_ref = refs[:4]
    if last:
        out_refs, (mixed_out, state_out, done) = refs[4:-3], refs[-3:]
    else:
        mixed_out, state_out = refs[4:]
    rows = mixed_ref.shape[2]
    place = lax.axis_index("place")
    offset, first = halo
    steps = halo_steps(group, first)
    mixed_out[...] = mixed_ref[...]
    state_out[...] = state_ref[...]
    for low in range(far_ref.shape[0]):
        slabs = [p ^ steps[p][at + low] for p in range(group)]
        mine = pick(place, slabs)
        for slab in sorted(set(slabs)):

            @pl.when(mine == slab)
            def _(low=low, slab=slab):
                value = slab_values(far_ref, low, rows)
                for dest in range(group):
                    turn = dest + offset * group - slab
                    if turn >= STEPS:
                        continue
                    score = source_scores(far_ref[low, :rows], query_ref[dest], turn, rows)[1]
                    before = state_out[dest, 0:1]
                    top = jnp.maximum(before, jnp.max(score, axis=0, keepdims=True))
                    factor = jnp.exp2(before - top)
                    total, mixed = add_sources(
                        [score],
                        [value],
                        top,
                        state_out[dest, 1:2] * factor,
                        mixed_out[dest] * factor,
                    )
                    mixed_out[dest] = mixed
                    state_out[dest, 0:1] = top
                    state_out[dest, 1:2] = total

    if last:
        for dest in range(group):
            done[dest] = (mixed_out[dest] / state_out[dest, 1:2]).astype(done.dtype)
        for step, out_ref in zip(sending_order(group), out_refs):
            out_ref[...] = done[jnp.bitwise_xor(place, step)]


def project_kernel(turned_ref, *refs, group, head_total):
    mix_refs, out_ref, mix = refs[:-2], refs[-2], refs[-1]
    place = lax.axis_index("place")
    for other in range(head_total):
        for at, step in enumerate(sending_order(group)):
            mix[other, jnp.bitwise_xor(place, step)] = mix_refs[other * group + at][...]
    result = None
    for other in range(head_total):
        part = jnp.dot(
            turned_ref[other],
            mix[other].reshape(turned_ref.shape[2], out_ref.shape[1]),
            preferred_element_type=jnp.float32,
        )
        result = part if result is None else result + part
    out_ref[...] = result.astype(out_ref.dtype)


def swapped(value, axis, step):
    count = lax.axis_size(axis)
    return lax.ppermute(value, axis, [(source, source ^ step) for source in range(count)])


def on_device(node_queries, node_keys, node_values, tile_index, tile_count, out_weight):
    rows, width = node_queries.shape
    group = width // HD
    groups = lax.axis_size("group")
    head_total = lax.axis_size("head")
    depth, feature_total = out_weight.shape
    features = feature_total // head_total
    bf16, f32 = jnp.bfloat16, jnp.float32
    shape = jax.ShapeDtypeStruct
    place = lax.axis_index("place")

    packed = pl.pallas_call(
        pack_kernel,
        out_shape=[shape((3 * rows + EXTRA, HD), bf16)] * group,
        in_specs=[HBM] * 5,
        out_specs=[VMEM] * group,
        scratch_shapes=[
            pltpu.VMEM((rows, width), bf16),
            pltpu.SMEM((rows // TILE, SLOTS, STEPS), jnp.int32),
            pltpu.SMEM((rows // TILE, STEPS), jnp.int32),
            pltpu.SemaphoreType.DMA((3 + 2 * group,)),
        ],
        compiler_params=PARAMS,
        name="pack",
    )(
        *[
            pltpu.with_memory_space_constraint(array, pltpu.HBM)
            for array in (
                node_queries,
                node_keys,
                node_values,
                jnp.transpose(tile_index, (1, 2, 0)),
                jnp.transpose(tile_count, (1, 0)),
            )
        ],
    )

    halos = []
    for offset in range(1, -(-(STEPS - 1) // group) + 1):
        halos.append((offset, max(0, offset * group - STEPS + 1)))
    got, far = [packed[0]], []
    waiting = [
        (halo, part, max(row[part[1] - 1] for row in halo_steps(group, halo[1])))
        for halo in halos
        for part in message_parts(group - halo[1])
    ]
    for step in range(group):
        if step:
            block = packed[step]
            if hops(step) > 1:
                block, got[1] = lax.optimization_barrier((block, got[1]))
            got.append(swapped(block, "place", step))
        for (offset, first), (at, until), needed in waiting:
            if needed != step:
                continue
            steps = halo_steps(group, first)
            pairs = [(source, (source + offset) % groups) for source in range(groups)]
            parts = []
            for low in range(at, until):
                piece = got[steps[-1][low]][: 2 * rows]
                for p in range(group - 1):
                    if steps[p][low] != steps[-1][low]:
                        piece = jnp.where(place == p, got[steps[p][low]][: 2 * rows], piece)
                parts.append(piece)
            message = jnp.stack(parts)
            message, *got = lax.optimization_barrier([message, *got])
            far.append(((offset, first), at, lax.ppermute(message, "group", pairs)))

    queries, mixed, state, turned = pl.pallas_call(
        functools.partial(near_kernel, group=group, head_total=head_total),
        out_shape=(
            shape((group, rows + EXTRA, HD), bf16),
            shape((group, HD, rows), f32),
            shape((group, 8, rows), f32),
            shape((head_total, features, depth // head_total), bf16),
        ),
        in_specs=[VMEM] * group + [HBM],
        out_specs=(VMEM, VMEM, VMEM, VMEM),
        scratch_shapes=[
            pltpu.VMEM((group, 2 * rows, HD), bf16),
            pltpu.VMEM((head_total, depth // head_total, features), bf16),
            pltpu.SemaphoreType.DMA((head_total,)),
        ],
        compiler_params=PARAMS,
        cost_estimate=pl.CostEstimate(flops=1, transcendentals=1, bytes_accessed=1),
        name="near",
    )(*got, pltpu.with_memory_space_constraint(out_weight, pltpu.HBM))

    for number, (halo, at, message) in enumerate(far):
        last = number == len(far) - 1
        state_shapes = [shape(mixed.shape, f32), shape(state.shape, f32)]
        outs = pl.pallas_call(
            functools.partial(far_kernel, group=group, halo=halo, at=at, last=last),
            out_shape=[shape((HD, rows), bf16)] * group if last else state_shapes,
            in_specs=[VMEM] * 4,
            out_specs=[VMEM] * (group if last else 2),
            scratch_shapes=[
                pltpu.VMEM(mixed.shape, f32),
                pltpu.VMEM(state.shape, f32),
                pltpu.VMEM((group, HD, rows), bf16),
            ]
            if last
            else [],
            compiler_params=PARAMS,
            cost_estimate=pl.CostEstimate(
                flops=COST, transcendentals=1, bytes_accessed=1
            ),
            name="far",
        )(queries, mixed, state, message)
        if not last:
            mixed, state = outs

    order = sending_order(group)
    mixes = [outs[0]] + [swapped(out, "place", step) for step, out in zip(order[1:], outs[1:])]
    for other in range(1, head_total):
        mixes += [swapped(mix, "head", other) for mix in mixes[:group]]
    return pl.pallas_call(
        functools.partial(project_kernel, group=group, head_total=head_total),
        out_shape=shape((features, rows), bf16),
        in_specs=[VMEM] * (1 + len(mixes)),
        out_specs=VMEM,
        scratch_shapes=[pltpu.VMEM((head_total, group, HD, rows), bf16)],
        compiler_params=PARAMS,
        name="project",
    )(turned, *mixes)


def solution(mesh):
    nodes, heads = mesh.devices.shape
    place = HEADS // heads
    split = Mesh(
        mesh.devices.reshape(nodes // place, place, heads), ("group", "place", "head")
    )
    node = ("group", "place")
    return jax.shard_map(
        on_device,
        mesh=split,
        in_specs=(
            P(node, "head"),
            P(node, "head"),
            P(node, "head"),
            P(None, node, None),
            P(None, node),
            P(),
        ),
        out_specs=P("head", node),
        check_vma=False,
    )
```

```python
import functools

import jax
import jax.numpy as jnp
from jax import lax
from jax.experimental import pallas as pl
from jax.experimental.pallas import tpu as pltpu
from jax.sharding import Mesh, PartitionSpec as P

HEADS = 8
HD = 128
TILE = 128
SLOTS = 2
STEPS = 4
LOG2E = 1.4426950408889634
SCALE = LOG2E * HD ** (-0.5)
MASKED = -1e30
EXTRA = 16
NEAR = 10**9
MORE = 1
FAR = 10**9
VMEM = pl.BlockSpec(memory_space=pltpu.VMEM)
HBM = pl.BlockSpec(memory_space=pltpu.HBM)
PARAMS = pltpu.CompilerParams(vmem_limit_bytes=48 * 1024 * 1024)


def use_rows(index_ref, count_ref, tiles):
    row = lax.broadcasted_iota(jnp.int32, (EXTRA, HD), 0)
    uses = jnp.zeros((EXTRA, HD), jnp.float32)
    for turn in range(STEPS):
        for dest in range(tiles):
            for source in range(tiles):
                times = jnp.float32(0)
                for slot in range(SLOTS):
                    used = (slot < count_ref[dest, turn]) & (index_ref[dest, slot, turn] == source)
                    times += jnp.where(used, 1.0, 0.0)
                uses = jnp.where(row == (turn * tiles + dest) * tiles + source, times, uses)
    return uses


def pack_kernel(query_ref, key_ref, value_ref, index_ref, count_ref, *refs):
    out_refs, (values, index, count, sem) = refs[:-4], refs[-4:]
    rows, width = query_ref.shape
    group = width // HD
    tiles = rows // TILE
    place = lax.axis_index("place")
    value_copy = pltpu.make_async_copy(value_ref, values, sem.at[0])
    value_copy.start()
    table_copies = [
        pltpu.make_async_copy(index_ref, index, sem.at[1]),
        pltpu.make_async_copy(count_ref, count, sem.at[2]),
    ]
    for copy in table_copies:
        copy.start()
    copies = []
    for step in range(group):
        cols = pl.ds(pl.multiple_of(jnp.bitwise_xor(place, step) * HD, HD), HD)
        out = out_refs[step]
        copies += [
            pltpu.make_async_copy(
                key_ref.at[:, cols], out.at[pl.ds(0, rows)], sem.at[3 + 2 * step]
            ),
            pltpu.make_async_copy(
                query_ref.at[:, cols], out.at[pl.ds(2 * rows, rows)], sem.at[4 + 2 * step]
            ),
        ]
    for copy in copies:
        copy.start()
    for copy in table_copies:
        copy.wait()
    uses = use_rows(index, count, tiles).astype(jnp.bfloat16)
    value_copy.wait()
    for step in range(group):
        cols = pl.ds(pl.multiple_of(jnp.bitwise_xor(place, step) * HD, HD), HD)
        out = out_refs[step]
        out[3 * rows :] = uses
        for at in range(0, rows, TILE):
            out[rows + at : rows + at + TILE] = values[at : at + TILE, cols].T
    for copy in copies:
        copy.wait()


def use_bias(block_ref, rows, turn):
    tiles = rows // TILE
    uses = block_ref[3 * rows :].astype(jnp.float32)
    per_turn = tiles * tiles
    times = uses[:per_turn]
    for other in range(1, STEPS):
        times = jnp.where(turn == other, uses[other * per_turn : (other + 1) * per_turn], times)
    return jnp.where(times > 0.5, times - 1.0, MASKED)


def pair_scores(keys, block_ref, rows, turn):
    tiles = rows // TILE
    raw = (
        lax.dot_general(
            keys,
            block_ref[2 * rows : 3 * rows],
            (((1,), (1,)), ((), ())),
            preferred_element_type=jnp.float32,
        )
        * SCALE
    )
    bias = use_bias(block_ref, rows, turn)
    parts = []
    for source in range(tiles):
        line = jnp.concatenate(
            [bias[tile * tiles + source : tile * tiles + source + 1] for tile in range(tiles)],
            axis=1,
        )
        parts.append(raw[source * TILE : (source + 1) * TILE] + line)
    return raw, jnp.concatenate(parts, axis=0)


def add_source(score, values, top, total, mixed):
    weights = jnp.exp2(score - top)
    total = total + jnp.sum(weights, axis=0, keepdims=True)
    mixed = mixed + jnp.dot(
        values, weights.astype(jnp.bfloat16), preferred_element_type=jnp.float32
    )
    return total, mixed


def turned_values(source_ref, rows):
    return jnp.concatenate(
        [source_ref[rows + at : rows + at + TILE] for at in range(0, rows, TILE)], axis=1
    )


def start_slab(block_ref, step, mixed_ref, state_ref):
    rows = mixed_ref.shape[2]
    raw, score = pair_scores(block_ref[:rows], block_ref, rows, 0)
    eye = lax.broadcasted_iota(jnp.int32, (TILE, TILE), 0) == lax.broadcasted_iota(
        jnp.int32, (TILE, TILE), 1
    )
    own = jnp.concatenate(
        [
            jnp.sum(
                jnp.where(eye, raw[at : at + TILE, at : at + TILE], 0.0), axis=0, keepdims=True
            )
            for at in range(0, rows, TILE)
        ],
        axis=1,
    )
    top = jnp.maximum(own, jnp.max(score, axis=0, keepdims=True))
    weight = jnp.exp2(own - top)
    values = turned_values(block_ref, rows)
    total, mixed = add_source(score, values, top, weight, weight * values.astype(jnp.float32))
    mixed_ref[step] = mixed
    state_ref[step, 0:1] = top
    state_ref[step, 1:2] = total


def add_slab(block_ref, source_ref, turn, step, mixed_ref, state_ref):
    rows = mixed_ref.shape[2]
    score = pair_scores(source_ref[:rows], block_ref, rows, turn)[1]
    before = state_ref[step, 0:1]
    top = jnp.maximum(before, jnp.max(score, axis=0, keepdims=True))
    factor = jnp.exp2(before - top)
    total, mixed = add_source(
        score,
        turned_values(source_ref, rows),
        top,
        state_ref[step, 1:2] * factor,
        mixed_ref[step] * factor,
    )
    mixed_ref[step] = mixed
    state_ref[step, 0:1] = top
    state_ref[step, 1:2] = total


def add_pairs(place, steps, fresh, blocks, mixed_ref, state_ref):
    for step in fresh:
        start_slab(blocks[step], step, mixed_ref, state_ref)
    for one in steps:
        for two in fresh:
            if two in steps[: steps.index(one) + 1]:
                continue
            ahead = jnp.bitwise_xor(place, one) - jnp.bitwise_xor(place, two)

            @pl.when(ahead > 0)
            def _(one=one, two=two, ahead=ahead):
                add_slab(blocks[one], blocks[two], ahead, one, mixed_ref, state_ref)

            @pl.when(ahead < 0)
            def _(one=one, two=two, ahead=ahead):
                add_slab(blocks[two], blocks[one], -ahead, two, mixed_ref, state_ref)


def near_kernel(*refs, steps, head_total):
    blocks, weight_ref = refs[: len(steps)], refs[len(steps)]
    mixed_ref, state_ref, turned_ref, held, sem = refs[len(steps) + 1 :]
    me = lax.axis_index("head")
    depth = weight_ref.shape[0] // head_total
    features = weight_ref.shape[1] // head_total
    copies = []
    for other in range(head_total):
        start = pl.multiple_of(jnp.bitwise_xor(me, other) * depth, depth)
        cols = pl.ds(pl.multiple_of(me * features, features), features)
        copies.append(
            pltpu.make_async_copy(
                weight_ref.at[pl.ds(start, depth), cols], held.at[other], sem.at[other]
            )
        )
        copies[-1].start()
    add_pairs(lax.axis_index("place"), steps, steps, blocks, mixed_ref, state_ref)
    for other in range(head_total):
        copies[other].wait()
        turned_ref[other] = held[other].T


def more_kernel(*refs, group, fresh):
    blocks, (mixed_ref, state_ref, mixed_out, state_out) = refs[:group], refs[group:]
    for step in range(group):
        if step not in fresh:
            mixed_out[step] = mixed_ref[step]
            state_out[step] = state_ref[step]
    steps = list(range(group))
    add_pairs(lax.axis_index("place"), steps, fresh, blocks, mixed_out, state_out)


def far_kernel(*refs, group, halo, ready, last):
    blocks, (mixed_ref, state_ref) = refs[:group], refs[group : group + 2]
    pieces = refs[group + 2 : group + 2 + len(halo)]
    outs = refs[group + 2 + len(halo) :]
    out_refs, (mixed_out, state_out) = outs[: len(ready)], outs[len(ready) :]
    place = lax.axis_index("place")
    mixed_out[...] = mixed_ref[...]
    state_out[...] = state_ref[...]
    for piece_ref, (offset, choices) in zip(pieces, halo):
        for low in range(piece_ref.shape[0]):
            slabs = [choice[low] ^ at if choice else group for at, choice in enumerate(choices)]
            ahead = offset * group - pick(place, slabs)
            for step in range(group):
                turn = jnp.bitwise_xor(place, step) + ahead
                used = (turn < STEPS) & (turn > 0)

                @pl.when(used & (ahead > (offset - 1) * group))
                def _(low=low, step=step, turn=turn, piece_ref=piece_ref):
                    add_slab(
                        blocks[step], piece_ref.at[low], turn, step, mixed_out, state_out
                    )

    for step, out_ref in zip(ready, out_refs):
        out_ref[...] = (mixed_out[step] / state_out[step, 1:2]).astype(out_ref.dtype)


def hops(step):
    return step.bit_count()


def sending_order(group):
    return sorted(range(group), key=lambda step: (step > 0, -hops(step), step))


def halo_messages(group):
    messages = []
    for offset in range(1, -(-(STEPS - 1) // group) + 1):
        first = max(0, offset * group - STEPS + 1)
        early, late = [], []
        for place in range(group):
            needed = [step for step in range(group) if place ^ step >= first]
            early.append([step for step in needed if hops(step) < 2])
            late.append([step for step in needed if hops(step) > 1])
        common = min(len(steps) for steps in early)
        parts = [(False, [steps[:common] for steps in early])]
        parts += [(False, [steps[common:] for steps in early]), (True, late)]
        messages += [(is_late, offset, choices) for is_late, choices in parts if any(choices)]
    return messages


def pick(place, choices):
    result = jnp.int32(choices[-1])
    for at, choice in enumerate(choices[:-1]):
        result = jnp.where(place == at, jnp.int32(choice), result)
    return result


def project_kernel(turned_ref, *refs, group, head_total):
    mix_refs, out_ref, mix = refs[:-2], refs[-2], refs[-1]
    place = lax.axis_index("place")
    for other in range(head_total):
        for at, step in enumerate(sending_order(group)):
            mix[other, jnp.bitwise_xor(place, step)] = mix_refs[other * group + at][...]
    result = None
    for other in range(head_total):
        part = jnp.dot(
            turned_ref[other],
            mix[other].reshape(turned_ref.shape[2], out_ref.shape[1]),
            preferred_element_type=jnp.float32,
        )
        result = part if result is None else result + part
    out_ref[...] = result.astype(out_ref.dtype)


def swapped(value, axis, step):
    count = lax.axis_size(axis)
    return lax.ppermute(value, axis, [(source, source ^ step) for source in range(count)])


def halo_message(got, place, choices, rows):
    length = max(len(steps) for steps in choices)
    parts = []
    for low in range(length):
        steps = [choice[low] if choice else None for choice in choices]
        known = [step for step in steps if step is not None]
        piece = got[known[-1]][: 2 * rows]
        for at, step in enumerate(steps):
            if step is not None and step != known[-1]:
                piece = jnp.where(place == at, got[step][: 2 * rows], piece)
        parts.append(piece)
    return jnp.stack(parts)


def on_device(node_queries, node_keys, node_values, tile_index, tile_count, out_weight):
    rows, width = node_queries.shape
    group = width // HD
    groups = lax.axis_size("group")
    head_total = lax.axis_size("head")
    depth, feature_total = out_weight.shape
    features = feature_total // head_total
    bf16, f32 = jnp.bfloat16, jnp.float32
    shape = jax.ShapeDtypeStruct
    place = lax.axis_index("place")

    packed = pl.pallas_call(
        pack_kernel,
        out_shape=[shape((3 * rows + EXTRA, HD), bf16)] * group,
        in_specs=[HBM] * 5,
        out_specs=[VMEM] * group,
        scratch_shapes=[
            pltpu.VMEM((rows, width), bf16),
            pltpu.SMEM((rows // TILE, SLOTS, STEPS), jnp.int32),
            pltpu.SMEM((rows // TILE, STEPS), jnp.int32),
            pltpu.SemaphoreType.DMA((3 + 2 * group,)),
        ],
        compiler_params=PARAMS,
        name="pack",
    )(
        *[
            pltpu.with_memory_space_constraint(array, pltpu.HBM)
            for array in (
                node_queries,
                node_keys,
                node_values,
                jnp.transpose(tile_index, (1, 2, 0)),
                jnp.transpose(tile_count, (1, 0)),
            )
        ],
    )

    state_shapes = [shape((group, HD, rows), f32), shape((group, 8, rows), f32)]
    first_steps = [step for step in range(group) if hops(step) < 2]
    rest = [step for step in range(group) if hops(step) > 1]
    got = [packed[0]]
    messages = halo_messages(group)
    sent = {False: [], True: []}
    for step in range(group):
        if step:
            block = packed[step]
            if hops(step) > 1:
                block, got[1] = lax.optimization_barrier((block, got[1]))
            got.append(swapped(block, "place", step))
        for late, offset, choices in messages:
            if step != max(max(steps, default=0) for steps in choices):
                continue
            pairs = [
                (at * group + p, (at + offset) % groups * group + p)
                for at in range(groups)
                for p in range(group)
                if choices[p]
            ]
            message = halo_message(got, place, choices, rows)
            if late:
                message, state = lax.optimization_barrier((message, state))
            message, *got = lax.optimization_barrier([message, *got])
            arrived = lax.ppermute(message, ("group", "place"), pairs)
            sent[late].append(((offset, choices), arrived))
        if step == first_steps[-1]:
            mixed, state, turned = pl.pallas_call(
                functools.partial(near_kernel, steps=first_steps, head_total=head_total),
                out_shape=[*state_shapes, shape((head_total, features, depth // head_total), bf16)],
                in_specs=[VMEM] * len(first_steps) + [HBM],
                out_specs=[VMEM] * 3,
                scratch_shapes=[
                    pltpu.VMEM((head_total, depth // head_total, features), bf16),
                    pltpu.SemaphoreType.DMA((head_total,)),
                ],
                compiler_params=PARAMS,
                cost_estimate=pl.CostEstimate(flops=NEAR, transcendentals=1, bytes_accessed=1),
                name="near",
            )(
                *[got[step] for step in first_steps],
                pltpu.with_memory_space_constraint(out_weight, pltpu.HBM),
            )

    if rest:
        mixed, state = pl.pallas_call(
            functools.partial(more_kernel, group=group, fresh=rest),
            out_shape=state_shapes,
            in_specs=[VMEM] * (group + 2),
            out_specs=[VMEM] * 2,
            compiler_params=PARAMS,
            cost_estimate=pl.CostEstimate(flops=MORE, transcendentals=1, bytes_accessed=1),
            name="more",
        )(*got, mixed, state)

    mix = {}
    for late in (False, True):
        if late and not sent[late]:
            continue
        last = late or not sent[True]
        ready = [s for s in range(group) if s not in mix and (last or hops(s) > 1)]
        state_out = [] if last else state_shapes
        outs = pl.pallas_call(
            functools.partial(
                far_kernel,
                group=group,
                halo=[entry[0] for entry in sent[late]],
                ready=ready,
                last=last,
            ),
            out_shape=[shape((HD, rows), bf16)] * len(ready) + state_out,
            in_specs=[VMEM] * (group + 2 + len(sent[late])),
            out_specs=[VMEM] * (len(ready) + len(state_out)),
            scratch_shapes=[pltpu.VMEM(s.shape, f32) for s in state_shapes] if last else [],
            compiler_params=PARAMS,
            cost_estimate=pl.CostEstimate(flops=FAR, transcendentals=1, bytes_accessed=1),
            name="far",
        )(*got, mixed, state, *[entry[1] for entry in sent[late]])
        mix.update(zip(ready, outs))
        for step in ready:
            if step:
                mix[step] = swapped(mix[step], "place", step)
        if not last:
            mixed, state = outs[len(ready) :]

    mixes = [mix[step] for step in sending_order(group)]
    for other in range(1, head_total):
        mixes += [swapped(entry, "head", other) for entry in mixes[:group]]
    return pl.pallas_call(
        functools.partial(project_kernel, group=group, head_total=head_total),
        out_shape=shape((features, rows), bf16),
        in_specs=[VMEM] * (1 + head_total * group),
        out_specs=VMEM,
        scratch_shapes=[pltpu.VMEM((head_total, group, HD, rows), bf16)],
        compiler_params=PARAMS,
        name="project",
    )(turned, *mixes)


def solution(mesh):
    nodes, heads = mesh.devices.shape
    place = HEADS // heads
    split = Mesh(
        mesh.devices.reshape(nodes // place, place, heads), ("group", "place", "head")
    )
    node = ("group", "place")
    return jax.shard_map(
        on_device,
        mesh=split,
        in_specs=(
            P(node, "head"),
            P(node, "head"),
            P(node, "head"),
            P(None, node, None),
            P(None, node),
            P(),
        ),
        out_specs=P("head", node),
        check_vma=False,
    )
```

```python
import functools

import jax
import jax.numpy as jnp
from jax import lax
from jax.experimental import pallas as pl
from jax.experimental.pallas import tpu as pltpu
from jax.sharding import Mesh, PartitionSpec as P

HEADS = 8
HD = 128
TILE = 128
SLOTS = 2
STEPS = 4
LOG2E = 1.4426950408889634
SCALE = LOG2E * HD ** (-0.5)
MASKED = -1e30
EXTRA = 16
OWN = 10**9
NEAR = 10**9
MORE = 1
FAR = 10**9
VMEM = pl.BlockSpec(memory_space=pltpu.VMEM)
HBM = pl.BlockSpec(memory_space=pltpu.HBM)
PARAMS = pltpu.CompilerParams(vmem_limit_bytes=48 * 1024 * 1024)


def use_rows(index_ref, count_ref, tiles):
    row = lax.broadcasted_iota(jnp.int32, (EXTRA, HD), 0)
    uses = jnp.zeros((EXTRA, HD), jnp.float32)
    for turn in range(STEPS):
        for dest in range(tiles):
            for source in range(tiles):
                times = jnp.float32(0)
                for slot in range(SLOTS):
                    used = (slot < count_ref[dest, turn]) & (index_ref[dest, slot, turn] == source)
                    times += jnp.where(used, 1.0, 0.0)
                uses = jnp.where(row == (turn * tiles + dest) * tiles + source, times, uses)
    return uses


def pack_kernel(query_ref, key_ref, value_ref, index_ref, count_ref, *refs):
    out_refs, (values, index, count, sem) = refs[:-4], refs[-4:]
    rows, width = query_ref.shape
    group = width // HD
    tiles = rows // TILE
    place = lax.axis_index("place")
    value_copy = pltpu.make_async_copy(value_ref, values, sem.at[0])
    value_copy.start()
    table_copies = [
        pltpu.make_async_copy(index_ref, index, sem.at[1]),
        pltpu.make_async_copy(count_ref, count, sem.at[2]),
    ]
    for copy in table_copies:
        copy.start()
    copies = []
    for step in range(group):
        cols = pl.ds(pl.multiple_of(jnp.bitwise_xor(place, step) * HD, HD), HD)
        out = out_refs[step]
        copies += [
            pltpu.make_async_copy(
                key_ref.at[:, cols], out.at[pl.ds(0, rows)], sem.at[3 + 2 * step]
            ),
            pltpu.make_async_copy(
                query_ref.at[:, cols], out.at[pl.ds(2 * rows, rows)], sem.at[4 + 2 * step]
            ),
        ]
    for copy in copies:
        copy.start()
    for copy in table_copies:
        copy.wait()
    uses = use_rows(index, count, tiles).astype(jnp.bfloat16)
    value_copy.wait()
    for step in range(group):
        cols = pl.ds(pl.multiple_of(jnp.bitwise_xor(place, step) * HD, HD), HD)
        out = out_refs[step]
        out[3 * rows :] = uses
        for at in range(0, rows, TILE):
            out[rows + at : rows + at + TILE] = values[at : at + TILE, cols].T
    for copy in copies:
        copy.wait()


def use_bias(block_ref, rows, turn):
    tiles = rows // TILE
    uses = block_ref[3 * rows :].astype(jnp.float32)
    per_turn = tiles * tiles
    times = uses[:per_turn]
    for other in range(1, STEPS):
        times = jnp.where(turn == other, uses[other * per_turn : (other + 1) * per_turn], times)
    return jnp.where(times > 0.5, times - 1.0, MASKED)


def pair_scores(keys, block_ref, rows, turn):
    tiles = rows // TILE
    raw = (
        lax.dot_general(
            keys,
            block_ref[2 * rows : 3 * rows],
            (((1,), (1,)), ((), ())),
            preferred_element_type=jnp.float32,
        )
        * SCALE
    )
    bias = use_bias(block_ref, rows, turn)
    parts = []
    for source in range(tiles):
        line = jnp.concatenate(
            [bias[tile * tiles + source : tile * tiles + source + 1] for tile in range(tiles)],
            axis=1,
        )
        parts.append(raw[source * TILE : (source + 1) * TILE] + line)
    return raw, jnp.concatenate(parts, axis=0)


def add_source(score, values, top, total, mixed):
    weights = jnp.exp2(score - top)
    total = total + jnp.sum(weights, axis=0, keepdims=True)
    mixed = mixed + jnp.dot(
        values, weights.astype(jnp.bfloat16), preferred_element_type=jnp.float32
    )
    return total, mixed


def turned_values(source_ref, rows):
    return jnp.concatenate(
        [source_ref[rows + at : rows + at + TILE] for at in range(0, rows, TILE)], axis=1
    )


def start_slab(block_ref, step, mixed_ref, state_ref):
    rows = mixed_ref.shape[2]
    raw, score = pair_scores(block_ref[:rows], block_ref, rows, 0)
    eye = lax.broadcasted_iota(jnp.int32, (TILE, TILE), 0) == lax.broadcasted_iota(
        jnp.int32, (TILE, TILE), 1
    )
    own = jnp.concatenate(
        [
            jnp.sum(
                jnp.where(eye, raw[at : at + TILE, at : at + TILE], 0.0), axis=0, keepdims=True
            )
            for at in range(0, rows, TILE)
        ],
        axis=1,
    )
    top = jnp.maximum(own, jnp.max(score, axis=0, keepdims=True))
    weight = jnp.exp2(own - top)
    values = turned_values(block_ref, rows)
    total, mixed = add_source(score, values, top, weight, weight * values.astype(jnp.float32))
    mixed_ref[step] = mixed
    state_ref[step, 0:1] = top
    state_ref[step, 1:2] = total


def add_slab(block_ref, source_ref, turn, step, mixed_ref, state_ref):
    rows = mixed_ref.shape[2]
    score = pair_scores(source_ref[:rows], block_ref, rows, turn)[1]
    before = state_ref[step, 0:1]
    top = jnp.maximum(before, jnp.max(score, axis=0, keepdims=True))
    factor = jnp.exp2(before - top)
    total, mixed = add_source(
        score,
        turned_values(source_ref, rows),
        top,
        state_ref[step, 1:2] * factor,
        mixed_ref[step] * factor,
    )
    mixed_ref[step] = mixed
    state_ref[step, 0:1] = top
    state_ref[step, 1:2] = total


def add_pairs(place, steps, fresh, blocks, mixed_ref, state_ref):
    for step in fresh:
        start_slab(blocks[step], step, mixed_ref, state_ref)
    for one in steps:
        for two in fresh:
            if two in steps[: steps.index(one) + 1]:
                continue
            ahead = jnp.bitwise_xor(place, one) - jnp.bitwise_xor(place, two)

            @pl.when(ahead > 0)
            def _(one=one, two=two, ahead=ahead):
                add_slab(blocks[one], blocks[two], ahead, one, mixed_ref, state_ref)

            @pl.when(ahead < 0)
            def _(one=one, two=two, ahead=ahead):
                add_slab(blocks[two], blocks[one], -ahead, two, mixed_ref, state_ref)


def own_kernel(block_ref, weight_ref, mixed_ref, state_ref, turned_ref, held, sem, *, head_total):
    me = lax.axis_index("head")
    depth = weight_ref.shape[0] // head_total
    features = weight_ref.shape[1] // head_total
    copies = []
    for other in range(head_total):
        start = pl.multiple_of(jnp.bitwise_xor(me, other) * depth, depth)
        cols = pl.ds(pl.multiple_of(me * features, features), features)
        copies.append(
            pltpu.make_async_copy(
                weight_ref.at[pl.ds(start, depth), cols], held.at[other], sem.at[other]
            )
        )
        copies[-1].start()
    start_slab(block_ref, 0, mixed_ref, state_ref)
    for other in range(head_total):
        copies[other].wait()
        turned_ref[other] = held[other].T


def near_kernel(*refs, steps, fresh):
    blocks, (mixed_ref, state_ref, mixed_out, state_out) = refs[: len(steps)], refs[len(steps) :]
    for step in steps:
        if step not in fresh:
            mixed_out[step] = mixed_ref[step]
            state_out[step] = state_ref[step]
    add_pairs(lax.axis_index("place"), steps, fresh, blocks, mixed_out, state_out)


def far_kernel(*refs, group, halo, last):
    blocks, (mixed_ref, state_ref) = refs[:group], refs[group : group + 2]
    pieces = refs[group + 2 : group + 2 + len(halo)]
    outs = refs[group + 2 + len(halo) :]
    out_refs, (mixed_out, state_out) = outs[:-2], outs[-2:]
    place = lax.axis_index("place")
    mixed_out[...] = mixed_ref[...]
    state_out[...] = state_ref[...]
    for piece_ref, (offset, choices) in zip(pieces, halo):
        for low in range(piece_ref.shape[0]):
            slabs = [choice[low] ^ at for at, choice in enumerate(choices)]
            ahead = offset * group - pick(place, slabs)
            for step in range(group):
                turn = jnp.bitwise_xor(place, step) + ahead

                @pl.when(turn < STEPS)
                def _(low=low, step=step, turn=turn, piece_ref=piece_ref):
                    add_slab(
                        blocks[step], piece_ref.at[low], turn, step, mixed_out, state_out
                    )

    if last:
        for step, out_ref in zip(sending_order(group), out_refs):
            out_ref[...] = (mixed_out[step] / state_out[step, 1:2]).astype(out_ref.dtype)


def hops(step):
    return step.bit_count()


def sending_order(group):
    return sorted(range(group), key=lambda step: (step > 0, -hops(step), step))


def halo_messages(group):
    messages = []
    for offset in range(1, -(-(STEPS - 1) // group) + 1):
        first = max(0, offset * group - STEPS + 1)
        needed = [[step for step in range(group) if place ^ step >= first] for place in range(group)]
        early = min(len([step for step in steps if hops(step) < 2]) for steps in needed)
        messages.append((False, offset, [steps[:early] for steps in needed]))
        if early < group - first:
            messages.append((True, offset, [steps[early:] for steps in needed]))
    return messages


def pick(place, choices):
    result = jnp.int32(choices[-1])
    for at, choice in enumerate(choices[:-1]):
        result = jnp.where(place == at, jnp.int32(choice), result)
    return result


def project_kernel(turned_ref, *refs, group, head_total):
    mix_refs, out_ref, mix = refs[:-2], refs[-2], refs[-1]
    place = lax.axis_index("place")
    for other in range(head_total):
        for at, step in enumerate(sending_order(group)):
            mix[other, jnp.bitwise_xor(place, step)] = mix_refs[other * group + at][...]
    result = None
    for other in range(head_total):
        part = jnp.dot(
            turned_ref[other],
            mix[other].reshape(turned_ref.shape[2], out_ref.shape[1]),
            preferred_element_type=jnp.float32,
        )
        result = part if result is None else result + part
    out_ref[...] = result.astype(out_ref.dtype)


def swapped(value, axis, step):
    count = lax.axis_size(axis)
    return lax.ppermute(value, axis, [(source, source ^ step) for source in range(count)])


def halo_message(got, place, choices, rows):
    parts = []
    for steps in zip(*choices):
        piece = got[steps[-1]][: 2 * rows]
        for at, step in enumerate(steps):
            if step != steps[-1]:
                piece = jnp.where(place == at, got[step][: 2 * rows], piece)
        parts.append(piece)
    return jnp.stack(parts)


def on_device(node_queries, node_keys, node_values, tile_index, tile_count, out_weight):
    rows, width = node_queries.shape
    group = width // HD
    groups = lax.axis_size("group")
    head_total = lax.axis_size("head")
    depth, feature_total = out_weight.shape
    features = feature_total // head_total
    bf16, f32 = jnp.bfloat16, jnp.float32
    shape = jax.ShapeDtypeStruct
    place = lax.axis_index("place")

    packed = pl.pallas_call(
        pack_kernel,
        out_shape=[shape((3 * rows + EXTRA, HD), bf16)] * group,
        in_specs=[HBM] * 5,
        out_specs=[VMEM] * group,
        scratch_shapes=[
            pltpu.VMEM((rows, width), bf16),
            pltpu.SMEM((rows // TILE, SLOTS, STEPS), jnp.int32),
            pltpu.SMEM((rows // TILE, STEPS), jnp.int32),
            pltpu.SemaphoreType.DMA((3 + 2 * group,)),
        ],
        compiler_params=PARAMS,
        name="pack",
    )(
        *[
            pltpu.with_memory_space_constraint(array, pltpu.HBM)
            for array in (
                node_queries,
                node_keys,
                node_values,
                jnp.transpose(tile_index, (1, 2, 0)),
                jnp.transpose(tile_count, (1, 0)),
            )
        ],
    )

    def state_shapes(count):
        return [shape((count, HD, rows), f32), shape((count, 8, rows), f32)]

    def near(steps, fresh, mixed, state, cost):
        return pl.pallas_call(
            functools.partial(near_kernel, steps=steps, fresh=fresh),
            out_shape=state_shapes(len(steps)),
            in_specs=[VMEM] * (len(steps) + 2),
            out_specs=[VMEM] * 2,
            compiler_params=PARAMS,
            cost_estimate=pl.CostEstimate(flops=cost, transcendentals=1, bytes_accessed=1),
            name="near",
        )(*[got[step] for step in steps], mixed, state)

    mixed, state, turned = pl.pallas_call(
        functools.partial(own_kernel, head_total=head_total),
        out_shape=[*state_shapes(1), shape((head_total, features, depth // head_total), bf16)],
        in_specs=[VMEM, HBM],
        out_specs=[VMEM] * 3,
        scratch_shapes=[
            pltpu.VMEM((head_total, depth // head_total, features), bf16),
            pltpu.SemaphoreType.DMA((head_total,)),
        ],
        compiler_params=PARAMS,
        cost_estimate=pl.CostEstimate(flops=OWN, transcendentals=1, bytes_accessed=1),
        name="own",
    )(packed[0], pltpu.with_memory_space_constraint(out_weight, pltpu.HBM))

    first_steps = [step for step in range(group) if hops(step) < 2]
    rest = [step for step in range(group) if hops(step) > 1]
    got = [packed[0]]
    messages = halo_messages(group)
    sent = {False: [], True: []}
    for step in range(group):
        if step:
            block = packed[step]
            if hops(step) > 1:
                block, turned = lax.optimization_barrier((block, turned))
            got.append(swapped(block, "place", step))
        for late, offset, choices in messages:
            if step != max(max(steps) for steps in choices):
                continue
            pairs = [(source, (source + offset) % groups) for source in range(groups)]
            message = halo_message(got, place, choices, rows)
            if late:
                message, state = lax.optimization_barrier((message, state))
            message, *got = lax.optimization_barrier([message, *got])
            sent[late].append(((offset, choices), lax.ppermute(message, "group", pairs)))
        if step == first_steps[-1]:
            mixed, state = near(first_steps, first_steps[1:], mixed, state, NEAR)
    if rest:
        mixed, state = near(list(range(group)), rest, mixed, state, MORE)

    for late in (False, True):
        if not sent[late]:
            continue
        last = late or not sent[True]
        outs = pl.pallas_call(
            functools.partial(
                far_kernel, group=group, halo=[entry[0] for entry in sent[late]], last=last
            ),
            out_shape=[shape((HD, rows), bf16)] * group if last else state_shapes(group),
            in_specs=[VMEM] * (group + 2 + len(sent[late])),
            out_specs=[VMEM] * (group if last else 2),
            scratch_shapes=[pltpu.VMEM(s.shape, f32) for s in state_shapes(group)] if last else [],
            compiler_params=PARAMS,
            cost_estimate=pl.CostEstimate(flops=FAR, transcendentals=1, bytes_accessed=1),
            name="far",
        )(*got, mixed, state, *[entry[1] for entry in sent[late]])
        if not last:
            mixed, state = outs

    order = sending_order(group)
    mixes = [outs[0]] + [swapped(out, "place", step) for step, out in zip(order[1:], outs[1:])]
    for other in range(1, head_total):
        mixes += [swapped(entry, "head", other) for entry in mixes[:group]]
    return pl.pallas_call(
        functools.partial(project_kernel, group=group, head_total=head_total),
        out_shape=shape((features, rows), bf16),
        in_specs=[VMEM] * (1 + head_total * group),
        out_specs=VMEM,
        scratch_shapes=[pltpu.VMEM((head_total, group, HD, rows), bf16)],
        compiler_params=PARAMS,
        name="project",
    )(turned, *mixes)


def solution(mesh):
    nodes, heads = mesh.devices.shape
    place = HEADS // heads
    split = Mesh(
        mesh.devices.reshape(nodes // place, place, heads), ("group", "place", "head")
    )
    node = ("group", "place")
    return jax.shard_map(
        on_device,
        mesh=split,
        in_specs=(
            P(node, "head"),
            P(node, "head"),
            P(node, "head"),
            P(None, node, None),
            P(None, node),
            P(),
        ),
        out_specs=P("head", node),
        check_vma=False,
    )
```

```python
import functools

import jax
import jax.numpy as jnp
from jax import lax
from jax.experimental import pallas as pl
from jax.experimental.pallas import tpu as pltpu
from jax.sharding import Mesh, PartitionSpec as P

HEADS = 8
HD = 128
TILE = 128
SLOTS = 2
STEPS = 4
LOG2E = 1.4426950408889634
SCALE = LOG2E * HD ** (-0.5)
MASKED = -1e30
EXTRA = 16
OWN = 10**9
NEAR = 1
FAR = 4 * 10**9
VMEM = pl.BlockSpec(memory_space=pltpu.VMEM)
HBM = pl.BlockSpec(memory_space=pltpu.HBM)
PARAMS = pltpu.CompilerParams(vmem_limit_bytes=48 * 1024 * 1024)


def use_rows(index_ref, count_ref, tiles):
    row = lax.broadcasted_iota(jnp.int32, (EXTRA, HD), 0)
    uses = jnp.zeros((EXTRA, HD), jnp.float32)
    for turn in range(STEPS):
        for dest in range(tiles):
            for source in range(tiles):
                times = jnp.float32(0)
                for slot in range(SLOTS):
                    used = (slot < count_ref[dest, turn]) & (index_ref[dest, slot, turn] == source)
                    times += jnp.where(used, 1.0, 0.0)
                uses = jnp.where(row == (turn * tiles + dest) * tiles + source, times, uses)
    return uses


def hops(step):
    return step.bit_count()


def query_places(refs, group, rows):
    apart = iter(refs[group:])
    return [
        next(apart) if hops(step) > 1 else refs[step].at[pl.ds(2 * rows, rows + EXTRA)]
        for step in range(group)
    ]


def pack_kernel(query_ref, key_ref, value_ref, index_ref, count_ref, *refs):
    out_refs, (values, index, count, sem) = refs[:-4], refs[-4:]
    group = query_ref.shape[1] // HD
    block_refs, query_refs = out_refs[:group], query_places(out_refs, group, query_ref.shape[0])
    rows = query_ref.shape[0]
    tiles = rows // TILE
    place = lax.axis_index("place")
    value_copy = pltpu.make_async_copy(value_ref, values, sem.at[0])
    value_copy.start()
    table_copies = [
        pltpu.make_async_copy(index_ref, index, sem.at[1]),
        pltpu.make_async_copy(count_ref, count, sem.at[2]),
    ]
    for copy in table_copies:
        copy.start()
    copies = []
    for step in range(group):
        cols = pl.ds(pl.multiple_of(jnp.bitwise_xor(place, step) * HD, HD), HD)
        copies += [
            pltpu.make_async_copy(
                key_ref.at[:, cols], block_refs[step].at[pl.ds(0, rows)], sem.at[3 + 2 * step]
            ),
            pltpu.make_async_copy(
                query_ref.at[:, cols], query_refs[step].at[pl.ds(0, rows)], sem.at[4 + 2 * step]
            ),
        ]
    for copy in copies:
        copy.start()
    for copy in table_copies:
        copy.wait()
    uses = use_rows(index, count, tiles).astype(jnp.bfloat16)
    value_copy.wait()
    for step in range(group):
        cols = pl.ds(pl.multiple_of(jnp.bitwise_xor(place, step) * HD, HD), HD)
        out = block_refs[step]
        query_refs[step][rows:] = uses
        for at in range(0, rows, TILE):
            out[rows + at : rows + at + TILE] = values[at : at + TILE, cols].T
    for copy in copies:
        copy.wait()


def source_scores(keys, query_uses, turn, rows):
    tiles = rows // TILE
    raw = (
        lax.dot_general(
            keys, query_uses[:rows], (((1,), (1,)), ((), ())), preferred_element_type=jnp.float32
        )
        * SCALE
    )
    parts = []
    for source in range(tiles):
        bias = []
        for tile in range(tiles):
            at = rows + (turn * tiles + tile) * tiles + source
            times = query_uses[at : at + 1].astype(jnp.float32)
            bias.append(jnp.where(times > 0.5, times - 1.0, MASKED))
        parts.append(
            raw[source * TILE : (source + 1) * TILE] + jnp.concatenate(bias, axis=1)
        )
    return raw, jnp.concatenate(parts, axis=0)


def slab_values(kv_ref, slot, rows):
    return jnp.concatenate(
        [kv_ref[slot, rows + at : rows + at + TILE] for at in range(0, rows, TILE)], axis=1
    )


def add_sources(scores, values, top, total, mixed):
    for score, value in zip(scores, values):
        weights = jnp.exp2(score - top)
        total = total + jnp.sum(weights, axis=0, keepdims=True)
        mixed = mixed + jnp.dot(
            value, weights.astype(jnp.bfloat16), preferred_element_type=jnp.float32
        )
    return total, mixed


def turn_kernel(block_ref, weight_ref, turned_ref, held, sem, *, head_total):
    me = lax.axis_index("head")
    depth = weight_ref.shape[0] // head_total
    features = weight_ref.shape[1] // head_total
    copies = []
    for other in range(head_total):
        start = pl.multiple_of(jnp.bitwise_xor(me, other) * depth, depth)
        cols = pl.ds(pl.multiple_of(me * features, features), features)
        copies.append(
            pltpu.make_async_copy(
                weight_ref.at[pl.ds(start, depth), cols], held.at[other], sem.at[other]
            )
        )
        copies[-1].start()
    for other in range(head_total):
        copies[other].wait()
        turned_ref[other] = held[other].T


def near_kernel(*refs, group):
    got_refs, (query_ref, mixed_ref, state_ref, kv) = refs[:-4], refs[-4:]
    rows = mixed_ref.shape[2]
    place = lax.axis_index("place")
    query_refs = query_places(got_refs, group, rows)
    for step in range(group):
        slab = jnp.bitwise_xor(place, step)
        kv[slab] = got_refs[step][: 2 * rows]
        query_ref[slab] = query_refs[step][...]
    eye = lax.broadcasted_iota(jnp.int32, (TILE, TILE), 0) == lax.broadcasted_iota(
        jnp.int32, (TILE, TILE), 1
    )
    for dest in range(group):
        scores, values = [], []
        query_uses = query_ref[dest]
        for turn in range(STEPS):
            slab = dest - turn
            if slab < 0:
                continue
            raw, score = source_scores(kv[slab, :rows], query_uses, turn, rows)
            if turn == 0:
                own = jnp.concatenate(
                    [
                        jnp.sum(
                            jnp.where(eye, raw[at : at + TILE, at : at + TILE], 0.0),
                            axis=0,
                            keepdims=True,
                        )
                        for at in range(0, rows, TILE)
                    ],
                    axis=1,
                )
            scores.append(score)
            values.append(slab_values(kv, slab, rows))
        top = own
        for score in scores:
            top = jnp.maximum(top, jnp.max(score, axis=0, keepdims=True))
        weight = jnp.exp2(own - top)
        total, mixed = add_sources(
            scores, values, top, weight, weight * values[0].astype(jnp.float32)
        )
        mixed_ref[dest] = mixed
        state_ref[dest, 0:1] = top
        state_ref[dest, 1:2] = total


def halo_steps(group, first):
    return [[k for k in range(group) if place ^ k >= first] for place in range(group)]


def sending_order(group):
    return sorted(range(group), key=lambda step: (step > 0, -hops(step), step))


def message_parts(total):
    return [(0, total)] if total < 3 else [(0, total - 1), (total - 1, total)]


def pick(place, choices):
    result = jnp.int32(choices[-1])
    for at, choice in enumerate(choices[:-1]):
        result = jnp.where(place == at, jnp.int32(choice), result)
    return result


def far_kernel(*refs, group, halo, at, last):
    query_ref, mixed_ref, state_ref, far_ref = refs[:4]
    if last:
        out_refs, (mixed_out, state_out, done) = refs[4:-3], refs[-3:]
    else:
        mixed_out, state_out = refs[4:]
    rows = mixed_ref.shape[2]
    place = lax.axis_index("place")
    offset, first = halo
    steps = halo_steps(group, first)
    mixed_out[...] = mixed_ref[...]
    state_out[...] = state_ref[...]
    for low in range(far_ref.shape[0]):
        slabs = [p ^ steps[p][at + low] for p in range(group)]
        mine = pick(place, slabs)
        for slab in sorted(set(slabs)):

            @pl.when(mine == slab)
            def _(low=low, slab=slab):
                value = slab_values(far_ref, low, rows)
                for dest in range(group):
                    turn = dest + offset * group - slab
                    if turn >= STEPS:
                        continue
                    score = source_scores(far_ref[low, :rows], query_ref[dest], turn, rows)[1]
                    before = state_out[dest, 0:1]
                    top = jnp.maximum(before, jnp.max(score, axis=0, keepdims=True))
                    factor = jnp.exp2(before - top)
                    total, mixed = add_sources(
                        [score],
                        [value],
                        top,
                        state_out[dest, 1:2] * factor,
                        mixed_out[dest] * factor,
                    )
                    mixed_out[dest] = mixed
                    state_out[dest, 0:1] = top
                    state_out[dest, 1:2] = total

    if last:
        for dest in range(group):
            done[dest] = (mixed_out[dest] / state_out[dest, 1:2]).astype(done.dtype)
        for step, out_ref in zip(sending_order(group), out_refs):
            out_ref[...] = done[jnp.bitwise_xor(place, step)]


def project_kernel(turned_ref, *refs, group, head_total):
    mix_refs, out_ref, mix = refs[:-2], refs[-2], refs[-1]
    place = lax.axis_index("place")
    for other in range(head_total):
        for at, step in enumerate(sending_order(group)):
            mix[other, jnp.bitwise_xor(place, step)] = mix_refs[other * group + at][...]
    result = None
    for other in range(head_total):
        part = jnp.dot(
            turned_ref[other],
            mix[other].reshape(turned_ref.shape[2], out_ref.shape[1]),
            preferred_element_type=jnp.float32,
        )
        result = part if result is None else result + part
    out_ref[...] = result.astype(out_ref.dtype)


def swapped(value, axis, step):
    count = lax.axis_size(axis)
    return lax.ppermute(value, axis, [(source, source ^ step) for source in range(count)])


def on_device(node_queries, node_keys, node_values, tile_index, tile_count, out_weight):
    rows, width = node_queries.shape
    group = width // HD
    groups = lax.axis_size("group")
    head_total = lax.axis_size("head")
    depth, feature_total = out_weight.shape
    features = feature_total // head_total
    bf16, f32 = jnp.bfloat16, jnp.float32
    shape = jax.ShapeDtypeStruct
    place = lax.axis_index("place")

    apart = [step for step in range(group) if hops(step) > 1]
    whole_block, query_block = shape((3 * rows + EXTRA, HD), bf16), shape((rows + EXTRA, HD), bf16)
    packed = pl.pallas_call(
        pack_kernel,
        out_shape=[
            shape((2 * rows, HD), bf16) if step in apart else whole_block for step in range(group)
        ]
        + [query_block] * len(apart),
        in_specs=[HBM] * 5,
        out_specs=[VMEM] * (group + len(apart)),
        scratch_shapes=[
            pltpu.VMEM((rows, width), bf16),
            pltpu.SMEM((rows // TILE, SLOTS, STEPS), jnp.int32),
            pltpu.SMEM((rows // TILE, STEPS), jnp.int32),
            pltpu.SemaphoreType.DMA((3 + 2 * group,)),
        ],
        compiler_params=PARAMS,
        name="pack",
    )(
        *[
            pltpu.with_memory_space_constraint(array, pltpu.HBM)
            for array in (
                node_queries,
                node_keys,
                node_values,
                jnp.transpose(tile_index, (1, 2, 0)),
                jnp.transpose(tile_count, (1, 0)),
            )
        ],
    )

    turned = pl.pallas_call(
        functools.partial(turn_kernel, head_total=head_total),
        out_shape=shape((head_total, features, depth // head_total), bf16),
        in_specs=[HBM, HBM],
        out_specs=VMEM,
        scratch_shapes=[
            pltpu.VMEM((head_total, depth // head_total, features), bf16),
            pltpu.SemaphoreType.DMA((head_total,)),
        ],
        compiler_params=PARAMS,
        cost_estimate=pl.CostEstimate(flops=OWN, transcendentals=1, bytes_accessed=1),
        name="turn",
    )(packed[0], pltpu.with_memory_space_constraint(out_weight, pltpu.HBM))

    halos = []
    for offset in range(1, -(-(STEPS - 1) // group) + 1):
        halos.append((offset, max(0, offset * group - STEPS + 1)))
    got, far = [packed[0]], []
    waiting = [
        (halo, part, max(row[part[1] - 1] for row in halo_steps(group, halo[1])))
        for halo in halos
        for part in message_parts(group - halo[1])
    ]
    for step in range(group):
        if step:
            block = packed[step]
            if hops(step) > 1:
                block, got[1], turned = lax.optimization_barrier((block, got[1], turned))
            got.append(swapped(block, "place", step))
        for (offset, first), (at, until), needed in waiting:
            if needed != step:
                continue
            steps = halo_steps(group, first)
            pairs = [(source, (source + offset) % groups) for source in range(groups)]
            parts = []
            for low in range(at, until):
                piece = got[steps[-1][low]][: 2 * rows]
                for p in range(group - 1):
                    if steps[p][low] != steps[-1][low]:
                        piece = jnp.where(place == p, got[steps[p][low]][: 2 * rows], piece)
                parts.append(piece)
            message = jnp.stack(parts)
            message, *got = lax.optimization_barrier([message, *got])
            far.append(((offset, first), at, lax.ppermute(message, "group", pairs)))

    far_queries = [
        swapped(block, "place", step) for step, block in zip(apart, packed[group:])
    ]

    queries, mixed, state = pl.pallas_call(
        functools.partial(near_kernel, group=group),
        out_shape=(
            shape((group, rows + EXTRA, HD), bf16),
            shape((group, HD, rows), f32),
            shape((group, 8, rows), f32),
        ),
        in_specs=[VMEM] * (group + len(apart)),
        out_specs=(VMEM, VMEM, VMEM),
        scratch_shapes=[pltpu.VMEM((group, 2 * rows, HD), bf16)],
        compiler_params=PARAMS,
        cost_estimate=pl.CostEstimate(flops=NEAR, transcendentals=1, bytes_accessed=1),
        name="near",
    )(*got, *far_queries)

    for number, (halo, at, message) in enumerate(far):
        last = number == len(far) - 1
        state_shapes = [shape(mixed.shape, f32), shape(state.shape, f32)]
        outs = pl.pallas_call(
            functools.partial(far_kernel, group=group, halo=halo, at=at, last=last),
            out_shape=[shape((HD, rows), bf16)] * group if last else state_shapes,
            in_specs=[VMEM] * 4,
            out_specs=[VMEM] * (group if last else 2),
            scratch_shapes=[
                pltpu.VMEM(mixed.shape, f32),
                pltpu.VMEM(state.shape, f32),
                pltpu.VMEM((group, HD, rows), bf16),
            ]
            if last
            else [],
            compiler_params=PARAMS,
            cost_estimate=pl.CostEstimate(
                flops=FAR, transcendentals=1, bytes_accessed=1
            ),
            name="far",
        )(queries, mixed, state, message)
        if not last:
            mixed, state = outs

    order = sending_order(group)
    mixes = [outs[0]] + [swapped(out, "place", step) for step, out in zip(order[1:], outs[1:])]
    for other in range(1, head_total):
        mixes += [swapped(mix, "head", other) for mix in mixes[:group]]
    return pl.pallas_call(
        functools.partial(project_kernel, group=group, head_total=head_total),
        out_shape=shape((features, rows), bf16),
        in_specs=[VMEM] * (1 + len(mixes)),
        out_specs=VMEM,
        scratch_shapes=[pltpu.VMEM((head_total, group, HD, rows), bf16)],
        compiler_params=PARAMS,
        name="project",
    )(turned, *mixes)


def solution(mesh):
    nodes, heads = mesh.devices.shape
    place = HEADS // heads
    split = Mesh(
        mesh.devices.reshape(nodes // place, place, heads), ("group", "place", "head")
    )
    node = ("group", "place")
    return jax.shard_map(
        on_device,
        mesh=split,
        in_specs=(
            P(node, "head"),
            P(node, "head"),
            P(node, "head"),
            P(None, node, None),
            P(None, node),
            P(),
        ),
        out_specs=P("head", node),
        check_vma=False,
    )
```

```python
import functools

import jax
import jax.numpy as jnp
from jax import lax
from jax.experimental import pallas as pl
from jax.experimental.pallas import tpu as pltpu
from jax.sharding import Mesh, PartitionSpec as P

HEADS = 8
HD = 128
TILE = 128
SLOTS = 2
STEPS = 4
LOG2E = 1.4426950408889634
SCALE = LOG2E * HD ** (-0.5)
MASKED = -1e30
EXTRA = 16
OWN = 10**9
NEAR = 1000000000
MORE = 1000000000
FAR = 1
VMEM = pl.BlockSpec(memory_space=pltpu.VMEM)
HBM = pl.BlockSpec(memory_space=pltpu.HBM)
PARAMS = pltpu.CompilerParams(vmem_limit_bytes=48 * 1024 * 1024)


def use_rows(index_ref, count_ref, tiles):
    row = lax.broadcasted_iota(jnp.int32, (EXTRA, HD), 0)
    uses = jnp.zeros((EXTRA, HD), jnp.float32)
    for turn in range(STEPS):
        for dest in range(tiles):
            for source in range(tiles):
                times = jnp.float32(0)
                for slot in range(SLOTS):
                    used = (slot < count_ref[dest, turn]) & (index_ref[dest, slot, turn] == source)
                    times += jnp.where(used, 1.0, 0.0)
                uses = jnp.where(row == (turn * tiles + dest) * tiles + source, times, uses)
    return uses


def hops(step):
    return step.bit_count()


def query_places(refs, group, rows):
    apart = iter(refs[group:])
    return [
        next(apart) if hops(step) > 1 else refs[step].at[pl.ds(2 * rows, rows + EXTRA)]
        for step in range(group)
    ]


def pack_kernel(query_ref, key_ref, value_ref, index_ref, count_ref, *refs):
    out_refs, (values, index, count, sem) = refs[:-4], refs[-4:]
    group = query_ref.shape[1] // HD
    block_refs, query_refs = out_refs[:group], query_places(out_refs, group, query_ref.shape[0])
    rows = query_ref.shape[0]
    tiles = rows // TILE
    place = lax.axis_index("place")
    value_copy = pltpu.make_async_copy(value_ref, values, sem.at[0])
    value_copy.start()
    table_copies = [
        pltpu.make_async_copy(index_ref, index, sem.at[1]),
        pltpu.make_async_copy(count_ref, count, sem.at[2]),
    ]
    for copy in table_copies:
        copy.start()
    copies = []
    for step in range(group):
        cols = pl.ds(pl.multiple_of(jnp.bitwise_xor(place, step) * HD, HD), HD)
        copies += [
            pltpu.make_async_copy(
                key_ref.at[:, cols], block_refs[step].at[pl.ds(0, rows)], sem.at[3 + 2 * step]
            ),
            pltpu.make_async_copy(
                query_ref.at[:, cols], query_refs[step].at[pl.ds(0, rows)], sem.at[4 + 2 * step]
            ),
        ]
    for copy in copies:
        copy.start()
    for copy in table_copies:
        copy.wait()
    uses = use_rows(index, count, tiles).astype(jnp.bfloat16)
    value_copy.wait()
    for step in range(group):
        cols = pl.ds(pl.multiple_of(jnp.bitwise_xor(place, step) * HD, HD), HD)
        out = block_refs[step]
        query_refs[step][rows:] = uses
        for at in range(0, rows, TILE):
            out[rows + at : rows + at + TILE] = values[at : at + TILE, cols].T
    for copy in copies:
        copy.wait()


def pair_scores(keys, query_ref, turn):
    rows = keys.shape[0]
    tiles = rows // TILE
    raw = (
        lax.dot_general(
            keys, query_ref[:rows], (((1,), (1,)), ((), ())), preferred_element_type=jnp.float32
        )
        * SCALE
    )
    uses = query_ref[rows:].astype(jnp.float32)
    parts = []
    for source in range(tiles):
        bias = []
        for tile in range(tiles):
            at = (turn * tiles + tile) * tiles + source
            times = uses[at : at + 1]
            bias.append(jnp.where(times > 0.5, times - 1.0, MASKED))
        parts.append(
            raw[source * TILE : (source + 1) * TILE] + jnp.concatenate(bias, axis=1)
        )
    return raw, jnp.concatenate(parts, axis=0)


def own_scores(raw):
    eye = lax.broadcasted_iota(jnp.int32, (TILE, TILE), 0) == lax.broadcasted_iota(
        jnp.int32, (TILE, TILE), 1
    )
    return jnp.concatenate(
        [
            jnp.sum(
                jnp.where(eye, raw[at : at + TILE, at : at + TILE], 0.0), axis=0, keepdims=True
            )
            for at in range(0, raw.shape[0], TILE)
        ],
        axis=1,
    )


def turned_values(source_ref, rows):
    return jnp.concatenate(
        [source_ref[rows + at : rows + at + TILE] for at in range(0, rows, TILE)], axis=1
    )


def attend(query_ref, sources, before):
    rows = query_ref.shape[0] - EXTRA
    scores = []
    for source_ref, turn in sources:
        raw, score = pair_scores(source_ref[:rows], query_ref, turn)
        scores.append(score)
        if turn == 0:
            own = own_scores(raw)
    top = own if before is None else before[0]
    for score in scores:
        top = jnp.maximum(top, jnp.max(score, axis=0, keepdims=True))
    if before is None:
        total = jnp.exp2(own - top)
        own_ref = next(source_ref for source_ref, turn in sources if turn == 0)
        mixed = total * turned_values(own_ref, rows).astype(jnp.float32)
    else:
        factor = jnp.exp2(before[0] - top)
        total, mixed = before[1] * factor, before[2] * factor
    for score, (source_ref, _) in zip(scores, sources):
        weights = jnp.exp2(score - top)
        total = total + jnp.sum(weights, axis=0, keepdims=True)
        mixed = mixed + jnp.dot(
            turned_values(source_ref, rows),
            weights.astype(jnp.bfloat16),
            preferred_element_type=jnp.float32,
        )
    return top, total, mixed


def sources_of(group, place, step):
    result = []
    for turn in range(STEPS):
        slab = (place ^ step) - turn
        result.append(((-(slab // group), place ^ (slab % group)), turn))
    return result


def stage_plan(group):
    steps = list(range(group))
    near = [step for step in steps if hops(step) < 2]
    stages = [(near, lambda offset, step: hops(step) < 2 and (offset == 0 or step == 0))]
    if len(near) < group:
        stages.append((steps, lambda offset, step: offset == 0 or step == 0))
    stages.append((steps, lambda offset, step: offset == 0 or hops(step) < 2))
    if len(near) < group:
        stages.append((steps, lambda offset, step: True))
    plan, taken = [], set()
    for dests, there in stages:
        work = []
        for place in range(group):
            table = {}
            for dest in dests:
                todo = [
                    (key, turn)
                    for key, turn in sources_of(group, place, dest)
                    if there(*key) and (place, dest, turn) not in taken
                ]
                taken.update((place, dest, turn) for _, turn in todo)
                if todo:
                    table[dest] = todo
            work.append(table)
        plan.append(work)
    return plan


def attend_kernel(*refs, names, work, started, active, ready, rows):
    named = dict(zip(names, refs))
    outs = refs[len(names) :]
    out_refs, state_refs = dict(zip(ready, outs)), outs[len(ready) :]
    group = len(work)

    def block(offset, step):
        for name in named:
            if name[0] == "halo" and name[1] == offset and step in name[2]:
                return named[name].at[name[2].index(step)]
        return named.get(("block", step), named.get(("kv", step)))

    def queries(step):
        if ("q", step) in named:
            return named["q", step]
        return named["block", step].at[pl.ds(2 * rows, rows + EXTRA)]

    here = lax.axis_index("place")
    for place in range(group):

        @pl.when(here == place)
        def _(place=place):
            for step in active:
                before = None
                if step in started:
                    mixed_ref, state_ref = named["mixed",], named["state",]
                    before = (state_ref[step, 0:1], state_ref[step, 1:2], mixed_ref[step])
                todo = [(block(*key), turn) for key, turn in work[place].get(step, [])]
                top, total, mixed = attend(queries(step), todo, before) if todo else before
                if step in ready:
                    out_refs[step][...] = (mixed / total).astype(out_refs[step].dtype)
                else:
                    state_refs[0][step] = mixed
                    state_refs[1][step, 0:1] = top
                    state_refs[1][step, 1:2] = total


def turn_kernel(block_ref, weight_ref, turned_ref, held, sem, *, head_total):
    me = lax.axis_index("head")
    depth = weight_ref.shape[0] // head_total
    features = weight_ref.shape[1] // head_total
    copies = []
    for other in range(head_total):
        start = pl.multiple_of(jnp.bitwise_xor(me, other) * depth, depth)
        cols = pl.ds(pl.multiple_of(me * features, features), features)
        copies.append(
            pltpu.make_async_copy(
                weight_ref.at[pl.ds(start, depth), cols], held.at[other], sem.at[other]
            )
        )
        copies[-1].start()
    for other in range(head_total):
        copies[other].wait()
        turned_ref[other] = held[other].T


def sending_order(group):
    return sorted(range(group), key=lambda step: (step > 0, -hops(step), step))


def project_kernel(turned_ref, *refs, group, head_total):
    mix_refs, out_ref, mix = refs[:-2], refs[-2], refs[-1]
    place = lax.axis_index("place")
    for other in range(head_total):
        for at, step in enumerate(sending_order(group)):
            mix[other, jnp.bitwise_xor(place, step)] = mix_refs[other * group + at][...]
    result = None
    for other in range(head_total):
        part = jnp.dot(
            turned_ref[other],
            mix[other].reshape(turned_ref.shape[2], out_ref.shape[1]),
            preferred_element_type=jnp.float32,
        )
        result = part if result is None else result + part
    out_ref[...] = result.astype(out_ref.dtype)


def swapped(value, axis, step):
    count = lax.axis_size(axis)
    return lax.ppermute(value, axis, [(source, source ^ step) for source in range(count)])


def on_device(node_queries, node_keys, node_values, tile_index, tile_count, out_weight):
    rows, width = node_queries.shape
    group = width // HD
    groups = lax.axis_size("group")
    head_total = lax.axis_size("head")
    depth, feature_total = out_weight.shape
    features = feature_total // head_total
    bf16, f32 = jnp.bfloat16, jnp.float32
    shape = jax.ShapeDtypeStruct

    apart = [step for step in range(group) if hops(step) > 1]
    whole_block, query_block = shape((3 * rows + EXTRA, HD), bf16), shape((rows + EXTRA, HD), bf16)
    packed = pl.pallas_call(
        pack_kernel,
        out_shape=[
            shape((2 * rows, HD), bf16) if step in apart else whole_block for step in range(group)
        ]
        + [query_block] * len(apart),
        in_specs=[HBM] * 5,
        out_specs=[VMEM] * (group + len(apart)),
        scratch_shapes=[
            pltpu.VMEM((rows, width), bf16),
            pltpu.SMEM((rows // TILE, SLOTS, STEPS), jnp.int32),
            pltpu.SMEM((rows // TILE, STEPS), jnp.int32),
            pltpu.SemaphoreType.DMA((3 + 2 * group,)),
        ],
        compiler_params=PARAMS,
        name="pack",
    )(
        *[
            pltpu.with_memory_space_constraint(array, pltpu.HBM)
            for array in (
                node_queries,
                node_keys,
                node_values,
                jnp.transpose(tile_index, (1, 2, 0)),
                jnp.transpose(tile_count, (1, 0)),
            )
        ],
    )

    turned = pl.pallas_call(
        functools.partial(turn_kernel, head_total=head_total),
        out_shape=shape((head_total, features, depth // head_total), bf16),
        in_specs=[HBM, HBM],
        out_specs=VMEM,
        scratch_shapes=[
            pltpu.VMEM((head_total, depth // head_total, features), bf16),
            pltpu.SemaphoreType.DMA((head_total,)),
        ],
        compiler_params=PARAMS,
        cost_estimate=pl.CostEstimate(flops=OWN, transcendentals=1, bytes_accessed=1),
        name="turn",
    )(packed[0], pltpu.with_memory_space_constraint(out_weight, pltpu.HBM))

    offsets = list(range(1, -(-(STEPS - 1) // group) + 1))
    plan = stage_plan(group)
    finish = [
        max(at for at, work in enumerate(plan) for table in work if step in table)
        for step in range(group)
    ]
    arrays = {("block", 0): packed[0]}
    near = [step for step in range(1, group) if hops(step) < 2]
    first = ("halo", 1, (0,))

    def send_on(steps):
        blocks = [arrays.get(("block", step), arrays.get(("kv", step))) for step in steps]
        message = jnp.stack([block[: 2 * rows] for block in blocks])
        if steps == near:
            message, arrays[first] = lax.optimization_barrier((message, arrays[first]))
        if steps[0] in apart:
            message, arrays["state",] = lax.optimization_barrier((message, arrays["state",]))
        for offset in offsets:
            pairs = [(source, (source + offset) % groups) for source in range(groups)]
            arrays["halo", offset, tuple(steps)] = lax.ppermute(message, "group", pairs)

    def stage(at, cost):
        work = plan[at]
        started = [
            step
            for step in range(group)
            if finish[step] >= at and any(step in table for work in plan[:at] for table in work)
        ]
        active = sorted(set(started) | {step for table in work for step in table})
        ready = [step for step in active if finish[step] == at]
        keys = {key for table in work for todo in table.values() for key, _ in todo}
        dests = {step for table in work for step in table}
        names = []
        for name in arrays:
            if name[0] == "halo":
                used = any((name[1], step) in keys for step in name[2])
            elif name[0] in ("block", "kv"):
                used = (0, name[1]) in keys or (name[0] == "block" and name[1] in dests)
            elif name[0] == "q":
                used = name[1] in dests
            else:
                used = bool(started)
            if used:
                names.append(name)
        states = [shape((group, HD, rows), f32), shape((group, 8, rows), f32)]
        if len(ready) == len(active):
            states = []
        outs = pl.pallas_call(
            functools.partial(
                attend_kernel,
                names=names,
                work=work,
                started=started,
                active=active,
                ready=ready,
                rows=rows,
            ),
            out_shape=[shape((HD, rows), bf16)] * len(ready) + states,
            in_specs=[VMEM] * len(names),
            out_specs=[VMEM] * (len(ready) + len(states)),
            compiler_params=PARAMS,
            cost_estimate=pl.CostEstimate(flops=cost, transcendentals=1, bytes_accessed=1),
            name="attend",
        )(*[arrays[name] for name in names])
        if states:
            arrays["mixed",], arrays["state",] = outs[len(ready) :]
        return dict(zip(ready, outs))

    for step in near:
        arrays["block", step] = swapped(packed[step], "place", step)
    arrays["block", 0], turned = lax.optimization_barrier((packed[0], turned))
    send_on([0])
    mix = {}
    held = packed[near[-1] + 1 :] if apart else []
    if apart:
        tied = lax.optimization_barrier((list(held), turned, arrays["block", 1]))
        held, turned, arrays["block", 1] = tied
    if near:
        send_on(near)
    for step, block in zip(apart, held):
        arrays["kv", step] = swapped(block, "place", step)
    mix.update(stage(0, NEAR))
    if apart:
        send_on(apart)
        for step, block in zip(apart, held[len(apart) :]):
            arrays["q", step] = swapped(block, "place", step)
    for at in range(1, len(plan)):
        done = stage(at, MORE if at == 1 and apart else FAR)
        order = [step for step in sending_order(group) if step in done]
        mix.update((step, swapped(done[step], "place", step) if step else done[0]) for step in order)

    mixes = [mix[step] for step in sending_order(group)]
    for other in range(1, head_total):
        mixes += [swapped(entry, "head", other) for entry in mixes[:group]]
    return pl.pallas_call(
        functools.partial(project_kernel, group=group, head_total=head_total),
        out_shape=shape((features, rows), bf16),
        in_specs=[VMEM] * (1 + head_total * group),
        out_specs=VMEM,
        scratch_shapes=[pltpu.VMEM((head_total, group, HD, rows), bf16)],
        compiler_params=PARAMS,
        name="project",
    )(turned, *mixes)


def solution(mesh):
    nodes, heads = mesh.devices.shape
    place = HEADS // heads
    split = Mesh(
        mesh.devices.reshape(nodes // place, place, heads), ("group", "place", "head")
    )
    node = ("group", "place")
    return jax.shard_map(
        on_device,
        mesh=split,
        in_specs=(
            P(node, "head"),
            P(node, "head"),
            P(node, "head"),
            P(None, node, None),
            P(None, node),
            P(),
        ),
        out_specs=P("head", node),
        check_vma=False,
    )
```

```python
import functools

import jax
import jax.numpy as jnp
from jax import lax
from jax.experimental import pallas as pl
from jax.experimental.pallas import tpu as pltpu
from jax.sharding import Mesh, PartitionSpec as P

HEADS = 8
HD = 128
TILE = 128
SLOTS = 2
STEPS = 4
LOG2E = 1.4426950408889634
SCALE = LOG2E * HD ** (-0.5)
MASKED = -1e30
EXTRA = 16
OWN = 10**9
NEAR = 1000000000
MORE = 1
FAR = 1000000000
VMEM = pl.BlockSpec(memory_space=pltpu.VMEM)
HBM = pl.BlockSpec(memory_space=pltpu.HBM)
PARAMS = pltpu.CompilerParams(vmem_limit_bytes=48 * 1024 * 1024)


def use_rows(index_ref, count_ref, tiles):
    row = lax.broadcasted_iota(jnp.int32, (EXTRA, HD), 0)
    uses = jnp.zeros((EXTRA, HD), jnp.float32)
    for turn in range(STEPS):
        for dest in range(tiles):
            for source in range(tiles):
                times = jnp.float32(0)
                for slot in range(SLOTS):
                    used = (slot < count_ref[dest, turn]) & (index_ref[dest, slot, turn] == source)
                    times += jnp.where(used, 1.0, 0.0)
                uses = jnp.where(row == (turn * tiles + dest) * tiles + source, times, uses)
    return uses


def hops(step):
    return step.bit_count()


def query_places(refs, group, rows):
    apart = iter(refs[group:])
    return [
        next(apart) if hops(step) > 1 else refs[step].at[pl.ds(2 * rows, rows + EXTRA)]
        for step in range(group)
    ]


def pack_kernel(query_ref, key_ref, value_ref, index_ref, count_ref, *refs):
    out_refs, (values, index, count, sem) = refs[:-4], refs[-4:]
    group = query_ref.shape[1] // HD
    block_refs, query_refs = out_refs[:group], query_places(out_refs, group, query_ref.shape[0])
    rows = query_ref.shape[0]
    tiles = rows // TILE
    place = lax.axis_index("place")
    value_copy = pltpu.make_async_copy(value_ref, values, sem.at[0])
    value_copy.start()
    table_copies = [
        pltpu.make_async_copy(index_ref, index, sem.at[1]),
        pltpu.make_async_copy(count_ref, count, sem.at[2]),
    ]
    for copy in table_copies:
        copy.start()
    copies = []
    for step in range(group):
        cols = pl.ds(pl.multiple_of(jnp.bitwise_xor(place, step) * HD, HD), HD)
        copies += [
            pltpu.make_async_copy(
                key_ref.at[:, cols], block_refs[step].at[pl.ds(0, rows)], sem.at[3 + 2 * step]
            ),
            pltpu.make_async_copy(
                query_ref.at[:, cols], query_refs[step].at[pl.ds(0, rows)], sem.at[4 + 2 * step]
            ),
        ]
    for copy in copies:
        copy.start()
    for copy in table_copies:
        copy.wait()
    uses = use_rows(index, count, tiles).astype(jnp.bfloat16)
    value_copy.wait()
    for step in range(group):
        cols = pl.ds(pl.multiple_of(jnp.bitwise_xor(place, step) * HD, HD), HD)
        out = block_refs[step]
        query_refs[step][rows:] = uses
        for at in range(0, rows, TILE):
            out[rows + at : rows + at + TILE] = values[at : at + TILE, cols].T
    for copy in copies:
        copy.wait()


def pair_scores(keys, query_ref, turn):
    rows = keys.shape[0]
    tiles = rows // TILE
    raw = (
        lax.dot_general(
            keys, query_ref[:rows], (((1,), (1,)), ((), ())), preferred_element_type=jnp.float32
        )
        * SCALE
    )
    uses = query_ref[rows:].astype(jnp.float32)
    parts = []
    for source in range(tiles):
        bias = []
        for tile in range(tiles):
            at = (turn * tiles + tile) * tiles + source
            times = uses[at : at + 1]
            bias.append(jnp.where(times > 0.5, times - 1.0, MASKED))
        parts.append(
            raw[source * TILE : (source + 1) * TILE] + jnp.concatenate(bias, axis=1)
        )
    return raw, jnp.concatenate(parts, axis=0)


def own_scores(raw):
    eye = lax.broadcasted_iota(jnp.int32, (TILE, TILE), 0) == lax.broadcasted_iota(
        jnp.int32, (TILE, TILE), 1
    )
    return jnp.concatenate(
        [
            jnp.sum(
                jnp.where(eye, raw[at : at + TILE, at : at + TILE], 0.0), axis=0, keepdims=True
            )
            for at in range(0, raw.shape[0], TILE)
        ],
        axis=1,
    )


def turned_values(source_ref, rows):
    return jnp.concatenate(
        [source_ref[rows + at : rows + at + TILE] for at in range(0, rows, TILE)], axis=1
    )


def attend(query_ref, sources, before):
    rows = query_ref.shape[0] - EXTRA
    scores = []
    for source_ref, turn in sources:
        raw, score = pair_scores(source_ref[:rows], query_ref, turn)
        scores.append(score)
        if turn == 0:
            own = own_scores(raw)
    top = own if before is None else before[0]
    for score in scores:
        top = jnp.maximum(top, jnp.max(score, axis=0, keepdims=True))
    if before is None:
        total = jnp.exp2(own - top)
        own_ref = next(source_ref for source_ref, turn in sources if turn == 0)
        mixed = total * turned_values(own_ref, rows).astype(jnp.float32)
    else:
        factor = jnp.exp2(before[0] - top)
        total, mixed = before[1] * factor, before[2] * factor
    for score, (source_ref, _) in zip(scores, sources):
        weights = jnp.exp2(score - top)
        total = total + jnp.sum(weights, axis=0, keepdims=True)
        mixed = mixed + jnp.dot(
            turned_values(source_ref, rows),
            weights.astype(jnp.bfloat16),
            preferred_element_type=jnp.float32,
        )
    return top, total, mixed


def sources_of(group, place, step):
    result = []
    for turn in range(STEPS):
        slab = (place ^ step) - turn
        result.append(((-(slab // group), place ^ (slab % group)), turn))
    return result


def stage_plan(group):
    steps = list(range(group))
    near = [step for step in steps if hops(step) < 2]
    stages = [(near, lambda offset, step: hops(step) < 2 and (offset == 0 or step == 0))]
    if len(near) < group:
        stages.append((steps, lambda offset, step: offset == 0 or step == 0))
    stages.append((steps, lambda offset, step: offset == 0 or hops(step) < 2))
    if len(near) < group:
        stages.append((steps, lambda offset, step: True))
    plan, taken = [], set()
    for dests, there in stages:
        work = []
        for place in range(group):
            table = {}
            for dest in dests:
                todo = [
                    (key, turn)
                    for key, turn in sources_of(group, place, dest)
                    if there(*key) and (place, dest, turn) not in taken
                ]
                taken.update((place, dest, turn) for _, turn in todo)
                if todo:
                    table[dest] = todo
            work.append(table)
        plan.append(work)
    return plan


def attend_kernel(*refs, names, work, started, active, ready, rows):
    named = dict(zip(names, refs))
    outs = refs[len(names) :]
    out_refs, state_refs = dict(zip(ready, outs)), outs[len(ready) :]
    group = len(work)

    def block(offset, step):
        for name in named:
            if name[0] == "halo" and name[1] == offset and step in name[2]:
                return named[name].at[name[2].index(step)]
        return named.get(("block", step), named.get(("kv", step)))

    def queries(step):
        if ("q", step) in named:
            return named["q", step]
        return named["block", step].at[pl.ds(2 * rows, rows + EXTRA)]

    here = lax.axis_index("place")
    for place in range(group):

        @pl.when(here == place)
        def _(place=place):
            for step in active:
                before = None
                if step in started:
                    mixed_ref, state_ref = named["mixed",], named["state",]
                    before = (state_ref[step, 0:1], state_ref[step, 1:2], mixed_ref[step])
                todo = [(block(*key), turn) for key, turn in work[place].get(step, [])]
                top, total, mixed = attend(queries(step), todo, before) if todo else before
                if step in ready:
                    out_refs[step][...] = (mixed / total).astype(out_refs[step].dtype)
                else:
                    state_refs[0][step] = mixed
                    state_refs[1][step, 0:1] = top
                    state_refs[1][step, 1:2] = total


def turn_kernel(block_ref, weight_ref, turned_ref, held, sem, *, head_total):
    me = lax.axis_index("head")
    depth = weight_ref.shape[0] // head_total
    features = weight_ref.shape[1] // head_total
    copies = []
    for other in range(head_total):
        start = pl.multiple_of(jnp.bitwise_xor(me, other) * depth, depth)
        cols = pl.ds(pl.multiple_of(me * features, features), features)
        copies.append(
            pltpu.make_async_copy(
                weight_ref.at[pl.ds(start, depth), cols], held.at[other], sem.at[other]
            )
        )
        copies[-1].start()
    for other in range(head_total):
        copies[other].wait()
        turned_ref[other] = held[other].T


def sending_order(group):
    return sorted(range(group), key=lambda step: (step > 0, -hops(step), step))


def project_kernel(turned_ref, *refs, group, head_total):
    mix_refs, out_ref, mix = refs[:-2], refs[-2], refs[-1]
    place = lax.axis_index("place")
    for other in range(head_total):
        for at, step in enumerate(sending_order(group)):
            mix[other, jnp.bitwise_xor(place, step)] = mix_refs[other * group + at][...]
    result = None
    for other in range(head_total):
        part = jnp.dot(
            turned_ref[other],
            mix[other].reshape(turned_ref.shape[2], out_ref.shape[1]),
            preferred_element_type=jnp.float32,
        )
        result = part if result is None else result + part
    out_ref[...] = result.astype(out_ref.dtype)


def swapped(value, axis, step):
    count = lax.axis_size(axis)
    return lax.ppermute(value, axis, [(source, source ^ step) for source in range(count)])


def on_device(node_queries, node_keys, node_values, tile_index, tile_count, out_weight):
    rows, width = node_queries.shape
    group = width // HD
    groups = lax.axis_size("group")
    head_total = lax.axis_size("head")
    depth, feature_total = out_weight.shape
    features = feature_total // head_total
    bf16, f32 = jnp.bfloat16, jnp.float32
    shape = jax.ShapeDtypeStruct

    apart = [step for step in range(group) if hops(step) > 1]
    whole_block, query_block = shape((3 * rows + EXTRA, HD), bf16), shape((rows + EXTRA, HD), bf16)
    packed = pl.pallas_call(
        pack_kernel,
        out_shape=[
            shape((2 * rows, HD), bf16) if step in apart else whole_block for step in range(group)
        ]
        + [query_block] * len(apart),
        in_specs=[HBM] * 5,
        out_specs=[VMEM] * (group + len(apart)),
        scratch_shapes=[
            pltpu.VMEM((rows, width), bf16),
            pltpu.SMEM((rows // TILE, SLOTS, STEPS), jnp.int32),
            pltpu.SMEM((rows // TILE, STEPS), jnp.int32),
            pltpu.SemaphoreType.DMA((3 + 2 * group,)),
        ],
        compiler_params=PARAMS,
        name="pack",
    )(
        *[
            pltpu.with_memory_space_constraint(array, pltpu.HBM)
            for array in (
                node_queries,
                node_keys,
                node_values,
                jnp.transpose(tile_index, (1, 2, 0)),
                jnp.transpose(tile_count, (1, 0)),
            )
        ],
    )

    turned = pl.pallas_call(
        functools.partial(turn_kernel, head_total=head_total),
        out_shape=shape((head_total, features, depth // head_total), bf16),
        in_specs=[HBM, HBM],
        out_specs=VMEM,
        scratch_shapes=[
            pltpu.VMEM((head_total, depth // head_total, features), bf16),
            pltpu.SemaphoreType.DMA((head_total,)),
        ],
        compiler_params=PARAMS,
        cost_estimate=pl.CostEstimate(flops=OWN, transcendentals=1, bytes_accessed=1),
        name="turn",
    )(packed[0], pltpu.with_memory_space_constraint(out_weight, pltpu.HBM))

    offsets = list(range(1, -(-(STEPS - 1) // group) + 1))
    plan = stage_plan(group)
    finish = [
        max(at for at, work in enumerate(plan) for table in work if step in table)
        for step in range(group)
    ]
    arrays = {("block", 0): packed[0]}
    near = [step for step in range(1, group) if hops(step) < 2]
    first = ("halo", 1, (0,))

    def send_on(steps):
        blocks = [arrays.get(("block", step), arrays.get(("kv", step))) for step in steps]
        message = jnp.stack([block[: 2 * rows] for block in blocks])
        for offset in offsets:
            pairs = [(source, (source + offset) % groups) for source in range(groups)]
            arrays["halo", offset, tuple(steps)] = lax.ppermute(message, "group", pairs)

    def stage(at, cost):
        work = plan[at]
        started = [
            step
            for step in range(group)
            if finish[step] >= at and any(step in table for work in plan[:at] for table in work)
        ]
        active = sorted(set(started) | {step for table in work for step in table})
        ready = [step for step in active if finish[step] == at]
        keys = {key for table in work for todo in table.values() for key, _ in todo}
        dests = {step for table in work for step in table}
        names = []
        for name in arrays:
            if name[0] == "halo":
                used = any((name[1], step) in keys for step in name[2])
            elif name[0] in ("block", "kv"):
                used = (0, name[1]) in keys or (name[0] == "block" and name[1] in dests)
            elif name[0] == "q":
                used = name[1] in dests
            else:
                used = bool(started)
            if used:
                names.append(name)
        states = [shape((group, HD, rows), f32), shape((group, 8, rows), f32)]
        if len(ready) == len(active):
            states = []
        outs = pl.pallas_call(
            functools.partial(
                attend_kernel,
                names=names,
                work=work,
                started=started,
                active=active,
                ready=ready,
                rows=rows,
            ),
            out_shape=[shape((HD, rows), bf16)] * len(ready) + states,
            in_specs=[VMEM] * len(names),
            out_specs=[VMEM] * (len(ready) + len(states)),
            compiler_params=PARAMS,
            cost_estimate=pl.CostEstimate(flops=cost, transcendentals=1, bytes_accessed=1),
            name="attend",
        )(*[arrays[name] for name in names])
        if states:
            arrays["mixed",], arrays["state",] = outs[len(ready) :]
        return dict(zip(ready, outs))

    for step in near:
        arrays["block", step] = swapped(packed[step], "place", step)
    send_on([0])
    mix = {}
    held = packed[near[-1] + 1 :] if apart else []
    if apart:
        tied = lax.optimization_barrier((list(held), turned, [arrays["block", step] for step in near]))
        held, turned, blocks = tied
        arrays.update((("block", step), block) for step, block in zip(near, blocks))
    for step in near:
        send_on([step])
    for step, block in zip(apart, held):
        arrays["kv", step] = swapped(block, "place", step)
    mix.update(stage(0, NEAR))
    if apart:
        send_on(apart)
        for step, block in zip(apart, held[len(apart) :]):
            block, arrays[first] = lax.optimization_barrier((block, arrays[first]))
            arrays["q", step] = swapped(block, "place", step)
    for at in range(1, len(plan)):
        done = stage(at, MORE if at == 1 and apart else FAR)
        order = [step for step in sending_order(group) if step in done]
        mix.update((step, swapped(done[step], "place", step) if step else done[0]) for step in order)

    mixes = [mix[step] for step in sending_order(group)]
    for other in range(1, head_total):
        mixes += [swapped(entry, "head", other) for entry in mixes[:group]]
    return pl.pallas_call(
        functools.partial(project_kernel, group=group, head_total=head_total),
        out_shape=shape((features, rows), bf16),
        in_specs=[VMEM] * (1 + head_total * group),
        out_specs=VMEM,
        scratch_shapes=[pltpu.VMEM((head_total, group, HD, rows), bf16)],
        compiler_params=PARAMS,
        name="project",
    )(turned, *mixes)


def solution(mesh):
    nodes, heads = mesh.devices.shape
    place = HEADS // heads
    split = Mesh(
        mesh.devices.reshape(nodes // place, place, heads), ("group", "place", "head")
    )
    node = ("group", "place")
    return jax.shard_map(
        on_device,
        mesh=split,
        in_specs=(
            P(node, "head"),
            P(node, "head"),
            P(node, "head"),
            P(None, node, None),
            P(None, node),
            P(),
        ),
        out_specs=P("head", node),
        check_vma=False,
    )
```

```python
import functools

import jax
import jax.numpy as jnp
from jax import lax
from jax.experimental import pallas as pl
from jax.experimental.pallas import tpu as pltpu
from jax.sharding import Mesh, PartitionSpec as P

HEADS = 8
HD = 128
TILE = 128
SLOTS = 2
STEPS = 4
LOG2E = 1.4426950408889634
SCALE = LOG2E * HD ** (-0.5)
MASKED = -1e30
EXTRA = 16
OWN = 10**9
NEAR = 1000000000
MORE = 1000000000
FAR = 1000000000
VMEM = pl.BlockSpec(memory_space=pltpu.VMEM)
HBM = pl.BlockSpec(memory_space=pltpu.HBM)
PARAMS = pltpu.CompilerParams(vmem_limit_bytes=48 * 1024 * 1024)


def use_rows(index_ref, count_ref, tiles):
    row = lax.broadcasted_iota(jnp.int32, (EXTRA, HD), 0)
    uses = jnp.zeros((EXTRA, HD), jnp.float32)
    for turn in range(STEPS):
        for dest in range(tiles):
            for source in range(tiles):
                times = jnp.float32(0)
                for slot in range(SLOTS):
                    used = (slot < count_ref[dest, turn]) & (index_ref[dest, slot, turn] == source)
                    times += jnp.where(used, 1.0, 0.0)
                uses = jnp.where(row == (turn * tiles + dest) * tiles + source, times, uses)
    return uses


def hops(step):
    return step.bit_count()


def query_places(refs, group, rows):
    apart = iter(refs[group:])
    return [
        next(apart) if hops(step) > 1 else refs[step].at[pl.ds(2 * rows, rows + EXTRA)]
        for step in range(group)
    ]


def pack_kernel(query_ref, key_ref, value_ref, index_ref, count_ref, *refs):
    out_refs, (values, index, count, sem) = refs[:-4], refs[-4:]
    group = query_ref.shape[1] // HD
    block_refs, query_refs = out_refs[:group], query_places(out_refs, group, query_ref.shape[0])
    rows = query_ref.shape[0]
    tiles = rows // TILE
    place = lax.axis_index("place")
    value_copy = pltpu.make_async_copy(value_ref, values, sem.at[0])
    value_copy.start()
    table_copies = [
        pltpu.make_async_copy(index_ref, index, sem.at[1]),
        pltpu.make_async_copy(count_ref, count, sem.at[2]),
    ]
    for copy in table_copies:
        copy.start()
    copies = []
    for step in range(group):
        cols = pl.ds(pl.multiple_of(jnp.bitwise_xor(place, step) * HD, HD), HD)
        copies += [
            pltpu.make_async_copy(
                key_ref.at[:, cols], block_refs[step].at[pl.ds(0, rows)], sem.at[3 + 2 * step]
            ),
            pltpu.make_async_copy(
                query_ref.at[:, cols], query_refs[step].at[pl.ds(0, rows)], sem.at[4 + 2 * step]
            ),
        ]
    for copy in copies:
        copy.start()
    for copy in table_copies:
        copy.wait()
    uses = use_rows(index, count, tiles).astype(jnp.bfloat16)
    value_copy.wait()
    for step in range(group):
        cols = pl.ds(pl.multiple_of(jnp.bitwise_xor(place, step) * HD, HD), HD)
        out = block_refs[step]
        query_refs[step][rows:] = uses
        for at in range(0, rows, TILE):
            out[rows + at : rows + at + TILE] = values[at : at + TILE, cols].T
    for copy in copies:
        copy.wait()


def pair_scores(keys, query_ref, turn):
    rows = keys.shape[0]
    tiles = rows // TILE
    raw = (
        lax.dot_general(
            keys, query_ref[:rows], (((1,), (1,)), ((), ())), preferred_element_type=jnp.float32
        )
        * SCALE
    )
    uses = query_ref[rows:].astype(jnp.float32)
    parts = []
    for source in range(tiles):
        bias = []
        for tile in range(tiles):
            at = (turn * tiles + tile) * tiles + source
            times = uses[at : at + 1]
            bias.append(jnp.where(times > 0.5, times - 1.0, MASKED))
        parts.append(
            raw[source * TILE : (source + 1) * TILE] + jnp.concatenate(bias, axis=1)
        )
    return raw, jnp.concatenate(parts, axis=0)


def own_scores(raw):
    eye = lax.broadcasted_iota(jnp.int32, (TILE, TILE), 0) == lax.broadcasted_iota(
        jnp.int32, (TILE, TILE), 1
    )
    return jnp.concatenate(
        [
            jnp.sum(
                jnp.where(eye, raw[at : at + TILE, at : at + TILE], 0.0), axis=0, keepdims=True
            )
            for at in range(0, raw.shape[0], TILE)
        ],
        axis=1,
    )


def turned_values(source_ref, rows):
    return jnp.concatenate(
        [source_ref[rows + at : rows + at + TILE] for at in range(0, rows, TILE)], axis=1
    )


def attend(query_ref, sources, before):
    rows = query_ref.shape[0] - EXTRA
    scores = []
    for source_ref, turn in sources:
        raw, score = pair_scores(source_ref[:rows], query_ref, turn)
        scores.append(score)
        if turn == 0:
            own = own_scores(raw)
    top = own if before is None else before[0]
    for score in scores:
        top = jnp.maximum(top, jnp.max(score, axis=0, keepdims=True))
    if before is None:
        total = jnp.exp2(own - top)
        own_ref = next(source_ref for source_ref, turn in sources if turn == 0)
        mixed = total * turned_values(own_ref, rows).astype(jnp.float32)
    else:
        factor = jnp.exp2(before[0] - top)
        total, mixed = before[1] * factor, before[2] * factor
    for score, (source_ref, _) in zip(scores, sources):
        weights = jnp.exp2(score - top)
        total = total + jnp.sum(weights, axis=0, keepdims=True)
        mixed = mixed + jnp.dot(
            turned_values(source_ref, rows),
            weights.astype(jnp.bfloat16),
            preferred_element_type=jnp.float32,
        )
    return top, total, mixed


def sources_of(group, place, step):
    result = []
    for turn in range(STEPS):
        slab = (place ^ step) - turn
        result.append(((-(slab // group), place ^ (slab % group)), turn))
    return result


def stage_plan(group):
    steps = list(range(group))
    near = [step for step in steps if hops(step) < 2]
    stages = [(near, lambda offset, step: hops(step) < 2 and (offset == 0 or step == 0))]
    if len(near) < group:
        stages.append((steps, lambda offset, step: offset == 0 or step == 0))
    stages.append((steps, lambda offset, step: offset == 0 or hops(step) < 2))
    if len(near) < group:
        stages.append((steps, lambda offset, step: True))
    plan, taken = [], set()
    for dests, there in stages:
        work = []
        for place in range(group):
            table = {}
            for dest in dests:
                todo = [
                    (key, turn)
                    for key, turn in sources_of(group, place, dest)
                    if there(*key) and (place, dest, turn) not in taken
                ]
                taken.update((place, dest, turn) for _, turn in todo)
                if todo:
                    table[dest] = todo
            work.append(table)
        plan.append(work)
    return plan


def attend_kernel(*refs, names, work, started, active, ready, rows):
    named = dict(zip(names, refs))
    outs = refs[len(names) :]
    out_refs, state_refs = dict(zip(ready, outs)), outs[len(ready) :]
    group = len(work)

    def block(offset, step):
        for name in named:
            if name[0] == "halo" and name[1] == offset and step in name[2]:
                return named[name].at[name[2].index(step)]
        return named.get(("block", step), named.get(("kv", step)))

    def queries(step):
        if ("q", step) in named:
            return named["q", step]
        return named["block", step].at[pl.ds(2 * rows, rows + EXTRA)]

    here = lax.axis_index("place")
    for place in range(group):

        @pl.when(here == place)
        def _(place=place):
            for step in active:
                before = None
                if step in started:
                    mixed_ref, state_ref = named["mixed",], named["state",]
                    before = (state_ref[step, 0:1], state_ref[step, 1:2], mixed_ref[step])
                todo = [(block(*key), turn) for key, turn in work[place].get(step, [])]
                top, total, mixed = attend(queries(step), todo, before) if todo else before
                if step in ready:
                    out_refs[step][...] = (mixed / total).astype(out_refs[step].dtype)
                else:
                    state_refs[0][step] = mixed
                    state_refs[1][step, 0:1] = top
                    state_refs[1][step, 1:2] = total


def turn_kernel(block_ref, weight_ref, turned_ref, held, sem, *, head_total):
    me = lax.axis_index("head")
    depth = weight_ref.shape[0] // head_total
    features = weight_ref.shape[1] // head_total
    copies = []
    for other in range(head_total):
        start = pl.multiple_of(jnp.bitwise_xor(me, other) * depth, depth)
        cols = pl.ds(pl.multiple_of(me * features, features), features)
        copies.append(
            pltpu.make_async_copy(
                weight_ref.at[pl.ds(start, depth), cols], held.at[other], sem.at[other]
            )
        )
        copies[-1].start()
    for other in range(head_total):
        copies[other].wait()
        turned_ref[other] = held[other].T


def sending_order(group):
    return sorted(range(group), key=lambda step: (step > 0, -hops(step), step))


def project_kernel(turned_ref, *refs, group, head_total):
    mix_refs, out_ref, mix = refs[:-2], refs[-2], refs[-1]
    place = lax.axis_index("place")
    for other in range(head_total):
        for at, step in enumerate(sending_order(group)):
            mix[other, jnp.bitwise_xor(place, step)] = mix_refs[other * group + at][...]
    result = None
    for other in range(head_total):
        part = jnp.dot(
            turned_ref[other],
            mix[other].reshape(turned_ref.shape[2], out_ref.shape[1]),
            preferred_element_type=jnp.float32,
        )
        result = part if result is None else result + part
    out_ref[...] = result.astype(out_ref.dtype)


def swapped(value, axis, step):
    count = lax.axis_size(axis)
    return lax.ppermute(value, axis, [(source, source ^ step) for source in range(count)])


def on_device(node_queries, node_keys, node_values, tile_index, tile_count, out_weight):
    rows, width = node_queries.shape
    group = width // HD
    groups = lax.axis_size("group")
    head_total = lax.axis_size("head")
    depth, feature_total = out_weight.shape
    features = feature_total // head_total
    bf16, f32 = jnp.bfloat16, jnp.float32
    shape = jax.ShapeDtypeStruct

    apart = [step for step in range(group) if hops(step) > 1]
    whole_block, query_block = shape((3 * rows + EXTRA, HD), bf16), shape((rows + EXTRA, HD), bf16)
    packed = pl.pallas_call(
        pack_kernel,
        out_shape=[
            shape((2 * rows, HD), bf16) if step in apart else whole_block for step in range(group)
        ]
        + [query_block] * len(apart),
        in_specs=[HBM] * 5,
        out_specs=[VMEM] * (group + len(apart)),
        scratch_shapes=[
            pltpu.VMEM((rows, width), bf16),
            pltpu.SMEM((rows // TILE, SLOTS, STEPS), jnp.int32),
            pltpu.SMEM((rows // TILE, STEPS), jnp.int32),
            pltpu.SemaphoreType.DMA((3 + 2 * group,)),
        ],
        compiler_params=PARAMS,
        name="pack",
    )(
        *[
            pltpu.with_memory_space_constraint(array, pltpu.HBM)
            for array in (
                node_queries,
                node_keys,
                node_values,
                jnp.transpose(tile_index, (1, 2, 0)),
                jnp.transpose(tile_count, (1, 0)),
            )
        ],
    )

    turned = pl.pallas_call(
        functools.partial(turn_kernel, head_total=head_total),
        out_shape=shape((head_total, features, depth // head_total), bf16),
        in_specs=[HBM, HBM],
        out_specs=VMEM,
        scratch_shapes=[
            pltpu.VMEM((head_total, depth // head_total, features), bf16),
            pltpu.SemaphoreType.DMA((head_total,)),
        ],
        compiler_params=PARAMS,
        cost_estimate=pl.CostEstimate(flops=OWN, transcendentals=1, bytes_accessed=1),
        name="turn",
    )(packed[0], pltpu.with_memory_space_constraint(out_weight, pltpu.HBM))

    offsets = list(range(1, -(-(STEPS - 1) // group) + 1))
    plan = stage_plan(group)
    finish = [
        max(at for at, work in enumerate(plan) for table in work if step in table)
        for step in range(group)
    ]
    arrays = {("block", 0): packed[0]}
    near = [step for step in range(1, group) if hops(step) < 2]
    first = ("halo", 1, (0,))

    def send_on(steps):
        blocks = [arrays.get(("block", step), arrays.get(("kv", step))) for step in steps]
        message = jnp.stack([block[: 2 * rows] for block in blocks])
        if apart and steps == near[-1:]:
            early = [first]
            message, got = lax.optimization_barrier((message, [arrays[name] for name in early]))
            arrays.update(zip(early, got))
        for offset in offsets:
            pairs = [(source, (source + offset) % groups) for source in range(groups)]
            arrays["halo", offset, tuple(steps)] = lax.ppermute(message, "group", pairs)

    def stage(at, cost):
        work = plan[at]
        started = [
            step
            for step in range(group)
            if finish[step] >= at and any(step in table for work in plan[:at] for table in work)
        ]
        active = sorted(set(started) | {step for table in work for step in table})
        ready = [step for step in active if finish[step] == at]
        keys = {key for table in work for todo in table.values() for key, _ in todo}
        dests = {step for table in work for step in table}
        names = []
        for name in arrays:
            if name[0] == "halo":
                used = any((name[1], step) in keys for step in name[2])
            elif name[0] in ("block", "kv"):
                used = (0, name[1]) in keys or (name[0] == "block" and name[1] in dests)
            elif name[0] == "q":
                used = name[1] in dests
            else:
                used = bool(started)
            if used:
                names.append(name)
        states = [shape((group, HD, rows), f32), shape((group, 8, rows), f32)]
        if len(ready) == len(active):
            states = []
        outs = pl.pallas_call(
            functools.partial(
                attend_kernel,
                names=names,
                work=work,
                started=started,
                active=active,
                ready=ready,
                rows=rows,
            ),
            out_shape=[shape((HD, rows), bf16)] * len(ready) + states,
            in_specs=[VMEM] * len(names),
            out_specs=[VMEM] * (len(ready) + len(states)),
            compiler_params=PARAMS,
            cost_estimate=pl.CostEstimate(flops=cost, transcendentals=1, bytes_accessed=1),
            name="attend",
        )(*[arrays[name] for name in names])
        if states:
            arrays["mixed",], arrays["state",] = outs[len(ready) :]
        return dict(zip(ready, outs))

    for step in near:
        arrays["block", step] = swapped(packed[step], "place", step)
    send_on([0])
    mix = {}
    if apart:
        blocks, queries = packed[:group], packed[group:]
        tied = lax.optimization_barrier((queries, turned))
        queries, turned = tied
        arrays["q", apart[0]] = swapped(queries[0], "place", apart[0])
        tied = lax.optimization_barrier((packed[apart[0]], turned, arrays["block", 1]))
        block, turned, arrays["block", 1] = tied
        arrays["kv", apart[0]] = swapped(block, "place", apart[0])
    for step in near:
        send_on([step])
    mix.update(stage(0, NEAR))
    if apart:
        send_on(apart)
    for at in range(1, len(plan)):
        done = stage(at, MORE if at == 1 and apart else FAR)
        order = [step for step in sending_order(group) if step in done]
        mix.update((step, swapped(done[step], "place", step) if step else done[0]) for step in order)

    mixes = [mix[step] for step in sending_order(group)]
    for other in range(1, head_total):
        mixes += [swapped(entry, "head", other) for entry in mixes[:group]]
    return pl.pallas_call(
        functools.partial(project_kernel, group=group, head_total=head_total),
        out_shape=shape((features, rows), bf16),
        in_specs=[VMEM] * (1 + head_total * group),
        out_specs=VMEM,
        scratch_shapes=[pltpu.VMEM((head_total, group, HD, rows), bf16)],
        compiler_params=PARAMS,
        name="project",
    )(turned, *mixes)


def solution(mesh):
    nodes, heads = mesh.devices.shape
    place = HEADS // heads
    split = Mesh(
        mesh.devices.reshape(nodes // place, place, heads), ("group", "place", "head")
    )
    node = ("group", "place")
    return jax.shard_map(
        on_device,
        mesh=split,
        in_specs=(
            P(node, "head"),
            P(node, "head"),
            P(node, "head"),
            P(None, node, None),
            P(None, node),
            P(),
        ),
        out_specs=P("head", node),
        check_vma=False,
    )
```

```python
import functools

import jax
import jax.numpy as jnp
from jax import lax
from jax.experimental import pallas as pl
from jax.experimental.pallas import tpu as pltpu
from jax.sharding import Mesh, PartitionSpec as P

HEADS = 8
HD = 128
TILE = 128
SLOTS = 2
STEPS = 4
LOG2E = 1.4426950408889634
SCALE = LOG2E * HD ** (-0.5)
MASKED = -1e30
EXTRA = 16
OWN = 10**9
NEAR = 1000000000
MORE = 1000000000
FAR = 1000000000
VMEM = pl.BlockSpec(memory_space=pltpu.VMEM)
HBM = pl.BlockSpec(memory_space=pltpu.HBM)
PARAMS = pltpu.CompilerParams(vmem_limit_bytes=48 * 1024 * 1024)


def use_rows(index_ref, count_ref, tiles):
    row = lax.broadcasted_iota(jnp.int32, (EXTRA, HD), 0)
    uses = jnp.zeros((EXTRA, HD), jnp.float32)
    for turn in range(STEPS):
        for dest in range(tiles):
            for source in range(tiles):
                times = jnp.float32(0)
                for slot in range(SLOTS):
                    used = (slot < count_ref[dest, turn]) & (index_ref[dest, slot, turn] == source)
                    times += jnp.where(used, 1.0, 0.0)
                uses = jnp.where(row == (turn * tiles + dest) * tiles + source, times, uses)
    return uses


def hops(step):
    return step.bit_count()


def query_places(refs, group, rows):
    apart = iter(refs[group:])
    return [
        next(apart) if hops(step) > 1 else refs[step].at[pl.ds(2 * rows, rows + EXTRA)]
        for step in range(group)
    ]


def pack_kernel(query_ref, key_ref, value_ref, index_ref, count_ref, *refs):
    out_refs, (values, index, count, sem) = refs[:-4], refs[-4:]
    group = query_ref.shape[1] // HD
    block_refs, query_refs = out_refs[:group], query_places(out_refs, group, query_ref.shape[0])
    rows = query_ref.shape[0]
    tiles = rows // TILE
    place = lax.axis_index("place")
    value_copy = pltpu.make_async_copy(value_ref, values, sem.at[0])
    value_copy.start()
    table_copies = [
        pltpu.make_async_copy(index_ref, index, sem.at[1]),
        pltpu.make_async_copy(count_ref, count, sem.at[2]),
    ]
    for copy in table_copies:
        copy.start()
    copies = []
    for step in range(group):
        cols = pl.ds(pl.multiple_of(jnp.bitwise_xor(place, step) * HD, HD), HD)
        copies += [
            pltpu.make_async_copy(
                key_ref.at[:, cols], block_refs[step].at[pl.ds(0, rows)], sem.at[3 + 2 * step]
            ),
            pltpu.make_async_copy(
                query_ref.at[:, cols], query_refs[step].at[pl.ds(0, rows)], sem.at[4 + 2 * step]
            ),
        ]
    for copy in copies:
        copy.start()
    for copy in table_copies:
        copy.wait()
    uses = use_rows(index, count, tiles).astype(jnp.bfloat16)
    value_copy.wait()
    for step in range(group):
        cols = pl.ds(pl.multiple_of(jnp.bitwise_xor(place, step) * HD, HD), HD)
        out = block_refs[step]
        query_refs[step][rows:] = uses
        for at in range(0, rows, TILE):
            out[rows + at : rows + at + TILE] = values[at : at + TILE, cols].T
    for copy in copies:
        copy.wait()


def pair_scores(keys, query_ref, turn):
    rows = keys.shape[0]
    tiles = rows // TILE
    raw = (
        lax.dot_general(
            keys, query_ref[:rows], (((1,), (1,)), ((), ())), preferred_element_type=jnp.float32
        )
        * SCALE
    )
    uses = query_ref[rows:].astype(jnp.float32)
    parts = []
    for source in range(tiles):
        bias = []
        for tile in range(tiles):
            at = (turn * tiles + tile) * tiles + source
            times = uses[at : at + 1]
            bias.append(jnp.where(times > 0.5, times - 1.0, MASKED))
        parts.append(
            raw[source * TILE : (source + 1) * TILE] + jnp.concatenate(bias, axis=1)
        )
    return raw, jnp.concatenate(parts, axis=0)


def own_scores(raw):
    eye = lax.broadcasted_iota(jnp.int32, (TILE, TILE), 0) == lax.broadcasted_iota(
        jnp.int32, (TILE, TILE), 1
    )
    return jnp.concatenate(
        [
            jnp.sum(
                jnp.where(eye, raw[at : at + TILE, at : at + TILE], 0.0), axis=0, keepdims=True
            )
            for at in range(0, raw.shape[0], TILE)
        ],
        axis=1,
    )


def turned_values(source_ref, rows):
    return jnp.concatenate(
        [source_ref[rows + at : rows + at + TILE] for at in range(0, rows, TILE)], axis=1
    )


def attend(query_ref, sources, before):
    rows = query_ref.shape[0] - EXTRA
    scores = []
    for source_ref, turn in sources:
        raw, score = pair_scores(source_ref[:rows], query_ref, turn)
        scores.append(score)
        if turn == 0:
            own = own_scores(raw)
    top = own if before is None else before[0]
    for score in scores:
        top = jnp.maximum(top, jnp.max(score, axis=0, keepdims=True))
    if before is None:
        total = jnp.exp2(own - top)
        own_ref = next(source_ref for source_ref, turn in sources if turn == 0)
        mixed = total * turned_values(own_ref, rows).astype(jnp.float32)
    else:
        factor = jnp.exp2(before[0] - top)
        total, mixed = before[1] * factor, before[2] * factor
    for score, (source_ref, _) in zip(scores, sources):
        weights = jnp.exp2(score - top)
        total = total + jnp.sum(weights, axis=0, keepdims=True)
        mixed = mixed + jnp.dot(
            turned_values(source_ref, rows),
            weights.astype(jnp.bfloat16),
            preferred_element_type=jnp.float32,
        )
    return top, total, mixed


def sources_of(group, place, step):
    result = []
    for turn in range(STEPS):
        slab = (place ^ step) - turn
        result.append(((-(slab // group), place ^ (slab % group)), turn))
    return result


def stage_plan(group):
    steps = list(range(group))
    near = [step for step in steps if hops(step) < 2]
    stages = [(near, lambda offset, step: hops(step) < 2 and (offset == 0 or step == 0))]
    if len(near) < group:
        stages.append((steps, lambda offset, step: offset == 0 or step == 0))
    stages.append((steps, lambda offset, step: offset == 0 or hops(step) < 2))
    if len(near) < group:
        stages.append((steps, lambda offset, step: True))
    plan, taken = [], set()
    for dests, there in stages:
        work = []
        for place in range(group):
            table = {}
            for dest in dests:
                todo = [
                    (key, turn)
                    for key, turn in sources_of(group, place, dest)
                    if there(*key) and (place, dest, turn) not in taken
                ]
                taken.update((place, dest, turn) for _, turn in todo)
                if todo:
                    table[dest] = todo
            work.append(table)
        plan.append(work)
    return plan


def attend_kernel(*refs, names, work, started, active, ready, rows):
    named = dict(zip(names, refs))
    outs = refs[len(names) :]
    out_refs, state_refs = dict(zip(ready, outs)), outs[len(ready) :]
    group = len(work)

    def block(offset, step):
        for name in named:
            if name[0] == "halo" and name[1] == offset and step in name[2]:
                return named[name].at[name[2].index(step)]
        return named.get(("block", step), named.get(("kv", step)))

    def queries(step):
        if ("q", step) in named:
            return named["q", step]
        return named["block", step].at[pl.ds(2 * rows, rows + EXTRA)]

    here = lax.axis_index("place")
    for place in range(group):

        @pl.when(here == place)
        def _(place=place):
            for step in active:
                before = None
                if step in started:
                    mixed_ref, state_ref = named["mixed",], named["state",]
                    before = (state_ref[step, 0:1], state_ref[step, 1:2], mixed_ref[step])
                todo = [(block(*key), turn) for key, turn in work[place].get(step, [])]
                top, total, mixed = attend(queries(step), todo, before) if todo else before
                if step in ready:
                    out_refs[step][...] = (mixed / total).astype(out_refs[step].dtype)
                else:
                    state_refs[0][step] = mixed
                    state_refs[1][step, 0:1] = top
                    state_refs[1][step, 1:2] = total


def turn_kernel(block_ref, weight_ref, turned_ref, held, sem, *, head_total):
    me = lax.axis_index("head")
    depth = weight_ref.shape[0] // head_total
    features = weight_ref.shape[1] // head_total
    copies = []
    for other in range(head_total):
        start = pl.multiple_of(jnp.bitwise_xor(me, other) * depth, depth)
        cols = pl.ds(pl.multiple_of(me * features, features), features)
        copies.append(
            pltpu.make_async_copy(
                weight_ref.at[pl.ds(start, depth), cols], held.at[other], sem.at[other]
            )
        )
        copies[-1].start()
    for other in range(head_total):
        copies[other].wait()
        turned_ref[other] = held[other].T


def sending_order(group):
    return sorted(range(group), key=lambda step: (step > 0, -hops(step), step))


def project_kernel(turned_ref, *refs, group, head_total):
    mix_refs, out_ref, mix = refs[:-2], refs[-2], refs[-1]
    place = lax.axis_index("place")
    for other in range(head_total):
        for at, step in enumerate(sending_order(group)):
            mix[other, jnp.bitwise_xor(place, step)] = mix_refs[other * group + at][...]
    result = None
    for other in range(head_total):
        part = jnp.dot(
            turned_ref[other],
            mix[other].reshape(turned_ref.shape[2], out_ref.shape[1]),
            preferred_element_type=jnp.float32,
        )
        result = part if result is None else result + part
    out_ref[...] = result.astype(out_ref.dtype)


def swapped(value, axis, step):
    count = lax.axis_size(axis)
    return lax.ppermute(value, axis, [(source, source ^ step) for source in range(count)])


def on_device(node_queries, node_keys, node_values, tile_index, tile_count, out_weight):
    rows, width = node_queries.shape
    group = width // HD
    groups = lax.axis_size("group")
    head_total = lax.axis_size("head")
    depth, feature_total = out_weight.shape
    features = feature_total // head_total
    bf16, f32 = jnp.bfloat16, jnp.float32
    shape = jax.ShapeDtypeStruct

    apart = [step for step in range(group) if hops(step) > 1]
    whole_block, query_block = shape((3 * rows + EXTRA, HD), bf16), shape((rows + EXTRA, HD), bf16)
    packed = pl.pallas_call(
        pack_kernel,
        out_shape=[
            shape((2 * rows, HD), bf16) if step in apart else whole_block for step in range(group)
        ]
        + [query_block] * len(apart),
        in_specs=[HBM] * 5,
        out_specs=[VMEM] * (group + len(apart)),
        scratch_shapes=[
            pltpu.VMEM((rows, width), bf16),
            pltpu.SMEM((rows // TILE, SLOTS, STEPS), jnp.int32),
            pltpu.SMEM((rows // TILE, STEPS), jnp.int32),
            pltpu.SemaphoreType.DMA((3 + 2 * group,)),
        ],
        compiler_params=PARAMS,
        name="pack",
    )(
        *[
            pltpu.with_memory_space_constraint(array, pltpu.HBM)
            for array in (
                node_queries,
                node_keys,
                node_values,
                jnp.transpose(tile_index, (1, 2, 0)),
                jnp.transpose(tile_count, (1, 0)),
            )
        ],
    )

    turned = pl.pallas_call(
        functools.partial(turn_kernel, head_total=head_total),
        out_shape=shape((head_total, features, depth // head_total), bf16),
        in_specs=[HBM, HBM],
        out_specs=VMEM,
        scratch_shapes=[
            pltpu.VMEM((head_total, depth // head_total, features), bf16),
            pltpu.SemaphoreType.DMA((head_total,)),
        ],
        compiler_params=PARAMS,
        cost_estimate=pl.CostEstimate(flops=OWN, transcendentals=1, bytes_accessed=1),
        name="turn",
    )(packed[0], pltpu.with_memory_space_constraint(out_weight, pltpu.HBM))

    offsets = list(range(1, -(-(STEPS - 1) // group) + 1))
    plan = stage_plan(group)
    finish = [
        max(at for at, work in enumerate(plan) for table in work if step in table)
        for step in range(group)
    ]
    arrays = {("block", 0): packed[0]}
    near = [step for step in range(1, group) if hops(step) < 2]
    first = ("halo", 1, (0,))

    def send_on(steps):
        blocks = [arrays.get(("block", step), arrays.get(("kv", step))) for step in steps]
        message = jnp.stack([block[: 2 * rows] for block in blocks])
        if apart and steps == apart:
            early = [first]
            message, got = lax.optimization_barrier((message, [arrays[name] for name in early]))
            arrays.update(zip(early, got))
        for offset in offsets:
            pairs = [(source, (source + offset) % groups) for source in range(groups)]
            arrays["halo", offset, tuple(steps)] = lax.ppermute(message, "group", pairs)

    def stage(at, cost):
        work = plan[at]
        started = [
            step
            for step in range(group)
            if finish[step] >= at and any(step in table for work in plan[:at] for table in work)
        ]
        active = sorted(set(started) | {step for table in work for step in table})
        ready = [step for step in active if finish[step] == at]
        keys = {key for table in work for todo in table.values() for key, _ in todo}
        dests = {step for table in work for step in table}
        names = []
        for name in arrays:
            if name[0] == "halo":
                used = any((name[1], step) in keys for step in name[2])
            elif name[0] in ("block", "kv"):
                used = (0, name[1]) in keys or (name[0] == "block" and name[1] in dests)
            elif name[0] == "q":
                used = name[1] in dests
            else:
                used = bool(started)
            if used:
                names.append(name)
        states = [shape((group, HD, rows), f32), shape((group, 8, rows), f32)]
        if len(ready) == len(active):
            states = []
        outs = pl.pallas_call(
            functools.partial(
                attend_kernel,
                names=names,
                work=work,
                started=started,
                active=active,
                ready=ready,
                rows=rows,
            ),
            out_shape=[shape((HD, rows), bf16)] * len(ready) + states,
            in_specs=[VMEM] * len(names),
            out_specs=[VMEM] * (len(ready) + len(states)),
            compiler_params=PARAMS,
            cost_estimate=pl.CostEstimate(flops=cost, transcendentals=1, bytes_accessed=1),
            name="attend",
        )(*[arrays[name] for name in names])
        if states:
            arrays["mixed",], arrays["state",] = outs[len(ready) :]
        return dict(zip(ready, outs))

    for step in near:
        arrays["block", step] = swapped(packed[step], "place", step)
    send_on([0])
    mix = {}
    if apart:
        queries, turned = lax.optimization_barrier((packed[group:], turned))
        arrays["q", apart[0]] = swapped(queries[0], "place", apart[0])
        tied = lax.optimization_barrier(
            (packed[apart[0]], turned, [arrays["block", step] for step in near])
        )
        far_block, turned, blocks = tied
        arrays.update((("block", step), block) for step, block in zip(near, blocks))
        arrays["kv", apart[0]] = swapped(far_block, "place", apart[0])
    for step in near:
        send_on([step])
    mix.update(stage(0, NEAR))
    if apart:
        send_on(apart)
    for at in range(1, len(plan)):
        done = stage(at, MORE if at == 1 and apart else FAR)
        order = [step for step in sending_order(group) if step in done]
        mix.update((step, swapped(done[step], "place", step) if step else done[0]) for step in order)

    mixes = [mix[step] for step in sending_order(group)]
    for other in range(1, head_total):
        mixes += [swapped(entry, "head", other) for entry in mixes[:group]]
    return pl.pallas_call(
        functools.partial(project_kernel, group=group, head_total=head_total),
        out_shape=shape((features, rows), bf16),
        in_specs=[VMEM] * (1 + head_total * group),
        out_specs=VMEM,
        scratch_shapes=[pltpu.VMEM((head_total, group, HD, rows), bf16)],
        compiler_params=PARAMS,
        name="project",
    )(turned, *mixes)


def solution(mesh):
    nodes, heads = mesh.devices.shape
    place = HEADS // heads
    split = Mesh(
        mesh.devices.reshape(nodes // place, place, heads), ("group", "place", "head")
    )
    node = ("group", "place")
    return jax.shard_map(
        on_device,
        mesh=split,
        in_specs=(
            P(node, "head"),
            P(node, "head"),
            P(node, "head"),
            P(None, node, None),
            P(None, node),
            P(),
        ),
        out_specs=P("head", node),
        check_vma=False,
    )
```

```python
import functools

import jax
import jax.numpy as jnp
from jax import lax
from jax.experimental import pallas as pl
from jax.experimental.pallas import tpu as pltpu
from jax.sharding import Mesh, PartitionSpec as P

HEADS = 8
HD = 128
TILE = 128
SLOTS = 2
STEPS = 4
LOG2E = 1.4426950408889634
SCALE = LOG2E * HD ** (-0.5)
MASKED = -1e30
EXTRA = 16
OWN = 10**9
NEAR = 1000000000
FAR = 1000000000
VMEM = pl.BlockSpec(memory_space=pltpu.VMEM)
HBM = pl.BlockSpec(memory_space=pltpu.HBM)
PARAMS = pltpu.CompilerParams(vmem_limit_bytes=48 * 1024 * 1024)


def use_rows(index_ref, count_ref, tiles):
    row = lax.broadcasted_iota(jnp.int32, (EXTRA, HD), 0)
    uses = jnp.zeros((EXTRA, HD), jnp.float32)
    for turn in range(STEPS):
        for dest in range(tiles):
            for source in range(tiles):
                times = jnp.float32(0)
                for slot in range(SLOTS):
                    used = (slot < count_ref[dest, turn]) & (index_ref[dest, slot, turn] == source)
                    times += jnp.where(used, 1.0, 0.0)
                uses = jnp.where(row == (turn * tiles + dest) * tiles + source, times, uses)
    return uses


def hops(step):
    return step.bit_count()


def pack_kernel(query_ref, key_ref, value_ref, index_ref, count_ref, *refs):
    out_refs, (values, index, count, sem) = refs[:-4], refs[-4:]
    group = query_ref.shape[1] // HD
    rows = query_ref.shape[0]
    tiles = rows // TILE
    place = lax.axis_index("place")
    value_copy = pltpu.make_async_copy(value_ref, values, sem.at[0])
    value_copy.start()
    table_copies = [
        pltpu.make_async_copy(index_ref, index, sem.at[1]),
        pltpu.make_async_copy(count_ref, count, sem.at[2]),
    ]
    for copy in table_copies:
        copy.start()
    copies = []
    for step in range(group):
        cols = pl.ds(pl.multiple_of(jnp.bitwise_xor(place, step) * HD, HD), HD)
        copies += [
            pltpu.make_async_copy(
                key_ref.at[:, cols], out_refs[step].at[pl.ds(0, rows)], sem.at[3 + 2 * step]
            ),
            pltpu.make_async_copy(
                query_ref.at[:, cols],
                out_refs[step].at[pl.ds(2 * rows, rows)],
                sem.at[4 + 2 * step],
            ),
        ]
    for copy in copies:
        copy.start()
    for copy in table_copies:
        copy.wait()
    uses = use_rows(index, count, tiles).astype(jnp.bfloat16)
    value_copy.wait()
    for step in range(group):
        cols = pl.ds(pl.multiple_of(jnp.bitwise_xor(place, step) * HD, HD), HD)
        out = out_refs[step]
        out[3 * rows :] = uses
        for at in range(0, rows, TILE):
            out[rows + at : rows + at + TILE] = values[at : at + TILE, cols].T
    for copy in copies:
        copy.wait()


def pair_scores(keys, query_ref, turn):
    rows = keys.shape[0]
    tiles = rows // TILE
    raw = (
        lax.dot_general(
            keys, query_ref[:rows], (((1,), (1,)), ((), ())), preferred_element_type=jnp.float32
        )
        * SCALE
    )
    uses = query_ref[rows:].astype(jnp.float32)
    parts = []
    for source in range(tiles):
        bias = []
        for tile in range(tiles):
            at = (turn * tiles + tile) * tiles + source
            times = uses[at : at + 1]
            bias.append(jnp.where(times > 0.5, times - 1.0, MASKED))
        parts.append(
            raw[source * TILE : (source + 1) * TILE] + jnp.concatenate(bias, axis=1)
        )
    return raw, jnp.concatenate(parts, axis=0)


def own_scores(raw):
    eye = lax.broadcasted_iota(jnp.int32, (TILE, TILE), 0) == lax.broadcasted_iota(
        jnp.int32, (TILE, TILE), 1
    )
    return jnp.concatenate(
        [
            jnp.sum(
                jnp.where(eye, raw[at : at + TILE, at : at + TILE], 0.0), axis=0, keepdims=True
            )
            for at in range(0, raw.shape[0], TILE)
        ],
        axis=1,
    )


def turned_values(source_ref, rows):
    return jnp.concatenate(
        [source_ref[rows + at : rows + at + TILE] for at in range(0, rows, TILE)], axis=1
    )


def attend(query_ref, sources, before):
    rows = query_ref.shape[0] - EXTRA
    scores = []
    for source_ref, turn in sources:
        raw, score = pair_scores(source_ref[:rows], query_ref, turn)
        scores.append(score)
        if turn == 0:
            own = own_scores(raw)
    top = own if before is None else before[0]
    for score in scores:
        top = jnp.maximum(top, jnp.max(score, axis=0, keepdims=True))
    if before is None:
        total = jnp.exp2(own - top)
        own_ref = next(source_ref for source_ref, turn in sources if turn == 0)
        mixed = total * turned_values(own_ref, rows).astype(jnp.float32)
    else:
        factor = jnp.exp2(before[0] - top)
        total, mixed = before[1] * factor, before[2] * factor
    for score, (source_ref, _) in zip(scores, sources):
        weights = jnp.exp2(score - top)
        total = total + jnp.sum(weights, axis=0, keepdims=True)
        mixed = mixed + jnp.dot(
            turned_values(source_ref, rows),
            weights.astype(jnp.bfloat16),
            preferred_element_type=jnp.float32,
        )
    return top, total, mixed


def sources_of(group, place, step):
    result = []
    for turn in range(STEPS):
        slab = (place ^ step) - turn
        result.append(((-(slab // group), place ^ (slab % group)), turn))
    return result


def stage_plan(group):
    steps = list(range(group))
    near = [step for step in steps if hops(step) < 2]
    stages = [(near, lambda offset, step: hops(step) < 2 and (offset == 0 or step == 0))]
    stages.append((steps, lambda offset, step: offset == 0 or hops(step) < 2))
    if len(near) < group:
        stages.append((steps, lambda offset, step: True))
    plan, taken = [], set()
    for dests, there in stages:
        work = []
        for place in range(group):
            table = {}
            for dest in dests:
                todo = [
                    (key, turn)
                    for key, turn in sources_of(group, place, dest)
                    if there(*key) and (place, dest, turn) not in taken
                ]
                taken.update((place, dest, turn) for _, turn in todo)
                if todo:
                    table[dest] = todo
            work.append(table)
        plan.append(work)
    return plan


def attend_kernel(*refs, names, work, started, active, ready, rows):
    named = dict(zip(names, refs))
    outs = refs[len(names) :]
    out_refs, state_refs = dict(zip(ready, outs)), outs[len(ready) :]
    group = len(work)

    def block(offset, step):
        for name in named:
            if name[0] == "halo" and name[1] == offset and step in name[2]:
                return named[name].at[name[2].index(step)]
        return named["block", step]

    def queries(step):
        return named["block", step].at[pl.ds(2 * rows, rows + EXTRA)]

    here = lax.axis_index("place")
    for place in range(group):

        @pl.when(here == place)
        def _(place=place):
            for step in active:
                before = None
                if step in started:
                    mixed_ref, state_ref = named["mixed",], named["state",]
                    before = (state_ref[step, 0:1], state_ref[step, 1:2], mixed_ref[step])
                todo = [(block(*key), turn) for key, turn in work[place].get(step, [])]
                top, total, mixed = attend(queries(step), todo, before) if todo else before
                if step in ready:
                    out_refs[step][...] = (mixed / total).astype(out_refs[step].dtype)
                else:
                    state_refs[0][step] = mixed
                    state_refs[1][step, 0:1] = top
                    state_refs[1][step, 1:2] = total


def turn_kernel(block_ref, weight_ref, turned_ref, held, sem, *, head_total):
    me = lax.axis_index("head")
    depth = weight_ref.shape[0] // head_total
    features = weight_ref.shape[1] // head_total
    copies = []
    for other in range(head_total):
        start = pl.multiple_of(jnp.bitwise_xor(me, other) * depth, depth)
        cols = pl.ds(pl.multiple_of(me * features, features), features)
        copies.append(
            pltpu.make_async_copy(
                weight_ref.at[pl.ds(start, depth), cols], held.at[other], sem.at[other]
            )
        )
        copies[-1].start()
    for other in range(head_total):
        copies[other].wait()
        turned_ref[other] = held[other].T


def sending_order(group):
    return sorted(range(group), key=lambda step: (step > 0, -hops(step), step))


def project_kernel(turned_ref, *refs, group, others):
    mix_refs, refs = refs[: len(others) * group], refs[len(others) * group :]
    so_far, (out_ref, mix) = refs[:-2], refs[-2:]
    place = lax.axis_index("place")
    for number in range(len(others)):
        for at, step in enumerate(sending_order(group)):
            mix[number, jnp.bitwise_xor(place, step)] = mix_refs[number * group + at][...]
    result = so_far[0][...] if so_far else None
    for number, other in enumerate(others):
        part = jnp.dot(
            turned_ref[other],
            mix[number].reshape(turned_ref.shape[2], out_ref.shape[1]),
            preferred_element_type=jnp.float32,
        )
        result = part if result is None else result + part
    out_ref[...] = result.astype(out_ref.dtype)


def swapped(value, axis, step):
    count = lax.axis_size(axis)
    return lax.ppermute(value, axis, [(source, source ^ step) for source in range(count)])


def on_device(node_queries, node_keys, node_values, tile_index, tile_count, out_weight):
    rows, width = node_queries.shape
    group = width // HD
    groups = lax.axis_size("group")
    head_total = lax.axis_size("head")
    depth, feature_total = out_weight.shape
    features = feature_total // head_total
    bf16, f32 = jnp.bfloat16, jnp.float32
    shape = jax.ShapeDtypeStruct

    apart = [step for step in range(group) if hops(step) > 1]
    packed = pl.pallas_call(
        pack_kernel,
        out_shape=[shape((3 * rows + EXTRA, HD), bf16)] * group,
        in_specs=[HBM] * 5,
        out_specs=[VMEM] * group,
        scratch_shapes=[
            pltpu.VMEM((rows, width), bf16),
            pltpu.SMEM((rows // TILE, SLOTS, STEPS), jnp.int32),
            pltpu.SMEM((rows // TILE, STEPS), jnp.int32),
            pltpu.SemaphoreType.DMA((3 + 2 * group,)),
        ],
        compiler_params=PARAMS,
        name="pack",
    )(
        *[
            pltpu.with_memory_space_constraint(array, pltpu.HBM)
            for array in (
                node_queries,
                node_keys,
                node_values,
                jnp.transpose(tile_index, (1, 2, 0)),
                jnp.transpose(tile_count, (1, 0)),
            )
        ],
    )

    turned = pl.pallas_call(
        functools.partial(turn_kernel, head_total=head_total),
        out_shape=shape((head_total, features, depth // head_total), bf16),
        in_specs=[HBM, HBM],
        out_specs=VMEM,
        scratch_shapes=[
            pltpu.VMEM((head_total, depth // head_total, features), bf16),
            pltpu.SemaphoreType.DMA((head_total,)),
        ],
        compiler_params=PARAMS,
        cost_estimate=pl.CostEstimate(flops=OWN, transcendentals=1, bytes_accessed=1),
        name="turn",
    )(packed[0], pltpu.with_memory_space_constraint(out_weight, pltpu.HBM))

    offsets = list(range(1, -(-(STEPS - 1) // group) + 1))
    plan = stage_plan(group)
    finish = [
        max(at for at, work in enumerate(plan) for table in work if step in table)
        for step in range(group)
    ]
    arrays = {("block", 0): packed[0]}
    near = [step for step in range(1, group) if hops(step) < 2]
    first = ("halo", 1, (0,))

    def send_on(steps):
        message = jnp.stack([arrays["block", step][: 2 * rows] for step in steps])
        for offset in offsets:
            pairs = [(source, (source + offset) % groups) for source in range(groups)]
            arrays["halo", offset, tuple(steps)] = lax.ppermute(message, "group", pairs)

    def stage(at, cost):
        work = plan[at]
        started = [
            step
            for step in range(group)
            if finish[step] >= at and any(step in table for work in plan[:at] for table in work)
        ]
        active = sorted(set(started) | {step for table in work for step in table})
        ready = [step for step in active if finish[step] == at]
        keys = {key for table in work for todo in table.values() for key, _ in todo}
        dests = {step for table in work for step in table}
        names = []
        for name in arrays:
            if name[0] == "halo":
                used = any((name[1], step) in keys for step in name[2])
            elif name[0] == "block":
                used = (0, name[1]) in keys or name[1] in dests
            else:
                used = bool(started)
            if used:
                names.append(name)
        states = [shape((group, HD, rows), f32), shape((group, 8, rows), f32)]
        if len(ready) == len(active):
            states = []
        outs = pl.pallas_call(
            functools.partial(
                attend_kernel,
                names=names,
                work=work,
                started=started,
                active=active,
                ready=ready,
                rows=rows,
            ),
            out_shape=[shape((HD, rows), bf16)] * len(ready) + states,
            in_specs=[VMEM] * len(names),
            out_specs=[VMEM] * (len(ready) + len(states)),
            compiler_params=PARAMS,
            cost_estimate=pl.CostEstimate(flops=cost, transcendentals=1, bytes_accessed=1),
            name="attend",
        )(*[arrays[name] for name in names])
        if states:
            arrays["mixed",], arrays["state",] = outs[len(ready) :]
        return dict(zip(ready, outs))

    for step in near:
        arrays["block", step] = swapped(packed[step], "place", step)
    send_on([0])
    mix = {}
    far_blocks = packed[len(near) + 1 :]
    if apart:
        tied = lax.optimization_barrier(
            (far_blocks, turned, [arrays["block", step] for step in near])
        )
        far_blocks, turned, blocks = tied
        arrays.update((("block", step), block) for step, block in zip(near, blocks))
    for step, block in zip(apart, far_blocks):
        arrays["block", step] = swapped(block, "place", step)
    for step in near:
        send_on([step])
    mix.update(stage(0, NEAR))
    if apart:
        tied = lax.optimization_barrier((arrays["block", apart[0]], arrays["state",]))
        arrays["block", apart[0]], arrays["state",] = tied
        send_on(apart)
    for at in range(1, len(plan)):
        done = stage(at, FAR)
        order = [step for step in sending_order(group) if step in done]
        mix.update((step, swapped(done[step], "place", step) if step else done[0]) for step in order)

    mixes = [mix[step] for step in sending_order(group)]
    output = []
    for others, kind in (([0], f32), (list(range(1, head_total)), bf16)):
        parts = mixes
        if output:
            parts = [swapped(entry, "head", other) for other in others for entry in mixes]
        output = [
            pl.pallas_call(
                functools.partial(project_kernel, group=group, others=others),
                out_shape=shape((features, rows), kind),
                in_specs=[VMEM] * (1 + len(parts) + len(output)),
                out_specs=VMEM,
                scratch_shapes=[pltpu.VMEM((len(others), group, HD, rows), bf16)],
                compiler_params=PARAMS,
                name="project",
            )(turned, *parts, *output)
        ]
    return output[0]


def solution(mesh):
    nodes, heads = mesh.devices.shape
    place = HEADS // heads
    split = Mesh(
        mesh.devices.reshape(nodes // place, place, heads), ("group", "place", "head")
    )
    node = ("group", "place")
    return jax.shard_map(
        on_device,
        mesh=split,
        in_specs=(
            P(node, "head"),
            P(node, "head"),
            P(node, "head"),
            P(None, node, None),
            P(None, node),
            P(),
        ),
        out_specs=P("head", node),
        check_vma=False,
    )
```

```python
import functools

import jax
import jax.numpy as jnp
from jax import lax
from jax.experimental import pallas as pl
from jax.experimental.pallas import tpu as pltpu
from jax.sharding import Mesh, PartitionSpec as P

HEADS = 8
HD = 128
TILE = 128
SLOTS = 2
STEPS = 4
LOG2E = 1.4426950408889634
SCALE = LOG2E * HD ** (-0.5)
MASKED = -1e30
EXTRA = 16
OWN = 1000000000
NEAR = 1000000000
FAR = 1000000000
VMEM = pl.BlockSpec(memory_space=pltpu.VMEM)
HBM = pl.BlockSpec(memory_space=pltpu.HBM)
PARAMS = pltpu.CompilerParams(vmem_limit_bytes=48 * 1024 * 1024)


def use_rows(index_ref, count_ref, tiles):
    row = lax.broadcasted_iota(jnp.int32, (EXTRA, HD), 0)
    uses = jnp.zeros((EXTRA, HD), jnp.float32)
    for turn in range(STEPS):
        for dest in range(tiles):
            for source in range(tiles):
                times = jnp.float32(0)
                for slot in range(SLOTS):
                    used = (slot < count_ref[dest, turn]) & (index_ref[dest, slot, turn] == source)
                    times += jnp.where(used, 1.0, 0.0)
                uses = jnp.where(row == (turn * tiles + dest) * tiles + source, times, uses)
    return uses


def hops(step):
    return step.bit_count()


def pack_kernel(query_ref, key_ref, value_ref, index_ref, count_ref, *refs):
    out_refs, (values, index, count, sem) = refs[:-4], refs[-4:]
    group = query_ref.shape[1] // HD
    rows = query_ref.shape[0]
    tiles = rows // TILE
    place = lax.axis_index("place")
    value_copy = pltpu.make_async_copy(value_ref, values, sem.at[0])
    value_copy.start()
    table_copies = [
        pltpu.make_async_copy(index_ref, index, sem.at[1]),
        pltpu.make_async_copy(count_ref, count, sem.at[2]),
    ]
    for copy in table_copies:
        copy.start()
    copies = []
    for step in range(group):
        cols = pl.ds(pl.multiple_of(jnp.bitwise_xor(place, step) * HD, HD), HD)
        copies += [
            pltpu.make_async_copy(
                key_ref.at[:, cols], out_refs[step].at[pl.ds(0, rows)], sem.at[3 + 2 * step]
            ),
            pltpu.make_async_copy(
                query_ref.at[:, cols],
                out_refs[step].at[pl.ds(2 * rows, rows)],
                sem.at[4 + 2 * step],
            ),
        ]
    for copy in copies:
        copy.start()
    for copy in table_copies:
        copy.wait()
    uses = use_rows(index, count, tiles).astype(jnp.bfloat16)
    value_copy.wait()
    for step in range(group):
        cols = pl.ds(pl.multiple_of(jnp.bitwise_xor(place, step) * HD, HD), HD)
        out = out_refs[step]
        out[3 * rows :] = uses
        for at in range(0, rows, TILE):
            out[rows + at : rows + at + TILE] = values[at : at + TILE, cols].T
    for copy in copies:
        copy.wait()


def pair_scores(keys, query_ref, turn):
    rows = keys.shape[0]
    tiles = rows // TILE
    raw = (
        lax.dot_general(
            keys, query_ref[:rows], (((1,), (1,)), ((), ())), preferred_element_type=jnp.float32
        )
        * SCALE
    )
    uses = query_ref[rows:].astype(jnp.float32)
    parts = []
    for source in range(tiles):
        bias = []
        for tile in range(tiles):
            at = (turn * tiles + tile) * tiles + source
            times = uses[at : at + 1]
            bias.append(jnp.where(times > 0.5, times - 1.0, MASKED))
        parts.append(
            raw[source * TILE : (source + 1) * TILE] + jnp.concatenate(bias, axis=1)
        )
    return raw, jnp.concatenate(parts, axis=0)


def own_scores(raw):
    eye = lax.broadcasted_iota(jnp.int32, (TILE, TILE), 0) == lax.broadcasted_iota(
        jnp.int32, (TILE, TILE), 1
    )
    return jnp.concatenate(
        [
            jnp.sum(
                jnp.where(eye, raw[at : at + TILE, at : at + TILE], 0.0), axis=0, keepdims=True
            )
            for at in range(0, raw.shape[0], TILE)
        ],
        axis=1,
    )


def turned_values(source_ref, rows):
    return jnp.concatenate(
        [source_ref[rows + at : rows + at + TILE] for at in range(0, rows, TILE)], axis=1
    )


def attend(query_ref, sources, before):
    rows = query_ref.shape[0] - EXTRA
    scores = []
    for source_ref, turn in sources:
        raw, score = pair_scores(source_ref[:rows], query_ref, turn)
        scores.append(score)
        if turn == 0:
            own = own_scores(raw)
    top = own if before is None else before[0]
    for score in scores:
        top = jnp.maximum(top, jnp.max(score, axis=0, keepdims=True))
    if before is None:
        total = jnp.exp2(own - top)
        own_ref = next(source_ref for source_ref, turn in sources if turn == 0)
        mixed = total * turned_values(own_ref, rows).astype(jnp.float32)
    else:
        factor = jnp.exp2(before[0] - top)
        total, mixed = before[1] * factor, before[2] * factor
    for score, (source_ref, _) in zip(scores, sources):
        weights = jnp.exp2(score - top)
        total = total + jnp.sum(weights, axis=0, keepdims=True)
        mixed = mixed + jnp.dot(
            turned_values(source_ref, rows),
            weights.astype(jnp.bfloat16),
            preferred_element_type=jnp.float32,
        )
    return top, total, mixed


def sources_of(group, place, step):
    result = []
    for turn in range(STEPS):
        slab = (place ^ step) - turn
        result.append(((-(slab // group), place ^ (slab % group)), turn))
    return result


def stage_plan(group):
    steps = list(range(group))
    near = [step for step in steps if hops(step) < 2]
    stages = [(near, lambda offset, step: hops(step) < 2 and (offset == 0 or step == 0))]
    stages.append((steps, lambda offset, step: offset == 0 or hops(step) < 2))
    if len(near) < group:
        stages.append((steps, lambda offset, step: True))
    plan, taken = [], set()
    for dests, there in stages:
        work = []
        for place in range(group):
            table = {}
            for dest in dests:
                todo = [
                    (key, turn)
                    for key, turn in sources_of(group, place, dest)
                    if there(*key) and (place, dest, turn) not in taken
                ]
                taken.update((place, dest, turn) for _, turn in todo)
                if todo:
                    table[dest] = todo
            work.append(table)
        plan.append(work)
    return plan


def attend_kernel(*refs, names, work, started, active, ready, rows):
    named = dict(zip(names, refs))
    outs = refs[len(names) :]
    out_refs, state_refs = dict(zip(ready, outs)), outs[len(ready) :]
    group = len(work)

    def block(offset, step):
        for name in named:
            if name[0] == "halo" and name[1] == offset and step in name[2]:
                return named[name].at[name[2].index(step)]
        return named["block", step]

    def queries(step):
        return named["block", step].at[pl.ds(2 * rows, rows + EXTRA)]

    here = lax.axis_index("place")
    for place in range(group):

        @pl.when(here == place)
        def _(place=place):
            for step in active:
                before = None
                if step in started:
                    mixed_ref, state_ref = named["mixed",], named["state",]
                    before = (state_ref[step, 0:1], state_ref[step, 1:2], mixed_ref[step])
                todo = [(block(*key), turn) for key, turn in work[place].get(step, [])]
                top, total, mixed = attend(queries(step), todo, before) if todo else before
                if step in ready:
                    out_refs[step][...] = (mixed / total).astype(out_refs[step].dtype)
                else:
                    state_refs[0][step] = mixed
                    state_refs[1][step, 0:1] = top
                    state_refs[1][step, 1:2] = total


def turn_kernel(block_ref, weight_ref, turned_ref, held, sem, *, head_total):
    me = lax.axis_index("head")
    depth = weight_ref.shape[0] // head_total
    features = weight_ref.shape[1] // head_total
    copies = []
    for other in range(head_total):
        start = pl.multiple_of(jnp.bitwise_xor(me, other) * depth, depth)
        cols = pl.ds(pl.multiple_of(me * features, features), features)
        copies.append(
            pltpu.make_async_copy(
                weight_ref.at[pl.ds(start, depth), cols], held.at[other], sem.at[other]
            )
        )
        copies[-1].start()
    for other in range(head_total):
        copies[other].wait()
        turned_ref[other] = held[other].T


def sending_order(group):
    return sorted(range(group), key=lambda step: (step > 0, -hops(step), step))


def project_kernel(turned_ref, *refs, group, others):
    mix_refs, refs = refs[: len(others) * group], refs[len(others) * group :]
    so_far, (out_ref, mix) = refs[:-2], refs[-2:]
    place = lax.axis_index("place")
    for number in range(len(others)):
        for at, step in enumerate(sending_order(group)):
            mix[number, jnp.bitwise_xor(place, step)] = mix_refs[number * group + at][...]
    result = so_far[0][...] if so_far else None
    for number, other in enumerate(others):
        part = jnp.dot(
            turned_ref[other],
            mix[number].reshape(turned_ref.shape[2], out_ref.shape[1]),
            preferred_element_type=jnp.float32,
        )
        result = part if result is None else result + part
    out_ref[...] = result.astype(out_ref.dtype)


def swapped(value, axis, step):
    count = lax.axis_size(axis)
    return lax.ppermute(value, axis, [(source, source ^ step) for source in range(count)])


def on_device(node_queries, node_keys, node_values, tile_index, tile_count, out_weight):
    rows, width = node_queries.shape
    group = width // HD
    groups = lax.axis_size("group")
    head_total = lax.axis_size("head")
    depth, feature_total = out_weight.shape
    features = feature_total // head_total
    bf16, f32 = jnp.bfloat16, jnp.float32
    shape = jax.ShapeDtypeStruct

    apart = [step for step in range(group) if hops(step) > 1]
    packed = pl.pallas_call(
        pack_kernel,
        out_shape=[shape((3 * rows + EXTRA, HD), bf16)] * group,
        in_specs=[HBM] * 5,
        out_specs=[VMEM] * group,
        scratch_shapes=[
            pltpu.VMEM((rows, width), bf16),
            pltpu.SMEM((rows // TILE, SLOTS, STEPS), jnp.int32),
            pltpu.SMEM((rows // TILE, STEPS), jnp.int32),
            pltpu.SemaphoreType.DMA((3 + 2 * group,)),
        ],
        compiler_params=PARAMS,
        name="pack",
    )(
        *[
            pltpu.with_memory_space_constraint(array, pltpu.HBM)
            for array in (
                node_queries,
                node_keys,
                node_values,
                jnp.transpose(tile_index, (1, 2, 0)),
                jnp.transpose(tile_count, (1, 0)),
            )
        ],
    )

    turned = pl.pallas_call(
        functools.partial(turn_kernel, head_total=head_total),
        out_shape=shape((head_total, features, depth // head_total), bf16),
        in_specs=[HBM, HBM],
        out_specs=VMEM,
        scratch_shapes=[
            pltpu.VMEM((head_total, depth // head_total, features), bf16),
            pltpu.SemaphoreType.DMA((head_total,)),
        ],
        compiler_params=PARAMS,
        cost_estimate=pl.CostEstimate(flops=OWN, transcendentals=1, bytes_accessed=1),
        name="turn",
    )(packed[0], pltpu.with_memory_space_constraint(out_weight, pltpu.HBM))

    offsets = list(range(1, -(-(STEPS - 1) // group) + 1))
    plan = stage_plan(group)
    finish = [
        max(at for at, work in enumerate(plan) for table in work if step in table)
        for step in range(group)
    ]
    arrays = {("block", 0): packed[0]}
    near = [step for step in range(1, group) if hops(step) < 2]
    first = ("halo", 1, (0,))

    def send_on(steps):
        message = jnp.stack([arrays["block", step][: 2 * rows] for step in steps])
        for offset in offsets:
            pairs = [(source, (source + offset) % groups) for source in range(groups)]
            arrays["halo", offset, tuple(steps)] = lax.ppermute(message, "group", pairs)

    def stage(at, cost):
        work = plan[at]
        started = [
            step
            for step in range(group)
            if finish[step] >= at and any(step in table for work in plan[:at] for table in work)
        ]
        active = sorted(set(started) | {step for table in work for step in table})
        ready = [step for step in active if finish[step] == at]
        keys = {key for table in work for todo in table.values() for key, _ in todo}
        dests = {step for table in work for step in table}
        names = []
        for name in arrays:
            if name[0] == "halo":
                used = any((name[1], step) in keys for step in name[2])
            elif name[0] == "block":
                used = (0, name[1]) in keys or name[1] in dests
            else:
                used = bool(started)
            if used:
                names.append(name)
        states = [shape((group, HD, rows), f32), shape((group, 8, rows), f32)]
        if len(ready) == len(active):
            states = []
        outs = pl.pallas_call(
            functools.partial(
                attend_kernel,
                names=names,
                work=work,
                started=started,
                active=active,
                ready=ready,
                rows=rows,
            ),
            out_shape=[shape((HD, rows), bf16)] * len(ready) + states,
            in_specs=[VMEM] * len(names),
            out_specs=[VMEM] * (len(ready) + len(states)),
            compiler_params=PARAMS,
            cost_estimate=pl.CostEstimate(flops=cost, transcendentals=1, bytes_accessed=1),
            name="attend",
        )(*[arrays[name] for name in names])
        if states:
            arrays["mixed",], arrays["state",] = outs[len(ready) :]
        return dict(zip(ready, outs))

    for step in near:
        arrays["block", step] = swapped(packed[step], "place", step)
    arrays["block", 0], turned = lax.optimization_barrier((packed[0], turned))
    send_on([0])
    mix = {}
    far_blocks = packed[len(near) + 1 :]
    for step in near[:1]:
        send_on([step])
    if apart:
        watch = near
        tied = lax.optimization_barrier(
            (far_blocks, turned, [arrays["block", step] for step in watch])
        )
        far_blocks, turned, blocks = tied
        arrays.update((("block", step), block) for step, block in zip(watch, blocks))
    for step in near[1:]:
        send_on([step])
    for step, block in zip(apart, far_blocks):
        arrays["block", step] = swapped(block, "place", step)
    mix.update(stage(0, NEAR))
    if apart:
        names = [("state",)]
        tied = lax.optimization_barrier((arrays["block", apart[0]], [arrays[name] for name in names]))
        arrays["block", apart[0]], got = tied
        arrays.update(zip(names, got))
        send_on(apart)
    for at in range(1, len(plan)):
        done = stage(at, FAR)
        order = [step for step in sending_order(group) if step in done]
        mix.update((step, swapped(done[step], "place", step) if step else done[0]) for step in order)

    mixes = [mix[step] for step in sending_order(group)]
    output = []
    for others, kind in (([0], f32), (list(range(1, head_total)), bf16)):
        parts = mixes
        if output:
            parts = [swapped(entry, "head", other) for other in others for entry in mixes]
        output = [
            pl.pallas_call(
                functools.partial(project_kernel, group=group, others=others),
                out_shape=shape((features, rows), kind),
                in_specs=[VMEM] * (1 + len(parts) + len(output)),
                out_specs=VMEM,
                scratch_shapes=[pltpu.VMEM((len(others), group, HD, rows), bf16)],
                compiler_params=PARAMS,
                name="project",
            )(turned, *parts, *output)
        ]
    return output[0]


def solution(mesh):
    nodes, heads = mesh.devices.shape
    place = HEADS // heads
    split = Mesh(
        mesh.devices.reshape(nodes // place, place, heads), ("group", "place", "head")
    )
    node = ("group", "place")
    return jax.shard_map(
        on_device,
        mesh=split,
        in_specs=(
            P(node, "head"),
            P(node, "head"),
            P(node, "head"),
            P(None, node, None),
            P(None, node),
            P(),
        ),
        out_specs=P("head", node),
        check_vma=False,
    )
```

```python
import functools

import jax
import jax.numpy as jnp
from jax import lax
from jax.experimental import pallas as pl
from jax.experimental.pallas import tpu as pltpu
from jax.sharding import Mesh, PartitionSpec as P

HEADS = 8
HD = 128
TILE = 128
SLOTS = 2
STEPS = 4
LOG2E = 1.4426950408889634
SCALE = LOG2E * HD ** (-0.5)
MASKED = -1e30
EXTRA = 16
OWN = 1000000000
NEAR = 1000000000
FAR = 1000000000
VMEM = pl.BlockSpec(memory_space=pltpu.VMEM)
HBM = pl.BlockSpec(memory_space=pltpu.HBM)
PARAMS = pltpu.CompilerParams(vmem_limit_bytes=48 * 1024 * 1024)


def use_rows(index_ref, count_ref, tiles):
    row = lax.broadcasted_iota(jnp.int32, (EXTRA, HD), 0)
    uses = jnp.zeros((EXTRA, HD), jnp.float32)
    for turn in range(STEPS):
        for dest in range(tiles):
            for source in range(tiles):
                times = jnp.float32(0)
                for slot in range(SLOTS):
                    used = (slot < count_ref[dest, turn]) & (index_ref[dest, slot, turn] == source)
                    times += jnp.where(used, 1.0, 0.0)
                uses = jnp.where(row == (turn * tiles + dest) * tiles + source, times, uses)
    return uses


def hops(step):
    return step.bit_count()


def pack_kernel(query_ref, key_ref, value_ref, index_ref, count_ref, *refs):
    out_refs, (values, index, count, sem) = refs[:-4], refs[-4:]
    group = query_ref.shape[1] // HD
    rows = query_ref.shape[0]
    tiles = rows // TILE
    place = lax.axis_index("place")
    value_copy = pltpu.make_async_copy(value_ref, values, sem.at[0])
    value_copy.start()
    table_copies = [
        pltpu.make_async_copy(index_ref, index, sem.at[1]),
        pltpu.make_async_copy(count_ref, count, sem.at[2]),
    ]
    for copy in table_copies:
        copy.start()
    copies = []
    for step in range(group):
        cols = pl.ds(pl.multiple_of(jnp.bitwise_xor(place, step) * HD, HD), HD)
        copies += [
            pltpu.make_async_copy(
                key_ref.at[:, cols], out_refs[step].at[pl.ds(0, rows)], sem.at[3 + 2 * step]
            ),
            pltpu.make_async_copy(
                query_ref.at[:, cols],
                out_refs[step].at[pl.ds(2 * rows, rows)],
                sem.at[4 + 2 * step],
            ),
        ]
    for copy in copies:
        copy.start()
    for copy in table_copies:
        copy.wait()
    uses = use_rows(index, count, tiles).astype(jnp.bfloat16)
    value_copy.wait()
    for step in range(group):
        cols = pl.ds(pl.multiple_of(jnp.bitwise_xor(place, step) * HD, HD), HD)
        out = out_refs[step]
        out[3 * rows :] = uses
        for at in range(0, rows, TILE):
            out[rows + at : rows + at + TILE] = values[at : at + TILE, cols].T
    for copy in copies:
        copy.wait()


def pair_scores(keys, query_ref, turn):
    rows = keys.shape[0]
    tiles = rows // TILE
    raw = (
        lax.dot_general(
            keys, query_ref[:rows], (((1,), (1,)), ((), ())), preferred_element_type=jnp.float32
        )
        * SCALE
    )
    uses = query_ref[rows:].astype(jnp.float32)
    parts = []
    for source in range(tiles):
        bias = []
        for tile in range(tiles):
            at = (turn * tiles + tile) * tiles + source
            times = uses[at : at + 1]
            bias.append(jnp.where(times > 0.5, times - 1.0, MASKED))
        parts.append(
            raw[source * TILE : (source + 1) * TILE] + jnp.concatenate(bias, axis=1)
        )
    return raw, jnp.concatenate(parts, axis=0)


def own_scores(raw):
    eye = lax.broadcasted_iota(jnp.int32, (TILE, TILE), 0) == lax.broadcasted_iota(
        jnp.int32, (TILE, TILE), 1
    )
    return jnp.concatenate(
        [
            jnp.sum(
                jnp.where(eye, raw[at : at + TILE, at : at + TILE], 0.0), axis=0, keepdims=True
            )
            for at in range(0, raw.shape[0], TILE)
        ],
        axis=1,
    )


def turned_values(source_ref, rows):
    return jnp.concatenate(
        [source_ref[rows + at : rows + at + TILE] for at in range(0, rows, TILE)], axis=1
    )


def attend(query_ref, sources, before):
    rows = query_ref.shape[0] - EXTRA
    scores = []
    for source_ref, turn in sources:
        raw, score = pair_scores(source_ref[:rows], query_ref, turn)
        scores.append(score)
        if turn == 0:
            own = own_scores(raw)
    top = own if before is None else before[0]
    for score in scores:
        top = jnp.maximum(top, jnp.max(score, axis=0, keepdims=True))
    if before is None:
        total = jnp.exp2(own - top)
        own_ref = next(source_ref for source_ref, turn in sources if turn == 0)
        mixed = total * turned_values(own_ref, rows).astype(jnp.float32)
    else:
        factor = jnp.exp2(before[0] - top)
        total, mixed = before[1] * factor, before[2] * factor
    for score, (source_ref, _) in zip(scores, sources):
        weights = jnp.exp2(score - top)
        total = total + jnp.sum(weights, axis=0, keepdims=True)
        mixed = mixed + jnp.dot(
            turned_values(source_ref, rows),
            weights.astype(jnp.bfloat16),
            preferred_element_type=jnp.float32,
        )
    return top, total, mixed


def sources_of(group, place, step):
    result = []
    for turn in range(STEPS):
        slab = (place ^ step) - turn
        result.append(((-(slab // group), place ^ (slab % group)), turn))
    return result


def stage_plan(group):
    steps = list(range(group))
    near = [step for step in steps if hops(step) < 2]
    stages = [(near, lambda offset, step: hops(step) < 2 and (offset == 0 or step == 0))]
    stages.append((steps, lambda offset, step: True))
    plan, taken = [], set()
    for dests, there in stages:
        work = []
        for place in range(group):
            table = {}
            for dest in dests:
                todo = [
                    (key, turn)
                    for key, turn in sources_of(group, place, dest)
                    if there(*key) and (place, dest, turn) not in taken
                ]
                taken.update((place, dest, turn) for _, turn in todo)
                if todo:
                    table[dest] = todo
            work.append(table)
        plan.append(work)
    return plan


def attend_kernel(*refs, names, work, started, active, ready, rows):
    named = dict(zip(names, refs))
    outs = refs[len(names) :]
    out_refs, state_refs = dict(zip(ready, outs)), outs[len(ready) :]
    group = len(work)

    def block(offset, step):
        for name in named:
            if name[0] == "halo" and name[1] == offset and step in name[2]:
                return named[name].at[name[2].index(step)]
        return named["block", step]

    def queries(step):
        return named["block", step].at[pl.ds(2 * rows, rows + EXTRA)]

    here = lax.axis_index("place")
    for place in range(group):

        @pl.when(here == place)
        def _(place=place):
            for step in active:
                before = None
                if step in started:
                    mixed_ref, state_ref = named["mixed",], named["state",]
                    before = (state_ref[step, 0:1], state_ref[step, 1:2], mixed_ref[step])
                todo = [(block(*key), turn) for key, turn in work[place].get(step, [])]
                top, total, mixed = attend(queries(step), todo, before) if todo else before
                if step in ready:
                    out_refs[step][...] = (mixed / total).astype(out_refs[step].dtype)
                else:
                    state_refs[0][step] = mixed
                    state_refs[1][step, 0:1] = top
                    state_refs[1][step, 1:2] = total


def turn_kernel(block_ref, weight_ref, turned_ref, held, sem, *, head_total):
    me = lax.axis_index("head")
    depth = weight_ref.shape[0] // head_total
    features = weight_ref.shape[1] // head_total
    copies = []
    for other in range(head_total):
        start = pl.multiple_of(jnp.bitwise_xor(me, other) * depth, depth)
        cols = pl.ds(pl.multiple_of(me * features, features), features)
        copies.append(
            pltpu.make_async_copy(
                weight_ref.at[pl.ds(start, depth), cols], held.at[other], sem.at[other]
            )
        )
        copies[-1].start()
    for other in range(head_total):
        copies[other].wait()
        turned_ref[other] = held[other].T


def sending_order(group):
    return sorted(range(group), key=lambda step: (step > 0, -hops(step), step))


def project_kernel(turned_ref, *refs, group, others):
    mix_refs, refs = refs[: len(others) * group], refs[len(others) * group :]
    so_far, (out_ref, mix) = refs[:-2], refs[-2:]
    place = lax.axis_index("place")
    for number in range(len(others)):
        for at, step in enumerate(sending_order(group)):
            mix[number, jnp.bitwise_xor(place, step)] = mix_refs[number * group + at][...]
    result = so_far[0][...] if so_far else None
    for number, other in enumerate(others):
        part = jnp.dot(
            turned_ref[other],
            mix[number].reshape(turned_ref.shape[2], out_ref.shape[1]),
            preferred_element_type=jnp.float32,
        )
        result = part if result is None else result + part
    out_ref[...] = result.astype(out_ref.dtype)


def swapped(value, axis, step):
    count = lax.axis_size(axis)
    return lax.ppermute(value, axis, [(source, source ^ step) for source in range(count)])


def on_device(node_queries, node_keys, node_values, tile_index, tile_count, out_weight):
    rows, width = node_queries.shape
    group = width // HD
    groups = lax.axis_size("group")
    head_total = lax.axis_size("head")
    depth, feature_total = out_weight.shape
    features = feature_total // head_total
    bf16, f32 = jnp.bfloat16, jnp.float32
    shape = jax.ShapeDtypeStruct

    apart = [step for step in range(group) if hops(step) > 1]
    packed = pl.pallas_call(
        pack_kernel,
        out_shape=[shape((3 * rows + EXTRA, HD), bf16)] * group,
        in_specs=[HBM] * 5,
        out_specs=[VMEM] * group,
        scratch_shapes=[
            pltpu.VMEM((rows, width), bf16),
            pltpu.SMEM((rows // TILE, SLOTS, STEPS), jnp.int32),
            pltpu.SMEM((rows // TILE, STEPS), jnp.int32),
            pltpu.SemaphoreType.DMA((3 + 2 * group,)),
        ],
        compiler_params=PARAMS,
        name="pack",
    )(
        *[
            pltpu.with_memory_space_constraint(array, pltpu.HBM)
            for array in (
                node_queries,
                node_keys,
                node_values,
                jnp.transpose(tile_index, (1, 2, 0)),
                jnp.transpose(tile_count, (1, 0)),
            )
        ],
    )

    turned = pl.pallas_call(
        functools.partial(turn_kernel, head_total=head_total),
        out_shape=shape((head_total, features, depth // head_total), bf16),
        in_specs=[HBM, HBM],
        out_specs=VMEM,
        scratch_shapes=[
            pltpu.VMEM((head_total, depth // head_total, features), bf16),
            pltpu.SemaphoreType.DMA((head_total,)),
        ],
        compiler_params=PARAMS,
        cost_estimate=pl.CostEstimate(flops=OWN, transcendentals=1, bytes_accessed=1),
        name="turn",
    )(packed[0], pltpu.with_memory_space_constraint(out_weight, pltpu.HBM))

    offsets = list(range(1, -(-(STEPS - 1) // group) + 1))
    plan = stage_plan(group)
    finish = [
        max(at for at, work in enumerate(plan) for table in work if step in table)
        for step in range(group)
    ]
    arrays = {("block", 0): packed[0]}
    near = [step for step in range(1, group) if hops(step) < 2]
    first = ("halo", 1, (0,))

    def send_on(steps):
        message = jnp.stack([arrays["block", step][: 2 * rows] for step in steps])
        for offset in offsets:
            pairs = [(source, (source + offset) % groups) for source in range(groups)]
            arrays["halo", offset, tuple(steps)] = lax.ppermute(message, "group", pairs)

    def send_across(step):
        for offset in offsets:
            pairs = [
                (at * group + p, (at + offset) % groups * group + (p ^ step))
                for at in range(groups)
                for p in range(group)
            ]
            message = packed[step][None, : 2 * rows]
            message, arrays["block", 0] = lax.optimization_barrier((message, arrays["block", 0]))
            arrived = lax.ppermute(message, ("group", "place"), pairs)
            arrays["halo", offset, (step,)] = arrived

    def stage(at, cost):
        work = plan[at]
        started = [
            step
            for step in range(group)
            if finish[step] >= at and any(step in table for work in plan[:at] for table in work)
        ]
        active = sorted(set(started) | {step for table in work for step in table})
        ready = [step for step in sending_order(group) if step in active and finish[step] == at]
        keys = {key for table in work for todo in table.values() for key, _ in todo}
        dests = {step for table in work for step in table}
        names = []
        for name in arrays:
            if name[0] == "halo":
                used = any((name[1], step) in keys for step in name[2])
            elif name[0] == "block":
                used = (0, name[1]) in keys or name[1] in dests
            else:
                used = bool(started)
            if used:
                names.append(name)
        states = [shape((group, HD, rows), f32), shape((group, 8, rows), f32)]
        if len(ready) == len(active):
            states = []
        outs = pl.pallas_call(
            functools.partial(
                attend_kernel,
                names=names,
                work=work,
                started=started,
                active=active,
                ready=ready,
                rows=rows,
            ),
            out_shape=[shape((HD, rows), bf16)] * len(ready) + states,
            in_specs=[VMEM] * len(names),
            out_specs=[VMEM] * (len(ready) + len(states)),
            compiler_params=PARAMS,
            cost_estimate=pl.CostEstimate(flops=cost, transcendentals=1, bytes_accessed=1),
            name="attend",
        )(*[arrays[name] for name in names])
        if states:
            arrays["mixed",], arrays["state",] = outs[len(ready) :]
        return dict(zip(ready, outs))

    for step in near:
        arrays["block", step] = swapped(packed[step], "place", step)
    arrays["block", 0], turned = lax.optimization_barrier((packed[0], turned))
    send_on([0])
    mix = {}
    far_blocks = packed[len(near) + 1 :]
    for step in apart:
        send_across(step)
    for step in near[:1]:
        send_on([step])
    if apart:
        tied = lax.optimization_barrier(
            (far_blocks, turned, [arrays["block", step] for step in near])
        )
        far_blocks, turned, blocks = tied
        arrays.update((("block", step), block) for step, block in zip(near, blocks))
    for step in near[1:]:
        send_on([step])
    for step, block in zip(apart, far_blocks):
        arrays["block", step] = swapped(block, "place", step)
    if apart:
        far_halo = ("halo", 1, tuple(apart))
        tied = lax.optimization_barrier((arrays["block", 0], arrays[far_halo]))
        arrays["block", 0], arrays[far_halo] = tied
    mix.update(stage(0, NEAR))
    for at in range(1, len(plan)):
        done = stage(at, FAR)
        order = [step for step in sending_order(group) if step in done]
        mix.update((step, swapped(done[step], "place", step) if step else done[0]) for step in order)

    mixes = [mix[step] for step in sending_order(group)]
    output = []
    for others, kind in (([0], f32), (list(range(1, head_total)), bf16)):
        parts = mixes
        if output:
            parts = [swapped(entry, "head", other) for other in others for entry in mixes]
        output = [
            pl.pallas_call(
                functools.partial(project_kernel, group=group, others=others),
                out_shape=shape((features, rows), kind),
                in_specs=[VMEM] * (1 + len(parts) + len(output)),
                out_specs=VMEM,
                scratch_shapes=[pltpu.VMEM((len(others), group, HD, rows), bf16)],
                compiler_params=PARAMS,
                name="project",
            )(turned, *parts, *output)
        ]
    return output[0]


def solution(mesh):
    nodes, heads = mesh.devices.shape
    place = HEADS // heads
    split = Mesh(
        mesh.devices.reshape(nodes // place, place, heads), ("group", "place", "head")
    )
    node = ("group", "place")
    return jax.shard_map(
        on_device,
        mesh=split,
        in_specs=(
            P(node, "head"),
            P(node, "head"),
            P(node, "head"),
            P(None, node, None),
            P(None, node),
            P(),
        ),
        out_specs=P("head", node),
        check_vma=False,
    )
```

```python
import functools

import jax
import jax.numpy as jnp
from jax import lax
from jax.experimental import pallas as pl
from jax.experimental.pallas import tpu as pltpu
from jax.sharding import Mesh, PartitionSpec as P

HEADS = 8
HD = 128
TILE = 128
SLOTS = 2
STEPS = 4
LOG2E = 1.4426950408889634
SCALE = LOG2E * HD ** (-0.5)
MASKED = -1e30
EXTRA = 16
OWN = 1000000000
NEAR = 1000000000
FAR = 1000000000
VMEM = pl.BlockSpec(memory_space=pltpu.VMEM)
HBM = pl.BlockSpec(memory_space=pltpu.HBM)
PARAMS = pltpu.CompilerParams(vmem_limit_bytes=48 * 1024 * 1024)


def use_rows(index_ref, count_ref, tiles):
    row = lax.broadcasted_iota(jnp.int32, (EXTRA, HD), 0)
    uses = jnp.zeros((EXTRA, HD), jnp.float32)
    for turn in range(STEPS):
        for dest in range(tiles):
            for source in range(tiles):
                times = jnp.float32(0)
                for slot in range(SLOTS):
                    used = (slot < count_ref[dest, turn]) & (index_ref[dest, slot, turn] == source)
                    times += jnp.where(used, 1.0, 0.0)
                uses = jnp.where(row == (turn * tiles + dest) * tiles + source, times, uses)
    return uses


def hops(step):
    return step.bit_count()


def pack_kernel(query_ref, key_ref, value_ref, index_ref, count_ref, *refs):
    out_refs, (values, index, count, sem) = refs[:-4], refs[-4:]
    group = query_ref.shape[1] // HD
    rows = query_ref.shape[0]
    tiles = rows // TILE
    place = lax.axis_index("place")
    value_copy = pltpu.make_async_copy(value_ref, values, sem.at[0])
    value_copy.start()
    table_copies = [
        pltpu.make_async_copy(index_ref, index, sem.at[1]),
        pltpu.make_async_copy(count_ref, count, sem.at[2]),
    ]
    for copy in table_copies:
        copy.start()
    copies = []
    for step in range(group):
        cols = pl.ds(pl.multiple_of(jnp.bitwise_xor(place, step) * HD, HD), HD)
        copies += [
            pltpu.make_async_copy(
                key_ref.at[:, cols], out_refs[step].at[pl.ds(0, rows)], sem.at[3 + 2 * step]
            ),
            pltpu.make_async_copy(
                query_ref.at[:, cols],
                out_refs[step].at[pl.ds(2 * rows, rows)],
                sem.at[4 + 2 * step],
            ),
        ]
    for copy in copies:
        copy.start()
    for copy in table_copies:
        copy.wait()
    uses = use_rows(index, count, tiles).astype(jnp.bfloat16)
    value_copy.wait()
    for step in range(group):
        cols = pl.ds(pl.multiple_of(jnp.bitwise_xor(place, step) * HD, HD), HD)
        out = out_refs[step]
        out[3 * rows :] = uses
        for at in range(0, rows, TILE):
            out[rows + at : rows + at + TILE] = values[at : at + TILE, cols].T
    for copy in copies:
        copy.wait()


def pair_scores(keys, query_ref, turn):
    rows = keys.shape[0]
    tiles = rows // TILE
    raw = (
        lax.dot_general(
            keys, query_ref[:rows], (((1,), (1,)), ((), ())), preferred_element_type=jnp.float32
        )
        * SCALE
    )
    uses = query_ref[rows:].astype(jnp.float32)
    parts = []
    for source in range(tiles):
        bias = []
        for tile in range(tiles):
            at = (turn * tiles + tile) * tiles + source
            times = uses[at : at + 1]
            bias.append(jnp.where(times > 0.5, times - 1.0, MASKED))
        parts.append(
            raw[source * TILE : (source + 1) * TILE] + jnp.concatenate(bias, axis=1)
        )
    return raw, jnp.concatenate(parts, axis=0)


def own_scores(raw):
    eye = lax.broadcasted_iota(jnp.int32, (TILE, TILE), 0) == lax.broadcasted_iota(
        jnp.int32, (TILE, TILE), 1
    )
    return jnp.concatenate(
        [
            jnp.sum(
                jnp.where(eye, raw[at : at + TILE, at : at + TILE], 0.0), axis=0, keepdims=True
            )
            for at in range(0, raw.shape[0], TILE)
        ],
        axis=1,
    )


def turned_values(source_ref, rows):
    return jnp.concatenate(
        [source_ref[rows + at : rows + at + TILE] for at in range(0, rows, TILE)], axis=1
    )


def attend(query_ref, sources, before):
    rows = query_ref.shape[0] - EXTRA
    scores = []
    for source_ref, turn in sources:
        raw, score = pair_scores(source_ref[:rows], query_ref, turn)
        scores.append(score)
        if turn == 0:
            own = own_scores(raw)
    top = own if before is None else before[0]
    for score in scores:
        top = jnp.maximum(top, jnp.max(score, axis=0, keepdims=True))
    if before is None:
        total = jnp.exp2(own - top)
        own_ref = next(source_ref for source_ref, turn in sources if turn == 0)
        mixed = total * turned_values(own_ref, rows).astype(jnp.float32)
    else:
        factor = jnp.exp2(before[0] - top)
        total, mixed = before[1] * factor, before[2] * factor
    for score, (source_ref, _) in zip(scores, sources):
        weights = jnp.exp2(score - top)
        total = total + jnp.sum(weights, axis=0, keepdims=True)
        mixed = mixed + jnp.dot(
            turned_values(source_ref, rows),
            weights.astype(jnp.bfloat16),
            preferred_element_type=jnp.float32,
        )
    return top, total, mixed


def sources_of(group, place, step):
    result = []
    for turn in range(STEPS):
        slab = (place ^ step) - turn
        result.append(((-(slab // group), place ^ (slab % group)), turn))
    return result


def stage_plan(group):
    steps = list(range(group))
    near = [step for step in steps if hops(step) < 2]
    stages = [(near, lambda offset, step: hops(step) < 2 and (offset == 0 or step == 0))]
    stages.append((steps, lambda offset, step: True))
    plan, taken = [], set()
    for dests, there in stages:
        work = []
        for place in range(group):
            table = {}
            for dest in dests:
                todo = [
                    (key, turn)
                    for key, turn in sources_of(group, place, dest)
                    if there(*key) and (place, dest, turn) not in taken
                ]
                taken.update((place, dest, turn) for _, turn in todo)
                if todo:
                    table[dest] = todo
            work.append(table)
        plan.append(work)
    return plan


def attend_kernel(*refs, names, work, started, active, ready, rows):
    named = dict(zip(names, refs))
    outs = refs[len(names) :]
    out_refs, state_refs = dict(zip(ready, outs)), outs[len(ready) :]
    group = len(work)

    def block(offset, step):
        for name in named:
            if name[0] == "halo" and name[1] == offset and step in name[2]:
                return named[name].at[name[2].index(step)]
        return named["block", step]

    def queries(step):
        return named["block", step].at[pl.ds(2 * rows, rows + EXTRA)]

    here = lax.axis_index("place")
    for place in range(group):

        @pl.when(here == place)
        def _(place=place):
            for step in active:
                before = None
                if step in started:
                    mixed_ref, state_ref = named["mixed",], named["state",]
                    before = (state_ref[step, 0:1], state_ref[step, 1:2], mixed_ref[step])
                todo = [(block(*key), turn) for key, turn in work[place].get(step, [])]
                top, total, mixed = attend(queries(step), todo, before) if todo else before
                if step in ready:
                    out_refs[step][...] = (mixed / total).astype(out_refs[step].dtype)
                else:
                    state_refs[0][step] = mixed
                    state_refs[1][step, 0:1] = top
                    state_refs[1][step, 1:2] = total


def turn_kernel(block_ref, weight_ref, turned_ref, held, sem, *, head_total):
    me = lax.axis_index("head")
    depth = weight_ref.shape[0] // head_total
    features = weight_ref.shape[1] // head_total
    copies = []
    for other in range(head_total):
        start = pl.multiple_of(jnp.bitwise_xor(me, other) * depth, depth)
        cols = pl.ds(pl.multiple_of(me * features, features), features)
        copies.append(
            pltpu.make_async_copy(
                weight_ref.at[pl.ds(start, depth), cols], held.at[other], sem.at[other]
            )
        )
        copies[-1].start()
    for other in range(head_total):
        copies[other].wait()
        turned_ref[other] = held[other].T


def sending_order(group):
    return sorted(range(group), key=lambda step: (step > 0, -hops(step), step))


def project_kernel(turned_ref, *refs, group, others):
    mix_refs, refs = refs[: len(others) * group], refs[len(others) * group :]
    so_far, (out_ref, mix) = refs[:-2], refs[-2:]
    place = lax.axis_index("place")
    for number in range(len(others)):
        for at, step in enumerate(sending_order(group)):
            mix[number, jnp.bitwise_xor(place, step)] = mix_refs[number * group + at][...]
    result = so_far[0][...] if so_far else None
    for number, other in enumerate(others):
        part = jnp.dot(
            turned_ref[other],
            mix[number].reshape(turned_ref.shape[2], out_ref.shape[1]),
            preferred_element_type=jnp.float32,
        )
        result = part if result is None else result + part
    out_ref[...] = result.astype(out_ref.dtype)


def swapped(value, axis, step):
    count = lax.axis_size(axis)
    return lax.ppermute(value, axis, [(source, source ^ step) for source in range(count)])


def on_device(node_queries, node_keys, node_values, tile_index, tile_count, out_weight):
    rows, width = node_queries.shape
    group = width // HD
    groups = lax.axis_size("group")
    head_total = lax.axis_size("head")
    depth, feature_total = out_weight.shape
    features = feature_total // head_total
    bf16, f32 = jnp.bfloat16, jnp.float32
    shape = jax.ShapeDtypeStruct

    apart = [step for step in range(group) if hops(step) > 1]
    packed = pl.pallas_call(
        pack_kernel,
        out_shape=[shape((3 * rows + EXTRA, HD), bf16)] * group,
        in_specs=[HBM] * 5,
        out_specs=[VMEM] * group,
        scratch_shapes=[
            pltpu.VMEM((rows, width), bf16),
            pltpu.SMEM((rows // TILE, SLOTS, STEPS), jnp.int32),
            pltpu.SMEM((rows // TILE, STEPS), jnp.int32),
            pltpu.SemaphoreType.DMA((3 + 2 * group,)),
        ],
        compiler_params=PARAMS,
        name="pack",
    )(
        *[
            pltpu.with_memory_space_constraint(array, pltpu.HBM)
            for array in (
                node_queries,
                node_keys,
                node_values,
                jnp.transpose(tile_index, (1, 2, 0)),
                jnp.transpose(tile_count, (1, 0)),
            )
        ],
    )

    turned = pl.pallas_call(
        functools.partial(turn_kernel, head_total=head_total),
        out_shape=shape((head_total, features, depth // head_total), bf16),
        in_specs=[HBM, HBM],
        out_specs=VMEM,
        scratch_shapes=[
            pltpu.VMEM((head_total, depth // head_total, features), bf16),
            pltpu.SemaphoreType.DMA((head_total,)),
        ],
        compiler_params=PARAMS,
        cost_estimate=pl.CostEstimate(flops=OWN, transcendentals=1, bytes_accessed=1),
        name="turn",
    )(packed[0], pltpu.with_memory_space_constraint(out_weight, pltpu.HBM))

    offsets = list(range(1, -(-(STEPS - 1) // group) + 1))
    plan = stage_plan(group)
    finish = [
        max(at for at, work in enumerate(plan) for table in work if step in table)
        for step in range(group)
    ]
    arrays = {("block", 0): packed[0]}
    near = [step for step in range(1, group) if hops(step) < 2]
    first = ("halo", 1, (0,))

    def send(message, step, across):
        for offset in offsets:
            first = max(0, offset * group - STEPS + 1)
            pairs = []
            for at in range(groups):
                for p in range(group):
                    slab, target = (p, p ^ step) if across else (p ^ step, p)
                    goal = (at + offset) % groups if slab >= first else at
                    pairs.append((at * group + p, goal * group + target))
            arrived = lax.ppermute(message, ("group", "place"), pairs)
            arrays["halo", offset, (step,)] = arrived

    def send_on(step):
        send(arrays["block", step][None, : 2 * rows], step, False)

    def send_across(step):
        message = packed[step][None, : 2 * rows]
        message, arrays["block", 0] = lax.optimization_barrier((message, arrays["block", 0]))
        send(message, step, True)

    def stage(at, cost):
        work = plan[at]
        started = [
            step
            for step in range(group)
            if finish[step] >= at and any(step in table for work in plan[:at] for table in work)
        ]
        active = sorted(set(started) | {step for table in work for step in table})
        ready = [step for step in sending_order(group) if step in active and finish[step] == at]
        keys = {key for table in work for todo in table.values() for key, _ in todo}
        dests = {step for table in work for step in table}
        names = []
        for name in arrays:
            if name[0] == "halo":
                used = any((name[1], step) in keys for step in name[2])
            elif name[0] == "block":
                used = (0, name[1]) in keys or name[1] in dests
            else:
                used = bool(started)
            if used:
                names.append(name)
        states = [shape((group, HD, rows), f32), shape((group, 8, rows), f32)]
        if len(ready) == len(active):
            states = []
        outs = pl.pallas_call(
            functools.partial(
                attend_kernel,
                names=names,
                work=work,
                started=started,
                active=active,
                ready=ready,
                rows=rows,
            ),
            out_shape=[shape((HD, rows), bf16)] * len(ready) + states,
            in_specs=[VMEM] * len(names),
            out_specs=[VMEM] * (len(ready) + len(states)),
            compiler_params=PARAMS,
            cost_estimate=pl.CostEstimate(flops=cost, transcendentals=1, bytes_accessed=1),
            name="attend",
        )(*[arrays[name] for name in names])
        if states:
            arrays["mixed",], arrays["state",] = outs[len(ready) :]
        return dict(zip(ready, outs))

    for step in near:
        arrays["block", step] = swapped(packed[step], "place", step)
    arrays["block", 0], turned = lax.optimization_barrier((packed[0], turned))
    send_on(0)
    mix = {}
    far_blocks = packed[len(near) + 1 :]
    for step in apart:
        send_across(step)
    for step in near[:1]:
        send_on(step)
    if apart:
        tied = lax.optimization_barrier(
            (far_blocks, turned, [arrays["block", step] for step in near])
        )
        far_blocks, turned, blocks = tied
        arrays.update((("block", step), block) for step, block in zip(near, blocks))
    for step in near[1:]:
        send_on(step)
    for step, block in zip(apart, far_blocks):
        arrays["block", step] = swapped(block, "place", step)
    if apart:
        far_halo = ("halo", 1, tuple(apart))
        tied = lax.optimization_barrier((arrays["block", 0], arrays[far_halo]))
        arrays["block", 0], arrays[far_halo] = tied
    mix.update(stage(0, NEAR))
    for at in range(1, len(plan)):
        done = stage(at, FAR)
        order = [step for step in sending_order(group) if step in done]
        mix.update((step, swapped(done[step], "place", step) if step else done[0]) for step in order)

    mixes = [mix[step] for step in sending_order(group)]
    output = []
    for others, kind in (([0], f32), (list(range(1, head_total)), bf16)):
        parts = mixes
        if output:
            parts = [swapped(entry, "head", other) for other in others for entry in mixes]
        output = [
            pl.pallas_call(
                functools.partial(project_kernel, group=group, others=others),
                out_shape=shape((features, rows), kind),
                in_specs=[VMEM] * (1 + len(parts) + len(output)),
                out_specs=VMEM,
                scratch_shapes=[pltpu.VMEM((len(others), group, HD, rows), bf16)],
                compiler_params=PARAMS,
                name="project",
            )(turned, *parts, *output)
        ]
    return output[0]


def solution(mesh):
    nodes, heads = mesh.devices.shape
    place = HEADS // heads
    split = Mesh(
        mesh.devices.reshape(nodes // place, place, heads), ("group", "place", "head")
    )
    node = ("group", "place")
    return jax.shard_map(
        on_device,
        mesh=split,
        in_specs=(
            P(node, "head"),
            P(node, "head"),
            P(node, "head"),
            P(None, node, None),
            P(None, node),
            P(),
        ),
        out_specs=P("head", node),
        check_vma=False,
    )
```

```python
import functools

import jax
import jax.numpy as jnp
from jax import lax
from jax.experimental import pallas as pl
from jax.experimental.pallas import tpu as pltpu
from jax.sharding import Mesh, PartitionSpec as P

HEADS = 8
HD = 128
TILE = 128
SLOTS = 2
STEPS = 4
LOG2E = 1.4426950408889634
SCALE = LOG2E * HD ** (-0.5)
MASKED = -1e30
EXTRA = 16
OWN = 1000000000
NEAR = 1000000000
FAR = 1000000000
VMEM = pl.BlockSpec(memory_space=pltpu.VMEM)
HBM = pl.BlockSpec(memory_space=pltpu.HBM)
PARAMS = pltpu.CompilerParams(vmem_limit_bytes=48 * 1024 * 1024)


def use_rows(index_ref, count_ref, tiles):
    row = lax.broadcasted_iota(jnp.int32, (EXTRA, HD), 0)
    uses = jnp.zeros((EXTRA, HD), jnp.float32)
    for turn in range(STEPS):
        for dest in range(tiles):
            for source in range(tiles):
                times = jnp.float32(0)
                for slot in range(SLOTS):
                    used = (slot < count_ref[dest, turn]) & (index_ref[dest, slot, turn] == source)
                    times += jnp.where(used, 1.0, 0.0)
                uses = jnp.where(row == (turn * tiles + dest) * tiles + source, times, uses)
    return uses


def hops(step):
    return step.bit_count()


def pack_kernel(query_ref, key_ref, value_ref, index_ref, count_ref, *refs):
    out_refs, (values, index, count, sem) = refs[:-4], refs[-4:]
    group = query_ref.shape[1] // HD
    rows = query_ref.shape[0]
    tiles = rows // TILE
    place = lax.axis_index("place")
    value_copy = pltpu.make_async_copy(value_ref, values, sem.at[0])
    value_copy.start()
    table_copies = [
        pltpu.make_async_copy(index_ref, index, sem.at[1]),
        pltpu.make_async_copy(count_ref, count, sem.at[2]),
    ]
    for copy in table_copies:
        copy.start()
    copies = []
    for step in range(group):
        cols = pl.ds(pl.multiple_of(jnp.bitwise_xor(place, step) * HD, HD), HD)
        copies += [
            pltpu.make_async_copy(
                key_ref.at[:, cols], out_refs[step].at[pl.ds(0, rows)], sem.at[3 + 2 * step]
            ),
            pltpu.make_async_copy(
                query_ref.at[:, cols],
                out_refs[step].at[pl.ds(2 * rows, rows)],
                sem.at[4 + 2 * step],
            ),
        ]
    for copy in copies:
        copy.start()
    for copy in table_copies:
        copy.wait()
    uses = use_rows(index, count, tiles).astype(jnp.bfloat16)
    value_copy.wait()
    for step in range(group):
        cols = pl.ds(pl.multiple_of(jnp.bitwise_xor(place, step) * HD, HD), HD)
        out = out_refs[step]
        out[3 * rows :] = uses
        for at in range(0, rows, TILE):
            out[rows + at : rows + at + TILE] = values[at : at + TILE, cols].T
    for copy in copies:
        copy.wait()


def pair_scores(keys, query_ref, turn):
    rows = keys.shape[0]
    tiles = rows // TILE
    raw = (
        lax.dot_general(
            keys, query_ref[:rows], (((1,), (1,)), ((), ())), preferred_element_type=jnp.float32
        )
        * SCALE
    )
    uses = query_ref[rows:].astype(jnp.float32)
    parts = []
    for source in range(tiles):
        bias = []
        for tile in range(tiles):
            at = (turn * tiles + tile) * tiles + source
            times = uses[at : at + 1]
            bias.append(jnp.where(times > 0.5, times - 1.0, MASKED))
        parts.append(
            raw[source * TILE : (source + 1) * TILE] + jnp.concatenate(bias, axis=1)
        )
    return raw, jnp.concatenate(parts, axis=0)


def own_scores(raw):
    eye = lax.broadcasted_iota(jnp.int32, (TILE, TILE), 0) == lax.broadcasted_iota(
        jnp.int32, (TILE, TILE), 1
    )
    return jnp.concatenate(
        [
            jnp.sum(
                jnp.where(eye, raw[at : at + TILE, at : at + TILE], 0.0), axis=0, keepdims=True
            )
            for at in range(0, raw.shape[0], TILE)
        ],
        axis=1,
    )


def turned_values(source_ref, rows):
    return jnp.concatenate(
        [source_ref[rows + at : rows + at + TILE] for at in range(0, rows, TILE)], axis=1
    )


def attend(query_ref, sources, before):
    rows = query_ref.shape[0] - EXTRA
    scores = []
    for source_ref, turn in sources:
        raw, score = pair_scores(source_ref[:rows], query_ref, turn)
        scores.append(score)
        if turn == 0:
            own = own_scores(raw)
    top = own if before is None else before[0]
    for score in scores:
        top = jnp.maximum(top, jnp.max(score, axis=0, keepdims=True))
    if before is None:
        total = jnp.exp2(own - top)
        own_ref = next(source_ref for source_ref, turn in sources if turn == 0)
        mixed = total * turned_values(own_ref, rows).astype(jnp.float32)
    else:
        factor = jnp.exp2(before[0] - top)
        total, mixed = before[1] * factor, before[2] * factor
    for score, (source_ref, _) in zip(scores, sources):
        weights = jnp.exp2(score - top)
        total = total + jnp.sum(weights, axis=0, keepdims=True)
        mixed = mixed + jnp.dot(
            turned_values(source_ref, rows),
            weights.astype(jnp.bfloat16),
            preferred_element_type=jnp.float32,
        )
    return top, total, mixed


def sources_of(group, place, step):
    result = []
    for turn in range(STEPS):
        slab = (place ^ step) - turn
        result.append(((-(slab // group), place ^ (slab % group)), turn))
    return result


def stage_plan(group):
    steps = list(range(group))
    near = [step for step in steps if hops(step) < 2]
    stages = [(near, lambda offset, step: hops(step) < 2 and (offset == 0 or step == 0))]
    stages.append((steps, lambda offset, step: offset == 0 or step != near[-1]))
    stages.append((steps, lambda offset, step: True))
    plan, taken = [], set()
    for dests, there in stages:
        work = []
        for place in range(group):
            table = {}
            for dest in dests:
                todo = [
                    (key, turn)
                    for key, turn in sources_of(group, place, dest)
                    if there(*key) and (place, dest, turn) not in taken
                ]
                taken.update((place, dest, turn) for _, turn in todo)
                if todo:
                    table[dest] = todo
            work.append(table)
        plan.append(work)
    return plan


def attend_kernel(*refs, names, work, started, active, ready, rows):
    named = dict(zip(names, refs))
    outs = refs[len(names) :]
    out_refs, state_refs = dict(zip(ready, outs)), outs[len(ready) :]
    group = len(work)

    def block(offset, step):
        for name in named:
            if name[0] == "halo" and name[1] == offset and step in name[2]:
                return named[name].at[name[2].index(step)]
        return named["block", step]

    def queries(step):
        return named["block", step].at[pl.ds(2 * rows, rows + EXTRA)]

    here = lax.axis_index("place")
    for place in range(group):

        @pl.when(here == place)
        def _(place=place):
            for step in active:
                before = None
                if step in started:
                    mixed_ref, state_ref = named["mixed",], named["state",]
                    before = (state_ref[step, 0:1], state_ref[step, 1:2], mixed_ref[step])
                todo = [(block(*key), turn) for key, turn in work[place].get(step, [])]
                top, total, mixed = attend(queries(step), todo, before) if todo else before
                if step in ready:
                    out_refs[step][...] = (mixed / total).astype(out_refs[step].dtype)
                else:
                    state_refs[0][step] = mixed
                    state_refs[1][step, 0:1] = top
                    state_refs[1][step, 1:2] = total


def turn_kernel(block_ref, weight_ref, turned_ref, held, sem, *, head_total):
    me = lax.axis_index("head")
    depth = weight_ref.shape[0] // head_total
    features = weight_ref.shape[1] // head_total
    copies = []
    for other in range(head_total):
        start = pl.multiple_of(jnp.bitwise_xor(me, other) * depth, depth)
        cols = pl.ds(pl.multiple_of(me * features, features), features)
        copies.append(
            pltpu.make_async_copy(
                weight_ref.at[pl.ds(start, depth), cols], held.at[other], sem.at[other]
            )
        )
        copies[-1].start()
    for other in range(head_total):
        copies[other].wait()
        turned_ref[other] = held[other].T


def sending_order(group):
    last = max(step for step in range(group) if hops(step) < 2)
    return sorted(range(group), key=lambda step: (step > 0, step != last, -hops(step), step))


def project_kernel(turned_ref, *refs, group, others):
    mix_refs, refs = refs[: len(others) * group], refs[len(others) * group :]
    so_far, (out_ref, mix) = refs[:-2], refs[-2:]
    place = lax.axis_index("place")
    for number in range(len(others)):
        for at, step in enumerate(sending_order(group)):
            mix[number, jnp.bitwise_xor(place, step)] = mix_refs[number * group + at][...]
    result = so_far[0][...] if so_far else None
    for number, other in enumerate(others):
        part = jnp.dot(
            turned_ref[other],
            mix[number].reshape(turned_ref.shape[2], out_ref.shape[1]),
            preferred_element_type=jnp.float32,
        )
        result = part if result is None else result + part
    out_ref[...] = result.astype(out_ref.dtype)


def swapped(value, axis, step):
    count = lax.axis_size(axis)
    return lax.ppermute(value, axis, [(source, source ^ step) for source in range(count)])


def on_device(node_queries, node_keys, node_values, tile_index, tile_count, out_weight):
    rows, width = node_queries.shape
    group = width // HD
    groups = lax.axis_size("group")
    head_total = lax.axis_size("head")
    depth, feature_total = out_weight.shape
    features = feature_total // head_total
    bf16, f32 = jnp.bfloat16, jnp.float32
    shape = jax.ShapeDtypeStruct

    apart = [step for step in range(group) if hops(step) > 1]
    packed = pl.pallas_call(
        pack_kernel,
        out_shape=[shape((3 * rows + EXTRA, HD), bf16)] * group,
        in_specs=[HBM] * 5,
        out_specs=[VMEM] * group,
        scratch_shapes=[
            pltpu.VMEM((rows, width), bf16),
            pltpu.SMEM((rows // TILE, SLOTS, STEPS), jnp.int32),
            pltpu.SMEM((rows // TILE, STEPS), jnp.int32),
            pltpu.SemaphoreType.DMA((3 + 2 * group,)),
        ],
        compiler_params=PARAMS,
        name="pack",
    )(
        *[
            pltpu.with_memory_space_constraint(array, pltpu.HBM)
            for array in (
                node_queries,
                node_keys,
                node_values,
                jnp.transpose(tile_index, (1, 2, 0)),
                jnp.transpose(tile_count, (1, 0)),
            )
        ],
    )

    turned = pl.pallas_call(
        functools.partial(turn_kernel, head_total=head_total),
        out_shape=shape((head_total, features, depth // head_total), bf16),
        in_specs=[HBM, HBM],
        out_specs=VMEM,
        scratch_shapes=[
            pltpu.VMEM((head_total, depth // head_total, features), bf16),
            pltpu.SemaphoreType.DMA((head_total,)),
        ],
        compiler_params=PARAMS,
        cost_estimate=pl.CostEstimate(flops=OWN, transcendentals=1, bytes_accessed=1),
        name="turn",
    )(packed[0], pltpu.with_memory_space_constraint(out_weight, pltpu.HBM))

    offsets = list(range(1, -(-(STEPS - 1) // group) + 1))
    plan = stage_plan(group)
    finish = [
        max(at for at, work in enumerate(plan) for table in work if step in table)
        for step in range(group)
    ]
    arrays = {("block", 0): packed[0]}
    near = [step for step in range(1, group) if hops(step) < 2]
    first = ("halo", 1, (0,))

    def send_on(steps):
        message = jnp.stack([arrays["block", step][: 2 * rows] for step in steps])
        for offset in offsets:
            pairs = [(source, (source + offset) % groups) for source in range(groups)]
            arrays["halo", offset, tuple(steps)] = lax.ppermute(message, "group", pairs)

    def send_across(step):
        for offset in offsets:
            pairs = [
                (at * group + p, (at + offset) % groups * group + (p ^ step))
                for at in range(groups)
                for p in range(group)
            ]
            message = packed[step][None, : 2 * rows]
            message, arrays["block", 0] = lax.optimization_barrier((message, arrays["block", 0]))
            arrived = lax.ppermute(message, ("group", "place"), pairs)
            arrays["halo", offset, (step,)] = arrived

    def stage(at, cost):
        work = plan[at]
        started = [
            step
            for step in range(group)
            if finish[step] >= at and any(step in table for work in plan[:at] for table in work)
        ]
        active = sorted(set(started) | {step for table in work for step in table})
        ready = [step for step in sending_order(group) if step in active and finish[step] == at]
        keys = {key for table in work for todo in table.values() for key, _ in todo}
        dests = {step for table in work for step in table}
        names = []
        for name in arrays:
            if name[0] == "halo":
                used = any((name[1], step) in keys for step in name[2])
            elif name[0] == "block":
                used = (0, name[1]) in keys or name[1] in dests
            else:
                used = bool(started)
            if used:
                names.append(name)
        states = [shape((group, HD, rows), f32), shape((group, 8, rows), f32)]
        if len(ready) == len(active):
            states = []
        outs = pl.pallas_call(
            functools.partial(
                attend_kernel,
                names=names,
                work=work,
                started=started,
                active=active,
                ready=ready,
                rows=rows,
            ),
            out_shape=[shape((HD, rows), bf16)] * len(ready) + states,
            in_specs=[VMEM] * len(names),
            out_specs=[VMEM] * (len(ready) + len(states)),
            compiler_params=PARAMS,
            cost_estimate=pl.CostEstimate(flops=cost, transcendentals=1, bytes_accessed=1),
            name="attend",
        )(*[arrays[name] for name in names])
        if states:
            arrays["mixed",], arrays["state",] = outs[len(ready) :]
        return dict(zip(ready, outs))

    for step in near:
        arrays["block", step] = swapped(packed[step], "place", step)
    arrays["block", 0], turned = lax.optimization_barrier((packed[0], turned))
    send_on([0])
    mix = {}
    far_blocks = packed[len(near) + 1 :]
    for step in apart:
        send_across(step)
    for step in near[:1]:
        send_on([step])
    if apart:
        tied = lax.optimization_barrier(
            (far_blocks, turned, [arrays["block", step] for step in near])
        )
        far_blocks, turned, blocks = tied
        arrays.update((("block", step), block) for step, block in zip(near, blocks))
    for step in near[1:]:
        send_on([step])
    for step, block in zip(apart, far_blocks):
        arrays["block", step] = swapped(block, "place", step)
    mix.update(stage(0, NEAR))
    for at in range(1, len(plan)):
        done = stage(at, FAR)
        order = [step for step in sending_order(group) if step in done]
        mix.update((step, swapped(done[step], "place", step) if step else done[0]) for step in order)

    mixes = [mix[step] for step in sending_order(group)]
    output = []
    for others, kind in (([0], f32), (list(range(1, head_total)), bf16)):
        parts = mixes
        if output:
            parts = [swapped(entry, "head", other) for other in others for entry in mixes]
        output = [
            pl.pallas_call(
                functools.partial(project_kernel, group=group, others=others),
                out_shape=shape((features, rows), kind),
                in_specs=[VMEM] * (1 + len(parts) + len(output)),
                out_specs=VMEM,
                scratch_shapes=[pltpu.VMEM((len(others), group, HD, rows), bf16)],
                compiler_params=PARAMS,
                name="project",
            )(turned, *parts, *output)
        ]
    return output[0]


def solution(mesh):
    nodes, heads = mesh.devices.shape
    place = HEADS // heads
    split = Mesh(
        mesh.devices.reshape(nodes // place, place, heads), ("group", "place", "head")
    )
    node = ("group", "place")
    return jax.shard_map(
        on_device,
        mesh=split,
        in_specs=(
            P(node, "head"),
            P(node, "head"),
            P(node, "head"),
            P(None, node, None),
            P(None, node),
            P(),
        ),
        out_specs=P("head", node),
        check_vma=False,
    )
```

```python
import functools

import jax
import jax.numpy as jnp
from jax import lax
from jax.experimental import pallas as pl
from jax.experimental.pallas import tpu as pltpu
from jax.sharding import Mesh, PartitionSpec as P

HEADS = 8
HD = 128
TILE = 128
SLOTS = 2
STEPS = 4
LOG2E = 1.4426950408889634
SCALE = LOG2E * HD ** (-0.5)
MASKED = -1e30
EXTRA = 16
OWN = 1000000000
NEAR = 1000000000
FAR = 1000000000
VMEM = pl.BlockSpec(memory_space=pltpu.VMEM)
HBM = pl.BlockSpec(memory_space=pltpu.HBM)
PARAMS = pltpu.CompilerParams(vmem_limit_bytes=48 * 1024 * 1024)


def use_rows(index_ref, count_ref, tiles):
    row = lax.broadcasted_iota(jnp.int32, (EXTRA, HD), 0)
    uses = jnp.zeros((EXTRA, HD), jnp.float32)
    for turn in range(STEPS):
        for dest in range(tiles):
            for source in range(tiles):
                times = jnp.float32(0)
                for slot in range(SLOTS):
                    used = (slot < count_ref[dest, turn]) & (index_ref[dest, slot, turn] == source)
                    times += jnp.where(used, 1.0, 0.0)
                uses = jnp.where(row == (turn * tiles + dest) * tiles + source, times, uses)
    return uses


def hops(step):
    return step.bit_count()


def pack_kernel(query_ref, key_ref, value_ref, index_ref, count_ref, *refs):
    out_refs, (values, index, count, sem) = refs[:-4], refs[-4:]
    group = query_ref.shape[1] // HD
    rows = query_ref.shape[0]
    tiles = rows // TILE
    place = lax.axis_index("place")
    value_copy = pltpu.make_async_copy(value_ref, values, sem.at[0])
    value_copy.start()
    table_copies = [
        pltpu.make_async_copy(index_ref, index, sem.at[1]),
        pltpu.make_async_copy(count_ref, count, sem.at[2]),
    ]
    for copy in table_copies:
        copy.start()
    copies = []
    for step in range(group):
        cols = pl.ds(pl.multiple_of(jnp.bitwise_xor(place, step) * HD, HD), HD)
        copies += [
            pltpu.make_async_copy(
                key_ref.at[:, cols], out_refs[step].at[pl.ds(0, rows)], sem.at[3 + 2 * step]
            ),
            pltpu.make_async_copy(
                query_ref.at[:, cols],
                out_refs[step].at[pl.ds(2 * rows, rows)],
                sem.at[4 + 2 * step],
            ),
        ]
    for copy in copies:
        copy.start()
    for copy in table_copies:
        copy.wait()
    uses = use_rows(index, count, tiles).astype(jnp.bfloat16)
    value_copy.wait()
    for step in range(group):
        cols = pl.ds(pl.multiple_of(jnp.bitwise_xor(place, step) * HD, HD), HD)
        out = out_refs[step]
        out[3 * rows :] = uses
        for at in range(0, rows, TILE):
            out[rows + at : rows + at + TILE] = values[at : at + TILE, cols].T
    for copy in copies:
        copy.wait()


def pair_scores(keys, query_ref, turn):
    rows = keys.shape[0]
    tiles = rows // TILE
    raw = (
        lax.dot_general(
            keys, query_ref[:rows], (((1,), (1,)), ((), ())), preferred_element_type=jnp.float32
        )
        * SCALE
    )
    uses = query_ref[rows:].astype(jnp.float32)
    parts = []
    for source in range(tiles):
        bias = []
        for tile in range(tiles):
            at = (turn * tiles + tile) * tiles + source
            times = uses[at : at + 1]
            bias.append(jnp.where(times > 0.5, times - 1.0, MASKED))
        parts.append(
            raw[source * TILE : (source + 1) * TILE] + jnp.concatenate(bias, axis=1)
        )
    return raw, jnp.concatenate(parts, axis=0)


def own_scores(raw):
    eye = lax.broadcasted_iota(jnp.int32, (TILE, TILE), 0) == lax.broadcasted_iota(
        jnp.int32, (TILE, TILE), 1
    )
    return jnp.concatenate(
        [
            jnp.sum(
                jnp.where(eye, raw[at : at + TILE, at : at + TILE], 0.0), axis=0, keepdims=True
            )
            for at in range(0, raw.shape[0], TILE)
        ],
        axis=1,
    )


def turned_values(source_ref, rows):
    return jnp.concatenate(
        [source_ref[rows + at : rows + at + TILE] for at in range(0, rows, TILE)], axis=1
    )


def attend(query_ref, sources, before):
    rows = query_ref.shape[0] - EXTRA
    scores = []
    for source_ref, turn in sources:
        raw, score = pair_scores(source_ref[:rows], query_ref, turn)
        scores.append(score)
        if turn == 0:
            own = own_scores(raw)
    top = own if before is None else before[0]
    for score in scores:
        top = jnp.maximum(top, jnp.max(score, axis=0, keepdims=True))
    if before is None:
        total = jnp.exp2(own - top)
        own_ref = next(source_ref for source_ref, turn in sources if turn == 0)
        mixed = total * turned_values(own_ref, rows).astype(jnp.float32)
    else:
        factor = jnp.exp2(before[0] - top)
        total, mixed = before[1] * factor, before[2] * factor
    for score, (source_ref, _) in zip(scores, sources):
        weights = jnp.exp2(score - top)
        total = total + jnp.sum(weights, axis=0, keepdims=True)
        mixed = mixed + jnp.dot(
            turned_values(source_ref, rows),
            weights.astype(jnp.bfloat16),
            preferred_element_type=jnp.float32,
        )
    return top, total, mixed


def sources_of(group, place, step):
    result = []
    for turn in range(STEPS):
        slab = (place ^ step) - turn
        result.append(((-(slab // group), place ^ (slab % group)), turn))
    return result


def stage_plan(group):
    steps = list(range(group))
    near = [step for step in steps if hops(step) < 2]
    stages = [(near, lambda offset, step: offset == 0 and hops(step) < 2)]
    if len(near) < group:
        stages.append((steps, lambda offset, step: offset == 0 or step == 1 or hops(step) > 1))
    stages.append((steps, lambda offset, step: True))
    plan, taken = [], set()
    for dests, there in stages:
        work = []
        for place in range(group):
            table = {}
            for dest in dests:
                todo = [
                    (key, turn)
                    for key, turn in sources_of(group, place, dest)
                    if there(*key) and (place, dest, turn) not in taken
                ]
                taken.update((place, dest, turn) for _, turn in todo)
                if todo:
                    table[dest] = todo
            work.append(table)
        plan.append(work)
    return plan


def attend_kernel(*refs, names, work, started, active, ready, rows):
    named = dict(zip(names, refs))
    outs = refs[len(names) :]
    out_refs, state_refs = dict(zip(ready, outs)), outs[len(ready) :]
    group = len(work)

    def block(offset, step):
        for name in named:
            if name[0] == "halo" and name[1] == offset and step in name[2]:
                return named[name].at[name[2].index(step)]
        return named["block", step]

    def queries(step):
        return named["block", step].at[pl.ds(2 * rows, rows + EXTRA)]

    here = lax.axis_index("place")
    for place in range(group):

        @pl.when(here == place)
        def _(place=place):
            for step in active:
                before = None
                if step in started:
                    mixed_ref, state_ref = named["mixed",], named["state",]
                    before = (state_ref[step, 0:1], state_ref[step, 1:2], mixed_ref[step])
                todo = [(block(*key), turn) for key, turn in work[place].get(step, [])]
                top, total, mixed = attend(queries(step), todo, before) if todo else before
                if step in ready:
                    out_refs[step][...] = (mixed / total).astype(out_refs[step].dtype)
                else:
                    state_refs[0][step] = mixed
                    state_refs[1][step, 0:1] = top
                    state_refs[1][step, 1:2] = total


def turn_kernel(block_ref, weight_ref, turned_ref, held, sem, *, head_total):
    me = lax.axis_index("head")
    depth = weight_ref.shape[0] // head_total
    features = weight_ref.shape[1] // head_total
    copies = []
    for other in range(head_total):
        start = pl.multiple_of(jnp.bitwise_xor(me, other) * depth, depth)
        cols = pl.ds(pl.multiple_of(me * features, features), features)
        copies.append(
            pltpu.make_async_copy(
                weight_ref.at[pl.ds(start, depth), cols], held.at[other], sem.at[other]
            )
        )
        copies[-1].start()
    for other in range(head_total):
        copies[other].wait()
        turned_ref[other] = held[other].T


def sending_order(group):
    last = max(step for step in range(group) if hops(step) < 2)
    return sorted(range(group), key=lambda step: (step > 0, step != last, -hops(step), step))


def project_kernel(turned_ref, *refs, group, others):
    mix_refs, refs = refs[: len(others) * group], refs[len(others) * group :]
    so_far, (out_ref, mix) = refs[:-2], refs[-2:]
    place = lax.axis_index("place")
    for number in range(len(others)):
        for at, step in enumerate(sending_order(group)):
            mix[number, jnp.bitwise_xor(place, step)] = mix_refs[number * group + at][...]
    result = so_far[0][...] if so_far else None
    for number, other in enumerate(others):
        part = jnp.dot(
            turned_ref[other],
            mix[number].reshape(turned_ref.shape[2], out_ref.shape[1]),
            preferred_element_type=jnp.float32,
        )
        result = part if result is None else result + part
    out_ref[...] = result.astype(out_ref.dtype)


def swapped(value, axis, step):
    count = lax.axis_size(axis)
    return lax.ppermute(value, axis, [(source, source ^ step) for source in range(count)])


def on_device(node_queries, node_keys, node_values, tile_index, tile_count, out_weight):
    rows, width = node_queries.shape
    group = width // HD
    groups = lax.axis_size("group")
    head_total = lax.axis_size("head")
    depth, feature_total = out_weight.shape
    features = feature_total // head_total
    bf16, f32 = jnp.bfloat16, jnp.float32
    shape = jax.ShapeDtypeStruct

    apart = [step for step in range(group) if hops(step) > 1]
    packed = pl.pallas_call(
        pack_kernel,
        out_shape=[shape((3 * rows + EXTRA, HD), bf16)] * group,
        in_specs=[HBM] * 5,
        out_specs=[VMEM] * group,
        scratch_shapes=[
            pltpu.VMEM((rows, width), bf16),
            pltpu.SMEM((rows // TILE, SLOTS, STEPS), jnp.int32),
            pltpu.SMEM((rows // TILE, STEPS), jnp.int32),
            pltpu.SemaphoreType.DMA((3 + 2 * group,)),
        ],
        compiler_params=PARAMS,
        name="pack",
    )(
        *[
            pltpu.with_memory_space_constraint(array, pltpu.HBM)
            for array in (
                node_queries,
                node_keys,
                node_values,
                jnp.transpose(tile_index, (1, 2, 0)),
                jnp.transpose(tile_count, (1, 0)),
            )
        ],
    )

    turned = pl.pallas_call(
        functools.partial(turn_kernel, head_total=head_total),
        out_shape=shape((head_total, features, depth // head_total), bf16),
        in_specs=[HBM, HBM],
        out_specs=VMEM,
        scratch_shapes=[
            pltpu.VMEM((head_total, depth // head_total, features), bf16),
            pltpu.SemaphoreType.DMA((head_total,)),
        ],
        compiler_params=PARAMS,
        cost_estimate=pl.CostEstimate(flops=OWN, transcendentals=1, bytes_accessed=1),
        name="turn",
    )(packed[0], pltpu.with_memory_space_constraint(out_weight, pltpu.HBM))

    offsets = list(range(1, -(-(STEPS - 1) // group) + 1))
    plan = stage_plan(group)
    finish = [
        max(at for at, work in enumerate(plan) for table in work if step in table)
        for step in range(group)
    ]
    arrays = {("block", 0): packed[0]}
    near = [step for step in range(1, group) if hops(step) < 2]
    first = ("halo", 1, (0,))

    def send_on(steps):
        message = jnp.stack([arrays["block", step][: 2 * rows] for step in steps])
        for offset in offsets:
            pairs = [(source, (source + offset) % groups) for source in range(groups)]
            arrays["halo", offset, tuple(steps)] = lax.ppermute(message, "group", pairs)

    def send_across(step):
        for offset in offsets:
            pairs = [
                (at * group + p, (at + offset) % groups * group + (p ^ step))
                for at in range(groups)
                for p in range(group)
            ]
            message = packed[step][None, : 2 * rows]
            message, arrays["block", 0] = lax.optimization_barrier((message, arrays["block", 0]))
            arrived = lax.ppermute(message, ("group", "place"), pairs)
            arrays["halo", offset, (step,)] = arrived

    def stage(at, cost):
        work = plan[at]
        started = [
            step
            for step in range(group)
            if finish[step] >= at and any(step in table for work in plan[:at] for table in work)
        ]
        active = sorted(set(started) | {step for table in work for step in table})
        ready = [step for step in sending_order(group) if step in active and finish[step] == at]
        keys = {key for table in work for todo in table.values() for key, _ in todo}
        dests = {step for table in work for step in table}
        names = []
        for name in arrays:
            if name[0] == "halo":
                used = any((name[1], step) in keys for step in name[2])
            elif name[0] == "block":
                used = (0, name[1]) in keys or name[1] in dests
            else:
                used = bool(started)
            if used:
                names.append(name)
        states = [shape((group, HD, rows), f32), shape((group, 8, rows), f32)]
        if len(ready) == len(active):
            states = []
        outs = pl.pallas_call(
            functools.partial(
                attend_kernel,
                names=names,
                work=work,
                started=started,
                active=active,
                ready=ready,
                rows=rows,
            ),
            out_shape=[shape((HD, rows), bf16)] * len(ready) + states,
            in_specs=[VMEM] * len(names),
            out_specs=[VMEM] * (len(ready) + len(states)),
            compiler_params=PARAMS,
            cost_estimate=pl.CostEstimate(flops=cost, transcendentals=1, bytes_accessed=1),
            name="attend",
        )(*[arrays[name] for name in names])
        if states:
            arrays["mixed",], arrays["state",] = outs[len(ready) :]
        return dict(zip(ready, outs))

    for step in near:
        arrays["block", step] = swapped(packed[step], "place", step)
    arrays["block", 0], turned = lax.optimization_barrier((packed[0], turned))
    mix = {}
    far_blocks = packed[len(near) + 1 :]
    for step in near[:1] + apart:
        send_across(step)
    if apart:
        tied = lax.optimization_barrier(
            (far_blocks, turned, [arrays["block", step] for step in near])
        )
        far_blocks, turned, blocks = tied
        arrays.update((("block", step), block) for step, block in zip(near, blocks))
    early_own = arrays["block", 0]
    if near:
        late = ("block", near[-1])
        tied = lax.optimization_barrier((early_own, arrays[late]))
        arrays["block", 0], arrays[late] = tied
    send_on([0])
    arrays["block", 0] = early_own
    for step in near[1:]:
        send_on([step])
    for step, block in zip(apart, far_blocks):
        arrays["block", step] = swapped(block, "place", step)
    mix.update(stage(0, NEAR))
    for at in range(1, len(plan)):
        done = stage(at, FAR)
        order = [step for step in sending_order(group) if step in done]
        mix.update((step, swapped(done[step], "place", step) if step else done[0]) for step in order)

    mixes = [mix[step] for step in sending_order(group)]
    output = []
    for others, kind in (([0], f32), (list(range(1, head_total)), bf16)):
        parts = mixes
        if output:
            parts = [swapped(entry, "head", other) for other in others for entry in mixes]
        output = [
            pl.pallas_call(
                functools.partial(project_kernel, group=group, others=others),
                out_shape=shape((features, rows), kind),
                in_specs=[VMEM] * (1 + len(parts) + len(output)),
                out_specs=VMEM,
                scratch_shapes=[pltpu.VMEM((len(others), group, HD, rows), bf16)],
                compiler_params=PARAMS,
                name="project",
            )(turned, *parts, *output)
        ]
    return output[0]


def solution(mesh):
    nodes, heads = mesh.devices.shape
    place = HEADS // heads
    split = Mesh(
        mesh.devices.reshape(nodes // place, place, heads), ("group", "place", "head")
    )
    node = ("group", "place")
    return jax.shard_map(
        on_device,
        mesh=split,
        in_specs=(
            P(node, "head"),
            P(node, "head"),
            P(node, "head"),
            P(None, node, None),
            P(None, node),
            P(),
        ),
        out_specs=P("head", node),
        check_vma=False,
    )
```

```python
import functools

import jax
import jax.numpy as jnp
from jax import lax
from jax.experimental import pallas as pl
from jax.experimental.pallas import tpu as pltpu
from jax.sharding import Mesh, PartitionSpec as P

HEADS = 8
HD = 128
TILE = 128
SLOTS = 2
STEPS = 4
LOG2E = 1.4426950408889634
SCALE = LOG2E * HD ** (-0.5)
MASKED = -1e30
EXTRA = 16
OWN = 1000000000
NEAR = 1000000000
FAR = 1000000000
VMEM = pl.BlockSpec(memory_space=pltpu.VMEM)
HBM = pl.BlockSpec(memory_space=pltpu.HBM)
PARAMS = pltpu.CompilerParams(vmem_limit_bytes=48 * 1024 * 1024)


def use_rows(index_ref, count_ref, tiles):
    row = lax.broadcasted_iota(jnp.int32, (EXTRA, HD), 0)
    uses = jnp.zeros((EXTRA, HD), jnp.float32)
    for turn in range(STEPS):
        for dest in range(tiles):
            for source in range(tiles):
                times = jnp.float32(0)
                for slot in range(SLOTS):
                    used = (slot < count_ref[dest, turn]) & (index_ref[dest, slot, turn] == source)
                    times += jnp.where(used, 1.0, 0.0)
                uses = jnp.where(row == (turn * tiles + dest) * tiles + source, times, uses)
    return uses


def hops(step):
    return step.bit_count()


def pack_kernel(query_ref, key_ref, value_ref, index_ref, count_ref, *refs):
    out_refs, (values, index, count, sem) = refs[:-4], refs[-4:]
    group = query_ref.shape[1] // HD
    rows = query_ref.shape[0]
    tiles = rows // TILE
    place = lax.axis_index("place")
    value_copy = pltpu.make_async_copy(value_ref, values, sem.at[0])
    value_copy.start()
    table_copies = [
        pltpu.make_async_copy(index_ref, index, sem.at[1]),
        pltpu.make_async_copy(count_ref, count, sem.at[2]),
    ]
    for copy in table_copies:
        copy.start()
    copies = []
    for step in range(group):
        cols = pl.ds(pl.multiple_of(jnp.bitwise_xor(place, step) * HD, HD), HD)
        copies += [
            pltpu.make_async_copy(
                key_ref.at[:, cols], out_refs[step].at[pl.ds(0, rows)], sem.at[3 + 2 * step]
            ),
            pltpu.make_async_copy(
                query_ref.at[:, cols],
                out_refs[step].at[pl.ds(2 * rows, rows)],
                sem.at[4 + 2 * step],
            ),
        ]
    for copy in copies:
        copy.start()
    for copy in table_copies:
        copy.wait()
    uses = use_rows(index, count, tiles).astype(jnp.bfloat16)
    value_copy.wait()
    for step in range(group):
        cols = pl.ds(pl.multiple_of(jnp.bitwise_xor(place, step) * HD, HD), HD)
        out = out_refs[step]
        out[3 * rows :] = uses
        for at in range(0, rows, TILE):
            out[rows + at : rows + at + TILE] = values[at : at + TILE, cols].T
    for copy in copies:
        copy.wait()


def pair_scores(keys, query_ref, turn):
    rows = keys.shape[0]
    tiles = rows // TILE
    raw = (
        lax.dot_general(
            keys, query_ref[:rows], (((1,), (1,)), ((), ())), preferred_element_type=jnp.float32
        )
        * SCALE
    )
    uses = query_ref[rows:].astype(jnp.float32)
    parts = []
    for source in range(tiles):
        bias = []
        for tile in range(tiles):
            at = (turn * tiles + tile) * tiles + source
            times = uses[at : at + 1]
            bias.append(jnp.where(times > 0.5, times - 1.0, MASKED))
        parts.append(
            raw[source * TILE : (source + 1) * TILE] + jnp.concatenate(bias, axis=1)
        )
    return raw, jnp.concatenate(parts, axis=0)


def own_scores(raw):
    eye = lax.broadcasted_iota(jnp.int32, (TILE, TILE), 0) == lax.broadcasted_iota(
        jnp.int32, (TILE, TILE), 1
    )
    return jnp.concatenate(
        [
            jnp.sum(
                jnp.where(eye, raw[at : at + TILE, at : at + TILE], 0.0), axis=0, keepdims=True
            )
            for at in range(0, raw.shape[0], TILE)
        ],
        axis=1,
    )


def turned_values(source_ref, rows):
    return jnp.concatenate(
        [source_ref[rows + at : rows + at + TILE] for at in range(0, rows, TILE)], axis=1
    )


def attend(query_ref, sources, before):
    rows = query_ref.shape[0] - EXTRA
    scores = []
    for source_ref, turn in sources:
        raw, score = pair_scores(source_ref[:rows], query_ref, turn)
        scores.append(score)
        if turn == 0:
            own = own_scores(raw)
    top = own if before is None else before[0]
    for score in scores:
        top = jnp.maximum(top, jnp.max(score, axis=0, keepdims=True))
    if before is None:
        total = jnp.exp2(own - top)
        own_ref = next(source_ref for source_ref, turn in sources if turn == 0)
        mixed = total * turned_values(own_ref, rows).astype(jnp.float32)
    else:
        factor = jnp.exp2(before[0] - top)
        total, mixed = before[1] * factor, before[2] * factor
    for score, (source_ref, _) in zip(scores, sources):
        weights = jnp.exp2(score - top)
        total = total + jnp.sum(weights, axis=0, keepdims=True)
        mixed = mixed + jnp.dot(
            turned_values(source_ref, rows),
            weights.astype(jnp.bfloat16),
            preferred_element_type=jnp.float32,
        )
    return top, total, mixed


def sources_of(group, place, step):
    result = []
    for turn in range(STEPS):
        slab = (place ^ step) - turn
        result.append(((-(slab // group), place ^ (slab % group)), turn))
    return result


def stage_plan(group):
    steps = list(range(group))
    near = [step for step in steps if hops(step) < 2]
    stages = [(near, lambda offset, step: hops(step) < 2 and (offset == 0 or step == 0))]
    stages.append((steps, lambda offset, step: offset == 0 or step != near[-1]))
    stages.append((steps, lambda offset, step: True))
    plan, taken = [], set()
    for dests, there in stages:
        work = []
        for place in range(group):
            table = {}
            for dest in dests:
                todo = [
                    (key, turn)
                    for key, turn in sources_of(group, place, dest)
                    if there(*key) and (place, dest, turn) not in taken
                ]
                taken.update((place, dest, turn) for _, turn in todo)
                if todo:
                    table[dest] = todo
            work.append(table)
        plan.append(work)
    return plan


def attend_kernel(*refs, names, work, started, active, ready, rows):
    named = dict(zip(names, refs))
    outs = refs[len(names) :]
    out_refs, state_refs = dict(zip(ready, outs)), outs[len(ready) :]
    group = len(work)

    def block(offset, step):
        for name in named:
            if name[0] == "halo" and name[1] == offset and step in name[2]:
                return named[name].at[name[2].index(step)]
        return named["block", step]

    def queries(step):
        return named["block", step].at[pl.ds(2 * rows, rows + EXTRA)]

    here = lax.axis_index("place")
    for place in range(group):

        @pl.when(here == place)
        def _(place=place):
            for step in active:
                before = None
                if step in started:
                    mixed_ref, state_ref = named["mixed",], named["state",]
                    before = (state_ref[step, 0:1], state_ref[step, 1:2], mixed_ref[step])
                todo = [(block(*key), turn) for key, turn in work[place].get(step, [])]
                top, total, mixed = attend(queries(step), todo, before) if todo else before
                if step in ready:
                    out_refs[step][...] = (mixed / total).astype(out_refs[step].dtype)
                else:
                    state_refs[0][step] = mixed
                    state_refs[1][step, 0:1] = top
                    state_refs[1][step, 1:2] = total


def turn_kernel(block_ref, weight_ref, turned_ref, held, sem, *, head_total):
    me = lax.axis_index("head")
    depth = weight_ref.shape[0] // head_total
    features = weight_ref.shape[1] // head_total
    copies = []
    for other in range(head_total):
        start = pl.multiple_of(jnp.bitwise_xor(me, other) * depth, depth)
        cols = pl.ds(pl.multiple_of(me * features, features), features)
        copies.append(
            pltpu.make_async_copy(
                weight_ref.at[pl.ds(start, depth), cols], held.at[other], sem.at[other]
            )
        )
        copies[-1].start()
    for other in range(head_total):
        copies[other].wait()
        turned_ref[other] = held[other].T


def sending_order(group):
    last = max(step for step in range(group) if hops(step) < 2)
    return sorted(range(group), key=lambda step: (step > 0, step != last, -hops(step), step))


def project_kernel(turned_ref, *refs, group, others):
    mix_refs, refs = refs[: len(others) * group], refs[len(others) * group :]
    so_far, (out_ref, mix) = refs[:-2], refs[-2:]
    place = lax.axis_index("place")
    for number in range(len(others)):
        for at, step in enumerate(sending_order(group)):
            mix[number, jnp.bitwise_xor(place, step)] = mix_refs[number * group + at][...]
    result = so_far[0][...] if so_far else None
    for number, other in enumerate(others):
        part = jnp.dot(
            turned_ref[other],
            mix[number].reshape(turned_ref.shape[2], out_ref.shape[1]),
            preferred_element_type=jnp.float32,
        )
        result = part if result is None else result + part
    out_ref[...] = result.astype(out_ref.dtype)


def swapped(value, axis, step):
    count = lax.axis_size(axis)
    return lax.ppermute(value, axis, [(source, source ^ step) for source in range(count)])


def on_device(node_queries, node_keys, node_values, tile_index, tile_count, out_weight):
    rows, width = node_queries.shape
    group = width // HD
    groups = lax.axis_size("group")
    head_total = lax.axis_size("head")
    depth, feature_total = out_weight.shape
    features = feature_total // head_total
    bf16, f32 = jnp.bfloat16, jnp.float32
    shape = jax.ShapeDtypeStruct

    apart = [step for step in range(group) if hops(step) > 1]
    packed = pl.pallas_call(
        pack_kernel,
        out_shape=[shape((3 * rows + EXTRA, HD), bf16)] * group,
        in_specs=[HBM] * 5,
        out_specs=[VMEM] * group,
        scratch_shapes=[
            pltpu.VMEM((rows, width), bf16),
            pltpu.SMEM((rows // TILE, SLOTS, STEPS), jnp.int32),
            pltpu.SMEM((rows // TILE, STEPS), jnp.int32),
            pltpu.SemaphoreType.DMA((3 + 2 * group,)),
        ],
        compiler_params=PARAMS,
        name="pack",
    )(
        *[
            pltpu.with_memory_space_constraint(array, pltpu.HBM)
            for array in (
                node_queries,
                node_keys,
                node_values,
                jnp.transpose(tile_index, (1, 2, 0)),
                jnp.transpose(tile_count, (1, 0)),
            )
        ],
    )

    turned = pl.pallas_call(
        functools.partial(turn_kernel, head_total=head_total),
        out_shape=shape((head_total, features, depth // head_total), bf16),
        in_specs=[HBM, HBM],
        out_specs=VMEM,
        scratch_shapes=[
            pltpu.VMEM((head_total, depth // head_total, features), bf16),
            pltpu.SemaphoreType.DMA((head_total,)),
        ],
        compiler_params=PARAMS,
        cost_estimate=pl.CostEstimate(flops=OWN, transcendentals=1, bytes_accessed=1),
        name="turn",
    )(packed[0], pltpu.with_memory_space_constraint(out_weight, pltpu.HBM))

    offsets = list(range(1, -(-(STEPS - 1) // group) + 1))
    plan = stage_plan(group)
    finish = [
        max(at for at, work in enumerate(plan) for table in work if step in table)
        for step in range(group)
    ]
    arrays = {("block", 0): packed[0]}
    near = [step for step in range(1, group) if hops(step) < 2]
    first = ("halo", 1, (0,))

    def send_on(steps):
        message = jnp.stack([arrays["block", step][: 2 * rows] for step in steps])
        for offset in offsets:
            pairs = [(source, (source + offset) % groups) for source in range(groups)]
            arrays["halo", offset, tuple(steps)] = lax.ppermute(message, "group", pairs)

    def send_across(step):
        for offset in offsets:
            pairs = [
                (at * group + p, (at + offset) % groups * group + (p ^ step))
                for at in range(groups)
                for p in range(group)
            ]
            message = packed[step][None, : 2 * rows]
            message, arrays["block", 0] = lax.optimization_barrier((message, arrays["block", 0]))
            arrived = lax.ppermute(message, ("group", "place"), pairs)
            arrays["halo", offset, (step,)] = arrived

    def stage(at, cost):
        work = plan[at]
        started = [
            step
            for step in range(group)
            if finish[step] >= at and any(step in table for work in plan[:at] for table in work)
        ]
        active = sorted(set(started) | {step for table in work for step in table})
        ready = [step for step in sending_order(group) if step in active and finish[step] == at]
        keys = {key for table in work for todo in table.values() for key, _ in todo}
        dests = {step for table in work for step in table}
        names = []
        for name in arrays:
            if name[0] == "halo":
                used = any((name[1], step) in keys for step in name[2])
            elif name[0] == "block":
                used = (0, name[1]) in keys or name[1] in dests
            else:
                used = bool(started)
            if used:
                names.append(name)
        states = [shape((group, HD, rows), f32), shape((group, 8, rows), f32)]
        if len(ready) == len(active):
            states = []
        outs = pl.pallas_call(
            functools.partial(
                attend_kernel,
                names=names,
                work=work,
                started=started,
                active=active,
                ready=ready,
                rows=rows,
            ),
            out_shape=[shape((HD, rows), bf16)] * len(ready) + states,
            in_specs=[VMEM] * len(names),
            out_specs=[VMEM] * (len(ready) + len(states)),
            compiler_params=PARAMS,
            cost_estimate=pl.CostEstimate(flops=cost, transcendentals=1, bytes_accessed=1),
            name="attend",
        )(*[arrays[name] for name in names])
        if states:
            arrays["mixed",], arrays["state",] = outs[len(ready) :]
        return dict(zip(ready, outs))

    for step in near:
        arrays["block", step] = swapped(packed[step], "place", step)
    send_on([0])
    arrays["block", 0], turned = lax.optimization_barrier((packed[0], turned))
    mix = {}
    far_blocks = packed[len(near) + 1 :]
    for step in apart:
        send_across(step)
    for step in near[:1]:
        send_on([step])
    if apart:
        tied = lax.optimization_barrier(
            (far_blocks, turned, [arrays["block", step] for step in near])
        )
        far_blocks, turned, blocks = tied
        arrays.update((("block", step), block) for step, block in zip(near, blocks))
    for step in near[1:]:
        send_on([step])
    for step, block in zip(apart, far_blocks):
        arrays["block", step] = swapped(block, "place", step)
    mix.update(stage(0, NEAR))
    for at in range(1, len(plan)):
        done = stage(at, FAR)
        order = [step for step in sending_order(group) if step in done]
        mix.update((step, swapped(done[step], "place", step) if step else done[0]) for step in order)

    mixes = [mix[step] for step in sending_order(group)]
    output = []
    for others, kind in (([0], f32), (list(range(1, head_total)), bf16)):
        parts = mixes
        if output:
            parts = [swapped(entry, "head", other) for other in others for entry in mixes]
        output = [
            pl.pallas_call(
                functools.partial(project_kernel, group=group, others=others),
                out_shape=shape((features, rows), kind),
                in_specs=[VMEM] * (1 + len(parts) + len(output)),
                out_specs=VMEM,
                scratch_shapes=[pltpu.VMEM((len(others), group, HD, rows), bf16)],
                compiler_params=PARAMS,
                name="project",
            )(turned, *parts, *output)
        ]
    return output[0]


def solution(mesh):
    nodes, heads = mesh.devices.shape
    place = HEADS // heads
    split = Mesh(
        mesh.devices.reshape(nodes // place, place, heads), ("group", "place", "head")
    )
    node = ("group", "place")
    return jax.shard_map(
        on_device,
        mesh=split,
        in_specs=(
            P(node, "head"),
            P(node, "head"),
            P(node, "head"),
            P(None, node, None),
            P(None, node),
            P(),
        ),
        out_specs=P("head", node),
        check_vma=False,
    )
```
